32 devices in a mesh: gz: 8 (over y, x, core), gy: 4 (over z).
Axes of the slice: x: 2, y: 2, z: 4, core: 2. Of those that a mesh axis runs over, the one named last changes fastest.
Arguments:
- applied_load: float32 [3, 64, 32, 512], P(None, 'gz', 'gy'), may hold values from -12 to 12
- start_field: float32 [3, 64, 32, 512], P(None, 'gz', 'gy'), may hold values from -2 to 2
- bone_mask: int32 [64, 32, 512], P('gz', 'gy'), may hold values 0 or 1
- element_stiffness: bfloat16 [24, 24], replicated, may hold values from -1.5 to 2, as said below
Outputs:
- corrected: float32 [3, 64, 32, 512], P(None, 'gz', 'gy')
The draws below stay inside these ranges and needn't reach their ends.
Inputs may be any that keep to these rules, and one draw needn't show every extreme that they name: element_stiffness is symmetric and positive definite, and each of its diagonal entries is at least 0.125.
All inputs are finite; a program needn't handle non-finite values. No bound on the sum of `bone_mask` on one device may be relied on, other than what follows from the above.
Results may differ from the reference program's by a relative error of at most 0.0059.
Values may be sent and summed in bfloat16 or wider, within the bound.
A program may use at most 64 MiB of HBM per device.

```python
import math
import jax
import jax.numpy as jnp
from jax import lax

DOF = 3
EDOF = 24
CHEB = 3
NX = 512
NZ = 64
NY = 32


def draw_element_stiffness(key, part):
    first_key = jax.random.fold_in(key, 0)
    third_key = jax.random.fold_in(key, 2)
    factors = jax.random.truncated_normal(first_key, -3.0, 3.0, (EDOF, EDOF), jnp.float32)
    shared = jax.random.uniform(third_key, (EDOF,), jnp.float32, 0.4, 1.0)
    gram = jnp.dot(factors, factors.T, precision=lax.Precision.HIGHEST) / (8.0 * EDOF)
    gram = 0.5 * (gram + gram.T)
    matrix = gram + 0.5 * shared[:, None] * shared[None, :] + 0.125 * jnp.eye(EDOF, dtype=jnp.float32)
    return matrix.astype(jnp.bfloat16)


def draw_start_field(key, part):
    freq_key, phase_key, amp_key, noise_key = jax.random.split(key, 4)
    freqs = jax.random.uniform(freq_key, (DOF, 3), jnp.float32, 0.5, 2.0)
    phases = jax.random.uniform(phase_key, (DOF, 3), jnp.float32, 0.0, 1.0)
    depth = jnp.arange(NZ, dtype=jnp.float32) / NZ
    rows = jnp.arange(NY, dtype=jnp.float32) / NY
    cols = jnp.arange(NX, dtype=jnp.float32) / NX
    wave_z = jnp.cos(2.0 * math.pi * (freqs[:, 0:1] * depth[None, :] + phases[:, 0:1]))
    wave_y = jnp.cos(2.0 * math.pi * (freqs[:, 1:2] * rows[None, :] + phases[:, 1:2]))
    wave_x = jnp.cos(2.0 * math.pi * (freqs[:, 2:3] * cols[None, :] + phases[:, 2:3]))
    smooth = 0.6 + 0.4 * wave_z[:, :, None, None] * wave_y[:, None, :, None] * wave_x[:, None, None, :]
    signs = jnp.where(jnp.arange(DOF) % 2 == 1, -1.0, 1.0).astype(jnp.float32)
    amps = jax.random.uniform(amp_key, (DOF,), jnp.float32, 0.5, 1.0)
    noise = 0.35 * jax.random.truncated_normal(noise_key, -2.8, 2.8, (DOF, NZ, NY, NX), jnp.float32)
    values = (signs * amps)[:, None, None, None] * smooth + noise
    return values.astype(jnp.float32)


def set_ends(array, rng, least, largest):
    index_at = [jax.random.randint(jax.random.fold_in(rng, axis), (), 0, length) for axis, length in enumerate(array.shape)]
    main_axis = array.shape.index(max(array.shape))
    neighbour = index_at[:main_axis] + [(index_at[main_axis] + 1) % array.shape[main_axis]] + index_at[main_axis + 1:]
    return array.at[tuple(index_at)].set(least).at[tuple(neighbour)].set(largest)


def levels(key, dims, cuts, smallest, high):
    def one(position, blocks):
        heights = jax.random.uniform(jax.random.fold_in(jax.random.fold_in(key, 6), position), (blocks,), jnp.float32, smallest / len(cuts), high / len(cuts))
        return jnp.repeat(jnp.exp(heights), dims[position] // blocks).reshape((-1,) + (1,) * (len(dims) - position - 1))

    gain = one(*cuts[0])
    for cut in cuts[1:]:
        gain = gain * one(*cut)
    return gain


def bell_draw(key, dims, scale, limit, shards=(), kind=jnp.bfloat16):
    values = scale * jax.random.normal(key, dims, jnp.float32)
    if shards:
        values = values * levels(key, dims, shards, -0.22, 0.18)
    return jnp.clip(values, -limit, limit).astype(kind)


def setup_inputs(seed: int = 0) -> dict:
    splits = jax.random.split(jax.random.key(seed), 5)
    applied_load = bell_draw(splits[0], (DOF, NZ, NY, NX), 2.0, 12.0, ((1, 8), (2, 4)), jnp.float32)
    start_field = draw_start_field(jax.random.fold_in(splits[4], 71), 0)
    bone_mask = set_ends((jax.random.randint(splits[2], (NZ, NY, NX), 0, 4) < 3).astype(jnp.int32), jax.random.fold_in(splits[2], 1), 0, 1)
    element_stiffness = draw_element_stiffness(jax.random.fold_in(splits[4], 71), 0)
    return dict(applied_load=applied_load, start_field=start_field, bone_mask=bone_mask, element_stiffness=element_stiffness)


corner_offsets = [(0, 0, 0), (0, 0, 1), (0, 1, 0), (0, 1, 1), (1, 0, 0), (1, 0, 1), (1, 1, 0), (1, 1, 1)]
low_ratio = 0.1


def scatter_full(terms):
    summed = None
    for offset, piece in zip(corner_offsets, terms):
        padded = jnp.pad(piece, ((0, 0), (offset[0], 1 - offset[0]), (offset[1], 1 - offset[1]), (offset[2], 1 - offset[2])))
        summed = padded if summed is None else summed + padded
    return summed


def element_global(values_bf, elem_scale, element_stiffness):
    depth_n, rows_n, cols_n = elem_scale.shape
    padded = lax.optimization_barrier(jnp.pad(values_bf, ((0, 0), (0, 1), (0, 1), (0, 1))))
    stiff_wide = element_stiffness.astype(jnp.float32)

    def one_layer(carried, layer_index):
        pair = lax.dynamic_slice_in_dim(padded, layer_index, 2, 1).astype(jnp.float32)
        layer_scale = lax.dynamic_slice_in_dim(elem_scale, layer_index, 1, 0)
        pieces = [pair[:, offset[0]:offset[0] + 1, offset[1]:offset[1] + rows_n, offset[2]:offset[2] + cols_n] for offset in corner_offsets]
        gathered = jnp.concatenate(pieces, axis=0)
        products = jnp.einsum("ij,jzyx->izyx", stiff_wide, gathered) * layer_scale
        summed = scatter_full([products[DOF * corner:DOF * corner + DOF] for corner in range(8)])
        summed = summed.at[:, 0].add(carried)
        return summed[:, 1], summed[:, 0]

    start_carry = jnp.zeros((DOF, rows_n + 1, cols_n + 1), jnp.float32)
    leftover, planes = lax.scan(one_layer, start_carry, jnp.arange(depth_n, dtype=jnp.int32))
    planes = jnp.transpose(planes, (1, 0, 2, 3))
    return planes[:, :, :rows_n, :cols_n]


def diagonal_global(elem_scale, stiff_diag):
    depth_n, rows_n, cols_n = elem_scale.shape
    summed = scatter_full([stiff_diag[corner][:, None, None, None] * elem_scale[None] for corner in range(8)])
    return summed[:, :depth_n, :rows_n, :cols_n]


def prepare_level(elem_scale, element_stiffness, stiff_diag):
    diagonal = diagonal_global(elem_scale, stiff_diag)
    inactive = (diagonal == 0.0).astype(jnp.float32)
    inverse = 1.0 / (diagonal + inactive)

    def operator(values_in):
        return element_global(values_in.astype(jnp.bfloat16), elem_scale, element_stiffness) + inactive * values_in

    return operator, inverse


def chebyshev(operator, rhs_vals, start_vals, inverse, mid_value, half_width):
    ratio_value = (1.0 + low_ratio) / (1.0 - low_ratio)
    rho_prev = 1.0 / ratio_value
    if start_vals is None:
        update = inverse * rhs_vals / mid_value
        current = update
    else:
        update = inverse * (rhs_vals - operator(start_vals)) / mid_value
        current = start_vals + update
    for sweep in range(CHEB - 1):
        rho_next = 1.0 / (2.0 * ratio_value - rho_prev)
        resid_now = rhs_vals - operator(current)
        update = (rho_next * rho_prev) * update + (2.0 * rho_next / half_width) * inverse * resid_now
        current = current + update
        rho_prev = rho_next
    return current


def halve_axis(values_in, axis_pos):
    length = values_in.shape[axis_pos]
    half_len = length // 2
    widths = [(0, 0)] * values_in.ndim
    widths[axis_pos] = (0, 2 * (half_len + 1) - length)
    padded = jnp.pad(values_in, widths)
    shape_new = values_in.shape[:axis_pos] + (half_len + 1, 2) + values_in.shape[axis_pos + 1:]
    pairs = padded.reshape(shape_new)
    even_part = lax.index_in_dim(pairs, 0, axis_pos + 1, keepdims=False)
    odd_part = lax.index_in_dim(pairs, 1, axis_pos + 1, keepdims=False)
    before = jnp.concatenate([jnp.zeros_like(lax.slice_in_dim(odd_part, 0, 1, axis=axis_pos)), lax.slice_in_dim(odd_part, 0, half_len, axis=axis_pos)], axis=axis_pos)
    return even_part + 0.5 * odd_part + 0.5 * before


def double_axis(values_in, axis_pos):
    coarse_len = values_in.shape[axis_pos] - 1
    lower_part = lax.slice_in_dim(values_in, 0, coarse_len, axis=axis_pos)
    upper_part = lax.slice_in_dim(values_in, 1, coarse_len + 1, axis=axis_pos)
    middle = 0.5 * (lower_part + upper_part)
    stacked = jnp.stack([lower_part, middle], axis=axis_pos + 1)
    shape_new = values_in.shape[:axis_pos] + (2 * coarse_len,) + values_in.shape[axis_pos + 1:]
    return stacked.reshape(shape_new)


def reference(applied_load, start_field, bone_mask, element_stiffness):
    stiff_wide = element_stiffness.astype(jnp.float32)
    upper_bound = jnp.max(jnp.sum(jnp.abs(stiff_wide), axis=1) / jnp.diagonal(stiff_wide))
    mid_value = 0.5 * (1.0 + low_ratio) * upper_bound
    half_width = 0.5 * (1.0 - low_ratio) * upper_bound
    stiff_diag = jnp.diagonal(stiff_wide).reshape(8, DOF)
    fine_scale = bone_mask.astype(jnp.float32)
    depth_n, rows_n, cols_n = bone_mask.shape
    coarse_scale = 0.25 * fine_scale.reshape(depth_n // 2, 2, rows_n // 2, 2, cols_n // 2, 2).sum(axis=(1, 3, 5))
    fine_op, fine_inverse = prepare_level(fine_scale, element_stiffness, stiff_diag)
    smoothed = chebyshev(fine_op, applied_load, start_field, fine_inverse, mid_value, half_width)
    residual = applied_load - fine_op(smoothed)
    coarse_rhs = halve_axis(halve_axis(halve_axis(residual, 1), 2), 3)[:, :-1, :-1, :-1]
    coarse_op, coarse_inverse = prepare_level(coarse_scale, element_stiffness, stiff_diag)
    correction = chebyshev(coarse_op, coarse_rhs, None, coarse_inverse, mid_value, half_width).astype(jnp.bfloat16)
    widened = lax.optimization_barrier(jnp.pad(correction, ((0, 0), (0, 1), (0, 1), (0, 1)))).astype(jnp.float32)
    return smoothed + double_axis(double_axis(double_axis(widened, 1), 2), 3)
```

```python
import functools

import jax
import jax.numpy as jnp
import ml_dtypes
import numpy as np
from jax import lax
from jax.experimental import pallas as pl
from jax.experimental.pallas import tpu as pltpu
from jax.sharding import PartitionSpec as P

DOF = 3
EDOF = 24
B = 8
C = B // 2
LOW = 0.1
MESH = pl.DeviceIdType.MESH
F32, BF16 = jnp.float32, jnp.bfloat16

NEAR = [(0, -1), (0, 1), (-1, -1), (-1, 1), (1, -1), (1, 1), (-1, 0), (1, 0)]
SPAN = [(0, 32), (32, 32), (64, 16), (80, 16), (96, 16), (112, 16), (128, 32), (160, 32)]
MASK_SPAN = {(-1, 0): 64, (0, -1): 80, (-1, -1): 96}


def col_code(col):
    p, rest = divmod(col, 64)
    sx, rc = divmod(rest, 32)
    if rc < 24:
        return p, sx, rc // 8, rc % 8
    if rc < 27:
        return p, sx, rc - 24, -1
    if rc < 30:
        return p, sx, rc - 27, 8
    return None


def tables(nx):
    half = nx // 2
    out = {}
    rep = np.zeros((192, EDOF))
    for r in range(192):
        rep[r, (r // 24) * 3 + (r % 24) // 8] = 1
    out["rep"] = rep
    rep_x = np.zeros((64, EDOF))
    for q in range(8):
        for d in range(3):
            rep_x[q * 8 + d, q * 3 + d] = 1
    out["rep_x"] = rep_x
    for cz2 in range(2):
        for cy2 in range(2):
            pick = np.zeros((32, 192))
            keep = np.zeros((192, 192))
            for col in range(192):
                code = col_code(col)
                if code is None:
                    continue
                p, sx, d, y2 = code
                pick[3 * (4 * cz2 + 2 * cy2 + sx) + d, col] = 1
                for r in range(192):
                    q, y = r // 24, r % 8
                    cz, cy = q // 4, (q // 2) % 2
                    if p == 1 - cz + cz2 and y2 == y - cy + cy2:
                        keep[r, col] = 1
            out["pick%d%d" % (cz2, cy2)] = pick
            out["keep%d%d" % (cz2, cy2)] = keep
    sel = np.zeros((128, 192))
    for z in range(B):
        for d in range(3):
            sel[z * 3 + d, z * 24 + d * 8] = 1
            sel[32 + z * 3 + d, z * 24 + d * 8 + 7] = 1
    for k, (z, y) in enumerate([(0, 0), (0, 7), (7, 0), (7, 7)]):
        for d in range(3):
            sel[64 + 16 * k + d, z * 24 + d * 8 + y] = 1
    out["sel"] = sel
    put = np.zeros((80, 128))
    for d in range(3):
        for z in range(B):
            put[(z + 1) * 8 + d, z * 3 + d] = 1
            put[(z + 1) * 8 + 3 + d, 32 + z * 3 + d] = 1
        put[d, 64 + d] = 1
        put[3 + d, 80 + d] = 1
        put[72 + d, 96 + d] = 1
        put[72 + 3 + d, 112 + d] = 1
    out["put"] = put
    mask_sel = np.zeros((64, 64))
    for i in range(8):
        mask_sel[i, 56 + i] = 1
        mask_sel[16 + i, i * 8 + 7] = 1
    mask_sel[32, 63] = 1
    for z in range(B):
        for y in range(B):
            mask_sel[48 + (z // 2) * C + y // 2, z * 8 + y] = 0.25
    out["mask_sel"] = mask_sel
    mask_put = np.zeros((144, 112))
    for layer in range(-1, B):
        for y in range(B):
            for cy in range(2):
                row, y2 = (layer + 1) * 16 + cy * 8 + y, y - cy
                if layer >= 0:
                    mask_put[row, layer * 8 + y2 if y2 >= 0 else 80 + layer] = 1
                else:
                    mask_put[row, 64 + y2 if y2 >= 0 else 96] = 1
    out["mask_put"] = mask_put
    pairs = np.zeros((nx, half))
    down = np.zeros((nx, half))
    for i in range(nx):
        pairs[i, i // 2] = 1
        if i % 2 == 0:
            down[i, i // 2] = 1
        else:
            down[i, i // 2] = 0.5
            if i // 2 + 1 < half:
                down[i, i // 2 + 1] = 0.5
    out["pairs"], out["down"] = pairs, down
    up = down.T
    out["up0"], out["up1"] = up[:, :half], up[:, half:]
    cs_put = np.zeros((320, 144))

    def place(index):
        return (index + C) // C, (index + C) % C

    for layer in range(-3, 7):
        zs, kz = place(layer)
        base = (layer + 3) * 32
        for t in range(8):
            for cy in range(2):
                ys, ky = place(t - 1 - cy)
                cs_put[base + cy * 8 + t, (zs * 3 + ys) * 16 + kz * C + ky] = 1
        for d in range(3):
            for cy in range(2):
                ys, ky = place(-2 - cy)
                cs_put[base + 16 + cy * 8 + d, (zs * 3 + ys) * 16 + kz * C + ky] = 1
    out["cs_put"] = cs_put
    line = np.zeros((C + 1, B))
    for i in range(B):
        if i % 2 == 0:
            line[i // 2, i] = 1
        else:
            line[i // 2, i] = 0.5
            line[i // 2 + 1, i] = 0.5
    shrink = np.zeros((80, 192))
    grow = np.zeros((192, 120))
    for k in range(C + 1):
        for j in range(C + 1):
            for z in range(B):
                for y in range(B):
                    for d in range(3):
                        w = line[k, z] * line[j, y]
                        shrink[k * 16 + j * 3 + d, z * 24 + d * 8 + y] = w
                        grow[z * 24 + d * 8 + y, k * 24 + d * 8 + j + 1] = w
    out["shrink"], out["grow"] = shrink, grow
    gather = np.zeros((32, 64))
    for d in range(3):
        for t in range(8):
            y = t - 1
            for slot, at in ((0, y + C), (1, y), (2, y - C), (3, y)):
                if 0 <= at <= C:
                    gather[d * 8 + t, slot * 16 + at * 3 + d] = 1
        gather[24 + d, (C - 2) * 3 + d] = 1
    out["gather"] = gather
    return out


def pack_tables(nx):
    width = max(256, nx // 2)
    where, parts, at = {}, [], 0
    for name, table in tables(nx).items():
        rows, cols = table.shape
        where[name] = (at, rows, cols)
        tall = -(-rows // 16) * 16
        padded = np.zeros((tall, width), np.float32)
        padded[:rows, :cols] = table
        parts.append(padded)
        at += tall
    return where, np.concatenate(parts).astype(ml_dtypes.bfloat16)


def kernel(where, n_z, n_y, load, start, mask, stiff, tab, out, xs, upd, inv, idle, ss, vb, sb, rb, mr, ms, cs, cr, rs, cx, cu, cinv, cidle, css, crhs, cvb,
           wmat, send_sem, recv_sem, msend, mrecv, csend, crecv, rsend, rrecv):
    nx = load.shape[-1]
    half = nx // 2
    gz, gy = lax.axis_index("gz"), lax.axis_index("gy")

    def t(name, rows=None):
        at, r, c = where[name]
        return tab[at : at + (rows or r), :c]

    def dot(a, b):
        return jnp.dot(a, b, preferred_element_type=F32)

    def exists(dz, dy):
        ok = None
        for delta, pos, n in ((dz, gz, n_z), (dy, gy, n_y)):
            if delta:
                test = pos > 0 if delta < 0 else pos < n - 1
                ok = test if ok is None else jnp.logical_and(ok, test)
        return ok

    barrier = pltpu.get_barrier_semaphore()
    count = 0
    for dz, dy in NEAR:
        ok = exists(dz, dy)
        count = count + ok.astype(jnp.int32)

        @pl.when(ok)
        def _():
            pl.semaphore_signal(barrier, inc=1, device_id=(gz + dz, gy + dy), device_id_type=MESH)

    for k, (dz, dy) in enumerate(NEAR):
        at, size = SPAN[k]

        @pl.when(jnp.logical_not(exists(dz, dy)))
        def _():
            for p in range(4):
                rb[p, at : at + size] = jnp.zeros((size, nx), BF16)
            slot = ((dz + 1) * 3 + dy + 1) * 16
            cr[slot : slot + 16] = jnp.zeros((16, half), BF16)
            if (dz, dy) in MASK_SPAN:
                m = MASK_SPAN[dz, dy]
                mr[m : m + 16] = jnp.zeros((16, nx), BF16)
            rs[dz + 1, :, (dy + 1) * 16 : (dy + 2) * 16] = jnp.zeros((5, 16, half), BF16)

    def field_copy(p, k):
        dz, dy = NEAR[k]
        back = NEAR.index((-dz, -dy))
        at, size = SPAN[k]
        to = SPAN[back][0]
        return pltpu.make_async_remote_copy(
            src_ref=sb.at[p, at : at + size], dst_ref=rb.at[p, to : to + size],
            send_sem=send_sem.at[p, k], recv_sem=recv_sem.at[p, back],
            device_id=(gz + dz, gy + dy), device_id_type=MESH)

    def field_arrival(p, k):
        at, size = SPAN[k]
        return pltpu.make_async_remote_copy(
            src_ref=sb.at[p, at : at + size], dst_ref=rb.at[p, at : at + size],
            send_sem=send_sem.at[p, k], recv_sem=recv_sem.at[p, k],
            device_id=(gz, gy), device_id_type=MESH)

    def mask_copy(k, dz, dy):
        at = 16 * k
        to = MASK_SPAN[-dz, -dy]
        return pltpu.make_async_remote_copy(
            src_ref=ms.at[at : at + 16], dst_ref=mr.at[to : to + 16],
            send_sem=msend.at[k], recv_sem=mrecv.at[k],
            device_id=(gz + dz, gy + dy), device_id_type=MESH)

    def scale_copy(k):
        dz, dy = NEAR[k]
        to = ((1 - dz) * 3 + 1 - dy) * 16
        return pltpu.make_async_remote_copy(
            src_ref=cs.at[...], dst_ref=cr.at[to : to + 16],
            send_sem=csend.at[k], recv_sem=crecv.at[NEAR.index((-dz, -dy))],
            device_id=(gz + dz, gy + dy), device_id_type=MESH)

    def rhs_part(dz):
        return (0, 5) if dz == 0 else ((0, 3) if dz < 0 else (2, 3))

    def rhs_copy(k):
        dz, dy = NEAR[k]
        first, n = rhs_part(dz)
        to = (1 - dy) * 16
        return pltpu.make_async_remote_copy(
            src_ref=rs.at[1, first : first + n, 16:32], dst_ref=rs.at[1 - dz, first : first + n, to : to + 16],
            send_sem=rsend.at[k], recv_sem=rrecv.at[NEAR.index((-dz, -dy))],
            device_id=(gz + dz, gy + dy), device_id_type=MESH)

    mask_to = [(1, 0), (0, 1), (1, 1)]

    def pack_field(p, planes):
        own = jnp.concatenate(planes, axis=0).astype(BF16)
        sb[p, 0:128] = dot(t("sel"), own).astype(BF16)
        zero = jnp.zeros((8, nx), F32)
        sb[p, 128:160] = jnp.concatenate(planes[0:3] + [zero], axis=0).astype(BF16)
        sb[p, 160:192] = jnp.concatenate(planes[21:24] + [zero], axis=0).astype(BF16)

    def send_field(p):
        for k, (dz, dy) in enumerate(NEAR):

            @pl.when(exists(dz, dy))
            def _():
                field_copy(p, k).start()

    def await_field(p):
        for k, (dz, dy) in enumerate(NEAR):

            @pl.when(exists(dz, dy))
            def _():
                field_arrival(p, k).wait_recv()

    pack_field(0, [start[d, z] for z in range(B) for d in range(3)])
    mask_own = jnp.concatenate([mask[z] for z in range(B)], axis=0).astype(F32).astype(BF16)
    mr[0:64] = mask_own
    picked = dot(t("mask_sel"), mask_own).astype(BF16)
    ms[...] = picked[0:48]
    cs[...] = dot(picked[48:64], t("pairs")).astype(BF16)
    cr[64:80] = cs[...]

    pl.semaphore_wait(barrier, count)
    send_field(0)
    for k, (dz, dy) in enumerate(mask_to):

        @pl.when(exists(dz, dy))
        def _():
            mask_copy(k, dz, dy).start()

    for k, (dz, dy) in enumerate(NEAR):

        @pl.when(exists(dz, dy))
        def _():
            scale_copy(k).start()

    stiff_bf = stiff[...]
    stiff_wide = stiff_bf.astype(F32)
    eye = lax.broadcasted_iota(jnp.int32, (EDOF, EDOF), 0) == lax.broadcasted_iota(jnp.int32, (EDOF, EDOF), 1)
    diag_mat = jnp.where(eye, stiff_wide, 0.0)
    bound = jnp.max(jnp.sum(jnp.abs(stiff_wide), axis=1, keepdims=True) / jnp.sum(diag_mat, axis=1, keepdims=True), axis=0, keepdims=True)
    rows_of = dot(t("rep"), stiff_bf).astype(BF16)
    total = None
    for cz2 in range(2):
        for cy2 in range(2):
            name = "%d%d" % (cz2, cy2)
            term = dot(rows_of, t("pick" + name, EDOF)) * t("keep" + name).astype(F32)
            total = term if total is None else total + term
    wmat[...] = total.astype(BF16)
    diag_bf = diag_mat.astype(BF16)
    diag_col = jnp.sum(dot(t("rep"), diag_bf), axis=1, keepdims=True)
    diag_col_x = jnp.sum(dot(t("rep_x"), diag_bf), axis=1, keepdims=True)

    def shift_up(v):
        lane = lax.broadcasted_iota(jnp.int32, v.shape, 1)
        return jnp.where(lane == 0, 0.0, pltpu.roll(v, 1, axis=1))

    def shift_down(v):
        n = v.shape[1]
        lane = lax.broadcasted_iota(jnp.int32, v.shape, 1)
        return jnp.where(lane == n - 1, 0.0, pltpu.roll(v, n - 1, axis=1))

    def diagonal(scale, z, d):
        sums = []
        for c in range(2):
            s = None
            for cz in range(2):
                for cy in range(2):
                    at = (4 * cz + 2 * cy + c) * 24 + d * 8
                    term = diag_col[at : at + 8] * scale(z - cz, cy)
                    s = term if s is None else s + term
            sums.append(s)
        return sums[0] + shift_up(sums[1])

    def apply(planes, scale_now, scale_below):
        terms = dot(wmat[...], planes)
        sums = []
        for c in range(2):
            parts = []
            for d in range(3):
                s = None
                for cz, sc in ((0, scale_now), (1, scale_below)):
                    for cy in range(2):
                        at = (4 * cz + 2 * cy + c) * 24 + d * 8
                        term = terms[at : at + 8] * sc[cy * 8 : cy * 8 + 8]
                        s = term if s is None else s + term
                parts.append(s)
            sums.append(jnp.concatenate(parts, axis=0))
        return sums[0] + shift_up(sums[1])

    def put_plane(ref, z, rows):
        ref[z, 0:32] = rows.astype(BF16)
        ref[z, 32:64] = shift_down(rows).astype(BF16)

    def build(p, x_of):
        placed = dot(t("put"), rb[p, 0:128])
        for z in range(B):
            put_plane(vb, z + 1, jnp.concatenate([x_of(z, d) for d in range(3)] + [placed[8 * z + 8 : 8 * z + 16]], axis=0))
        for z, at in ((0, 128), (B + 1, 160)):
            put_plane(vb, z, jnp.concatenate([rb[p, at : at + 32].astype(F32)[0:24], placed[8 * z : 8 * z + 8]], axis=0))

    for k, (dz, dy) in enumerate(mask_to):

        @pl.when(exists(-dz, -dy))
        def _():
            mask_copy(k, dz, dy).wait_recv()

    ss[...] = dot(t("mask_put"), mr[...]).reshape(B + 1, 16, nx)

    def prepare(z, carry):
        for d in range(3):
            dg = diagonal(lambda layer, cy: ss[layer + 1, cy * 8 : cy * 8 + 8], z, d)
            no = jnp.where(dg == 0.0, 1.0, 0.0)
            inv[z, d * 8 : d * 8 + 8] = 1.0 / ((dg + no) * bound)
            if d == 0:
                idle[z] = no
        return carry

    lax.fori_loop(0, B, prepare, 0)

    ratio = (1.0 + LOW) / (1.0 - LOW)
    rho = [1.0 / ratio]
    for _ in range(2):
        rho.append(1.0 / (2.0 * ratio - rho[-1]))
    steps = [(0.0, 1.0 / (0.5 * (1.0 + LOW)))]
    for i in range(2):
        steps.append((rho[i + 1] * rho[i], 2.0 * rho[i + 1] / (0.5 * (1.0 - LOW))))

    def stack(ref, z):
        return jnp.concatenate([ref[0, z], ref[1, z], ref[2, z]], axis=0)

    def three(v):
        return jnp.concatenate([v, v, v], axis=0)

    for p in range(4):
        if p > 0:
            pack_field(p, [xs[z, 8 * d : 8 * d + 8] for z in range(B) for d in range(3)])
            send_field(p)
        await_field(p)
        if p == 0:
            build(p, lambda z, d: start[d, z])
        else:
            build(p, lambda z, d: xs[z, 8 * d : 8 * d + 8])

        def plane(z):
            x = stack(start, z) if p == 0 else xs[z]
            kv = apply(vb[pl.ds(z, 3)].reshape(192, nx), ss[z + 1], ss[z])
            r = stack(load, z) - kv - three(idle[z]) * x
            if p < 3:
                u = steps[p][1] * inv[z] * r
                if p > 0:
                    u = u + steps[p][0] * upd[z]
                xs[z] = x + u
                upd[z] = u
            else:
                upd[z] = r

        def two(i, carry):
            for j in range(4):
                plane(4 * i + j)
            return carry

        lax.fori_loop(0, B // 4, two, 0)

    def split(v):
        hi = v.astype(BF16)
        return hi, (v - hi.astype(F32)).astype(BF16)

    hi, lo = split(upd[...].reshape(192, nx))
    narrow = dot(t("shrink"), hi) + dot(t("shrink"), lo)
    hi, lo = split(narrow)
    partial = dot(hi, t("down")) + dot(lo, t("down"))
    hi, lo = split(partial)
    rs[1, :, 16:32] = hi.reshape(5, 16, half)
    rs[1, :, 48:64] = lo.reshape(5, 16, half)
    for k, (dz, dy) in enumerate(NEAR):

        @pl.when(exists(dz, dy))
        def _():
            rhs_copy(k).start()

    for k, (dz, dy) in enumerate(NEAR):

        @pl.when(exists(dz, dy))
        def _():
            scale_copy(NEAR.index((-dz, -dy))).wait_recv()

    css[...] = dot(t("cs_put"), cr[...]).reshape(10, 32, half)
    last_z, last_y = gz == n_z - 1, gy == n_y - 1
    row8 = lax.broadcasted_iota(jnp.int32, (8, half), 0)
    good_y = jnp.where(jnp.logical_and(last_y, row8 >= C + 1), 0.0, 1.0)
    for k in range(9):
        good = good_y
        if k - 2 >= C:
            good = good * jnp.where(last_z, 0.0, 1.0)
        for d in range(3):
            dg = diagonal(lambda layer, cy: css[layer + 1, cy * 8 : cy * 8 + 8], k, d)
            no = jnp.where(dg == 0.0, 1.0, 0.0)
            cinv[k, d * 8 : d * 8 + 8] = good / ((dg + no) * bound)
            if d == 0:
                cidle[k] = no
        sums = []
        for c in range(2):
            s = None
            for cz in range(2):
                for cy in range(2):
                    at = (4 * cz + 2 * cy + c) * 8
                    term = diag_col_x[at : at + 8] * css[k + 1 - cz, 16 + cy * 8 : 24 + cy * 8]
                    s = term if s is None else s + term
            sums.append(s)
        dg = sums[0] + shift_up(sums[1])
        no = jnp.where(dg == 0.0, 1.0, 0.0)
        extra = 1.0 / ((dg + no) * bound)
        if k - 2 >= C:
            extra = extra * jnp.where(last_z, 0.0, 1.0)
        cinv[k, 24:32] = extra

    for k, (dz, dy) in enumerate(NEAR):

        @pl.when(exists(dz, dy))
        def _():
            rhs_copy(NEAR.index((-dz, -dy))).wait_recv()

    for k in range(9):
        kz = k - 2
        total = None
        for zs, at in ((0, kz + C), (1, kz), (2, kz - C)):
            if 0 <= at <= C:
                rows = 64 if zs == 1 else 48
                where_at = where["gather"][0]
                term = dot(tab[where_at : where_at + 32, :rows], rs[zs, at, 0:rows])
                total = term if total is None else total + term
        crhs[k] = total[0:24]
        x = steps[0][1] * cinv[k] * total
        cx[k] = x[0:24]
        cu[k] = x[0:24]
        put_plane(cvb, k, x)

    zero8 = jnp.zeros((8, half), F32)
    for p, (first, last) in ((1, (1, 7)), (2, (2, 6))):
        for k in range(first, last + 1):
            kv = apply(cvb[k - 1 : k + 2].reshape(192, half), css[k + 1], css[k])
            x = cx[k]
            r = crhs[k] - kv - three(cidle[k]) * x
            u = steps[p][0] * cu[k] + steps[p][1] * cinv[k, 0:24] * r
            cx[k] = x + u
            cu[k] = u
        if p == 1:
            for k in range(first, last + 1):
                put_plane(cvb, k, jnp.concatenate([cx[k], zero8], axis=0))

    fix = cx[2:7].reshape(120, half).astype(BF16)
    hi, lo = split(dot(t("grow"), fix))
    for c in range(2):
        side = dot(hi, t("up%d" % c)) + dot(lo, t("up%d" % c))
        lanes = slice(c * half, (c + 1) * half)
        for z in range(B):
            for d in range(3):
                at = z * 24 + d * 8
                out[d, z, :, lanes] = xs[z, 8 * d : 8 * d + 8, lanes] + side[at : at + 8]

    for k, (dz, dy) in enumerate(NEAR):

        @pl.when(exists(dz, dy))
        def _():
            for p in range(4):
                field_copy(p, k).wait_send()
            scale_copy(k).wait_send()
            rhs_copy(k).wait_send()

    for k, (dz, dy) in enumerate(mask_to):

        @pl.when(exists(dz, dy))
        def _():
            mask_copy(k, dz, dy).wait_send()


def body(n_z, n_y, load, start, mask, stiff):
    nx = load.shape[-1]
    half = nx // 2
    where, packed = pack_tables(nx)
    dma = pltpu.SemaphoreType.DMA
    vmem = pl.BlockSpec(memory_space=pltpu.VMEM)
    return pl.pallas_call(
        functools.partial(kernel, where, n_z, n_y),
        out_shape=jax.ShapeDtypeStruct(load.shape, F32),
        in_specs=[vmem] * 5,
        out_specs=vmem,
        scratch_shapes=[
            pltpu.VMEM((B, 24, nx), F32),
            pltpu.VMEM((B, 24, nx), F32),
            pltpu.VMEM((B, 24, nx), F32),
            pltpu.VMEM((B, 8, nx), F32),
            pltpu.VMEM((B + 1, 16, nx), F32),
            pltpu.VMEM((B + 2, 64, nx), BF16),
            pltpu.VMEM((4, 192, nx), BF16),
            pltpu.VMEM((4, 192, nx), BF16),
            pltpu.VMEM((112, nx), BF16),
            pltpu.VMEM((48, nx), BF16),
            pltpu.VMEM((16, half), BF16),
            pltpu.VMEM((144, half), BF16),
            pltpu.VMEM((3, 5, 64, half), BF16),
            pltpu.VMEM((9, 24, half), F32),
            pltpu.VMEM((9, 24, half), F32),
            pltpu.VMEM((9, 32, half), F32),
            pltpu.VMEM((9, 8, half), F32),
            pltpu.VMEM((10, 32, half), F32),
            pltpu.VMEM((9, 24, half), F32),
            pltpu.VMEM((9, 64, half), BF16),
            pltpu.VMEM((192, 192), BF16),
            dma((4, 8)), dma((4, 8)), dma((3,)), dma((3,)), dma((8,)), dma((8,)), dma((8,)), dma((8,)),
        ],
        compiler_params=pltpu.CompilerParams(collective_id=0, has_side_effects=True, vmem_limit_bytes=48 * 1024 * 1024),
    )(load, start, mask, stiff, jnp.asarray(packed))


def solution(mesh):
    in_specs = (P(None, "gz", "gy", None), P(None, "gz", "gy", None), P("gz", "gy", None), P())
    out_specs = P(None, "gz", "gy", None)
    fn = functools.partial(body, mesh.shape["gz"], mesh.shape["gy"])
    return jax.shard_map(fn, mesh=mesh, in_specs=in_specs, out_specs=out_specs, check_vma=False)
```

```python
import functools

import jax
import jax.numpy as jnp
import ml_dtypes
import numpy as np
from jax import lax
from jax.experimental import pallas as pl
from jax.experimental.pallas import tpu as pltpu
from jax.sharding import PartitionSpec as P

DOF = 3
EDOF = 24
B = 8
C = B // 2
LOW = 0.1
MESH = pl.DeviceIdType.MESH
F32, BF16 = jnp.float32, jnp.bfloat16

NEAR = [(-1, -1), (-1, 1), (1, -1), (1, 1), (0, -1), (0, 1), (-1, 0), (1, 0)]
EDGE = {-1: (0, 3), 0: (0, 5), 1: (2, 3)}
RHS_ROWS = [32, 32, 32, 32, 48, 48, 48, 48]
RHS_AT = [0, 32, 64, 96, 128, 176, 224, 272]
RHS_ALL = 320


def col_code(col):
    if col < 144:
        return col // 48, col % 48 // 24, col % 24 // 8, col % 8
    p, sx, r = (col - 144) // 16, col % 16 // 8, col % 8
    if r < 6:
        return p, sx, r % 3, -1 if r < 3 else 8
    return None


def tables(nx):
    half = nx // 2
    out = {}
    rep = np.zeros((192, EDOF))
    for r in range(192):
        rep[r, (r // 24) * 3 + (r % 24) // 8] = 1
    out["rep"] = rep
    rep_x = np.zeros((64, EDOF))
    for q in range(8):
        for d in range(3):
            rep_x[q * 8 + d, q * 3 + d] = 1
    out["rep_x"] = rep_x
    for cz2 in range(2):
        for cy2 in range(2):
            pick = np.zeros((32, 192))
            keep = np.zeros((192, 192))
            for col in range(192):
                code = col_code(col)
                if code is None:
                    continue
                p, sx, d, y2 = code
                pick[3 * (4 * cz2 + 2 * cy2 + sx) + d, col] = 1
                for r in range(192):
                    q, y = r // 24, r % 8
                    cz, cy = q // 4, (q // 2) % 2
                    if p == 1 - cz + cz2 and y2 == y - cy + cy2:
                        keep[r, col] = 1
            out["pick%d%d" % (cz2, cy2)] = pick
            out["keep%d%d" % (cz2, cy2)] = keep
    sel_y = np.zeros((48, 192))
    for z in range(B):
        for d in range(3):
            sel_y[z * 3 + d, z * 24 + d * 8] = 1
            sel_y[24 + z * 3 + d, z * 24 + d * 8 + 7] = 1
    out["sel_y"] = sel_y
    for b in range(4):
        sel = np.zeros((64, 192))
        put = np.zeros((16, 64))
        for k, (z, y) in enumerate([(0, 0), (0, 7), (7, 0), (7, 7)]):
            for d in range(3):
                sel[16 * k + 3 * b + d, z * 24 + d * 8 + y] = 1
                put[8 * (k // 2) + 3 * (k % 2) + d, 16 * k + 3 * b + d] = 1
        out["sel_c%d" % b] = sel
        out["put_c%d" % b] = put
    for h in range(2):
        put = np.zeros((64, 96))
        for d in range(3):
            for z in range(B):
                put[z * 8 + d, h * 24 + z * 3 + d] = 1
                put[z * 8 + 3 + d, 48 + h * 24 + z * 3 + d] = 1
        out["put_y%d" % h] = put
    mask_sel = np.zeros((48, 64))
    for i in range(8):
        mask_sel[i, 56 + i] = 1
        mask_sel[8 + i, i * 8 + 7] = 1
    mask_sel[16, 63] = 1
    for z in range(B):
        for y in range(B):
            mask_sel[32 + (z // 2) * C + y // 2, z * 8 + y] = 0.25
    out["mask_sel"] = mask_sel
    mask_put = np.zeros((144, 96))
    for layer in range(-1, B):
        for y in range(B):
            for cy in range(2):
                row, y2 = (layer + 1) * 16 + cy * 8 + y, y - cy
                if layer >= 0:
                    mask_put[row, layer * 8 + y2 if y2 >= 0 else 72 + layer] = 1
                else:
                    mask_put[row, 64 + y2 if y2 >= 0 else 80] = 1
    out["mask_put"] = mask_put
    pairs = np.zeros((nx, half))
    down = np.zeros((nx, half))
    for i in range(nx):
        pairs[i, i // 2] = 1
        if i % 2 == 0:
            down[i, i // 2] = 1
        else:
            down[i, i // 2] = 0.5
            if i // 2 + 1 < half:
                down[i, i // 2 + 1] = 0.5
    out["pairs"], out["down"] = pairs, down
    up = down.T
    out["up"] = up
    cs_put = np.zeros((320, 144))

    def place(index):
        return (index + C) // C, (index + C) % C

    for layer in range(-3, 7):
        zs, kz = place(layer)
        base = (layer + 3) * 32
        for t in range(8):
            for cy in range(2):
                ys, ky = place(t - 1 - cy)
                cs_put[base + cy * 8 + t, (zs * 3 + ys) * 16 + kz * C + ky] = 1
        for d in range(3):
            for cy in range(2):
                ys, ky = place(-2 - cy)
                cs_put[base + 16 + cy * 8 + d, (zs * 3 + ys) * 16 + kz * C + ky] = 1
    out["cs_put"] = cs_put
    line = np.zeros((C + 1, B))
    for i in range(B):
        if i % 2 == 0:
            line[i // 2, i] = 1
        else:
            line[i // 2, i] = 0.5
            line[i // 2 + 1, i] = 0.5
    shrink = np.zeros((80, 192))
    grow = np.zeros((192, 120))
    for k in range(C + 1):
        for j in range(C + 1):
            for z in range(B):
                for y in range(B):
                    for d in range(3):
                        w = line[k, z] * line[j, y]
                        shrink[k * 16 + j * 3 + d, z * 24 + d * 8 + y] = w
                        grow[z * 24 + d * 8 + y, k * 24 + d * 8 + j + 1] = w
    out["shrink"], out["grow"] = shrink, grow
    hand = np.zeros((RHS_ALL, 80))
    gather = np.zeros((288, RHS_ALL + 160))

    def message(dz, dy):
        (z0, nz), (y0, ny) = EDGE[dz], EDGE[dy]
        return [(k, y, d) for k in range(z0, z0 + nz) for y in range(y0, y0 + ny) for d in range(3)]

    for n, (dz, dy) in enumerate(NEAR):
        for i, (k, y, d) in enumerate(message(dz, dy)):
            hand[RHS_AT[n] + i, k * 16 + y * 3 + d] = 1
    sources = [(RHS_AT[n], dz, dy, message(-dz, -dy)) for n, (dz, dy) in enumerate(NEAR)]
    own = {(k, y, d): k * 16 + y * 3 + d for k in range(5) for y in range(5) for d in range(3)}
    for at, dz, dy, rows in sources:
        for i, (k, y, d) in enumerate(rows):
            k2, y2 = k + C * dz, y + C * dy
            if -2 <= k2 <= 6 and -1 <= y2 <= 6:
                gather[(k2 + 2) * 32 + d * 8 + y2 + 1, at + i] = 1
            if -2 <= k2 <= 6 and y2 == -2:
                gather[(k2 + 2) * 32 + 24 + d, at + i] = 1
    for (k, y, d), i in own.items():
        for at in (RHS_ALL, RHS_ALL + 80):
            gather[(k + 2) * 32 + d * 8 + y + 1, at + i] = 1
    out["hand"], out["gather"] = hand, gather
    return out


EARLY = ["sel_y", "sel_c0", "sel_c1", "sel_c2", "sel_c3", "mask_sel"]


def pack_tables(nx):
    all_tables = tables(nx)
    wide = [n for n, v in all_tables.items() if v.shape[1] > 256]
    rest = [n for n in all_tables if n not in EARLY and n not in wide]
    where, packed = {}, []
    for group, names in enumerate((EARLY, rest, wide)):
        width = max(all_tables[n].shape[1] for n in names)
        width = -(-width // 128) * 128
        parts, at = [], 0
        for name in names:
            rows, cols = all_tables[name].shape
            where[name] = (group, at, rows, cols)
            tall = -(-rows // 16) * 16
            padded = np.zeros((tall, width), np.float32)
            padded[:rows, :cols] = all_tables[name]
            parts.append(padded)
            at += tall
        packed.append(np.concatenate(parts).astype(ml_dtypes.bfloat16))
    return where, packed


def kernel(where, n_z, n_y, load_h, start_h, mask_h, stiff_h, tab0_h, tab1_h, tab2_h, out, load, start, mask, stiff, tab0, tab1, tab2,
           xs, upd, inv, idle, ss, vb, vh, sw, sc, rw, rc, mr, ms, cs, cr, rsend_buf, rr, cx, cu, cinv, cidle, css, crhs, cvb, cvh,
           wmat, local_sem, send_sem, recv_sem, msend, mrecv, csend, crecv, rsend, rrecv):
    nx = load.shape[-1]
    half, quarter = nx // 2, nx // 4
    gz, gy = lax.axis_index("gz"), lax.axis_index("gy")
    moves = {}
    for k, (name, src, dst) in enumerate([("start", start_h, start), ("tab0", tab0_h, tab0), ("mask", mask_h, mask), ("tab1", tab1_h, tab1),
                                          ("stiff", stiff_h, stiff), ("load", load_h, load), ("tab2", tab2_h, tab2)]):
        moves[name] = pltpu.make_async_copy(src, dst, local_sem.at[k])
        moves[name].start()

    def t(name, rows=None):
        group, at, r, c = where[name]
        return (tab0, tab1, tab2)[group][at : at + (rows or r), :c]

    def dot(a, b):
        return jnp.dot(a, b, preferred_element_type=F32)

    def exists(dz, dy):
        ok = None
        for delta, pos, n in ((dz, gz, n_z), (dy, gy, n_y)):
            if delta:
                test = pos > 0 if delta < 0 else pos < n - 1
                ok = test if ok is None else jnp.logical_and(ok, test)
        return ok

    mask_to = [(1, 0), (0, 1), (1, 1)]
    barrier = pltpu.get_barrier_semaphore()
    count = 0
    for dz, dy in NEAR:
        ok = exists(dz, dy)
        count = count + ok.astype(jnp.int32)

        @pl.when(ok)
        def _():
            pl.semaphore_signal(barrier, inc=1, device_id=(gz + dz, gy + dy), device_id_type=MESH)

    for k, (dz, dy) in enumerate(NEAR):

        @pl.when(jnp.logical_not(exists(dz, dy)))
        def _():
            if k < 4:
                rc[:, 16 * k : 16 * k + 16] = jnp.zeros((4, 16, quarter), BF16)
            else:
                rw[:, k - 4] = jnp.zeros((4, 48, half), BF16)
            slot = ((dz + 1) * 3 + dy + 1) * 16
            cr[slot : slot + 16] = jnp.zeros((16, half), BF16)
            if (-dz, -dy) in mask_to:
                mr[mask_to.index((-dz, -dy))] = jnp.zeros((16, half), BF16)
            rr[RHS_AT[k] : RHS_AT[k] + RHS_ROWS[k]] = jnp.zeros((RHS_ROWS[k], half), BF16)

    def push(src, dst, send, recv, k):
        dz, dy = NEAR[k]
        return pltpu.make_async_remote_copy(
            src_ref=src, dst_ref=dst, send_sem=send, recv_sem=recv, device_id=(gz + dz, gy + dy), device_id_type=MESH)

    def back(k):
        return NEAR.index((-NEAR[k][0], -NEAR[k][1]))

    def field_copy(p, k):
        j = back(k)
        if k < 4:
            src, dst = sc.at[p, 16 * k : 16 * k + 16], rc.at[p, 16 * j : 16 * j + 16]
        else:
            src, dst = sw.at[p, k - 4], rw.at[p, j - 4]
        return push(src, dst, send_sem.at[p, k], recv_sem.at[p, j], k)

    def mask_copy(m):
        return push(ms.at[m], mr.at[m], msend.at[m], mrecv.at[m], NEAR.index(mask_to[m]))

    def scale_copy(k):
        dz, dy = NEAR[k]
        to = ((1 - dz) * 3 + 1 - dy) * 16
        return push(cs, cr.at[to : to + 16], csend.at[k], crecv.at[back(k)], k)

    def rhs_copy(k):
        j, n = back(k), RHS_ROWS[k]
        return push(rsend_buf.at[RHS_AT[k] : RHS_AT[k] + n], rr.at[RHS_AT[j] : RHS_AT[j] + n], rsend.at[k], rrecv.at[j], k)

    def halves(v):
        return jnp.concatenate([v[:, :half], v[:, half:]], axis=0)

    def joined(v):
        n = v.shape[0] // 2
        return jnp.concatenate([v[:n], v[n:]], axis=1)

    def pack_field(p, planes):
        own = jnp.concatenate(planes, axis=0).astype(BF16)
        corner = None
        for b in range(4):
            term = dot(t("sel_c%d" % b), own[:, b * quarter : (b + 1) * quarter])
            corner = term if corner is None else corner + term
        sc[p] = corner.astype(BF16)
        rows = dot(t("sel_y"), own)
        sw[p, 0] = halves(rows[0:24]).astype(BF16)
        sw[p, 1] = halves(rows[24:48]).astype(BF16)
        sw[p, 2] = halves(jnp.concatenate(planes[0:3], axis=0)).astype(BF16)
        sw[p, 3] = halves(jnp.concatenate(planes[21:24], axis=0)).astype(BF16)

    def each(copy, do, ks=range(8)):
        for k in ks:

            @pl.when(exists(*NEAR[k]))
            def _():
                do(copy(k))

    def begin(c):
        c.start()

    def arrived(copy):
        each(lambda k: copy(back(k)), lambda c: c.wait_recv())

    moves["start"].wait()
    moves["tab0"].wait()
    pack_field(0, [start[d, z] for z in range(B) for d in range(3)])
    moves["mask"].wait()
    mask_wide = jnp.concatenate([mask[z] for z in range(B)], axis=0).astype(F32)
    picked = dot(t("mask_sel"), mask_wide.astype(BF16))
    for m in range(3):
        ms[m] = halves(picked[8 * m : 8 * m + 8]).astype(BF16)

    pl.semaphore_wait(barrier, count)
    each(lambda k: field_copy(0, k), begin)
    for m in range(3):

        @pl.when(exists(*mask_to[m]))
        def _():
            mask_copy(m).start()

    moves["tab1"].wait()
    moves["stiff"].wait()
    stiff_bf = stiff[...]
    stiff_wide = stiff_bf.astype(F32)
    eye = lax.broadcasted_iota(jnp.int32, (EDOF, EDOF), 0) == lax.broadcasted_iota(jnp.int32, (EDOF, EDOF), 1)
    diag_mat = jnp.where(eye, stiff_wide, 0.0)
    bound = jnp.max(jnp.sum(jnp.abs(stiff_wide), axis=1, keepdims=True) / jnp.sum(diag_mat, axis=1, keepdims=True), axis=0, keepdims=True)
    rows_of = dot(t("rep"), stiff_bf).astype(BF16)
    total = None
    for cz2 in range(2):
        for cy2 in range(2):
            name = "%d%d" % (cz2, cy2)
            term = dot(rows_of, t("pick" + name, EDOF)) * t("keep" + name).astype(F32)
            total = term if total is None else total + term
    wmat[...] = total.astype(BF16)
    diag_bf = diag_mat.astype(BF16)
    diag_col = jnp.sum(dot(t("rep"), diag_bf), axis=1, keepdims=True)
    diag_col_x = jnp.sum(dot(t("rep_x"), diag_bf), axis=1, keepdims=True)

    def shift_up(v):
        lane = lax.broadcasted_iota(jnp.int32, v.shape, 1)
        return jnp.where(lane == 0, 0.0, pltpu.roll(v, 1, axis=1))

    def shift_down(v):
        n = v.shape[1]
        lane = lax.broadcasted_iota(jnp.int32, v.shape, 1)
        return jnp.where(lane == n - 1, 0.0, pltpu.roll(v, n - 1, axis=1))

    def diagonal(scale, z, d):
        sums = []
        for c in range(2):
            s = None
            for cz in range(2):
                for cy in range(2):
                    at = (4 * cz + 2 * cy + c) * 24 + d * 8
                    term = diag_col[at : at + 8] * scale(z - cz, cy)
                    s = term if s is None else s + term
            sums.append(s)
        return sums[0] + shift_up(sums[1])

    def apply(planes, scale_now, scale_below):
        terms = dot(wmat[...], planes)
        sums = []
        for c in range(2):
            parts = []
            for d in range(3):
                s = None
                for cz, sc in ((0, scale_now), (1, scale_below)):
                    for cy in range(2):
                        at = (4 * cz + 2 * cy + c) * 24 + d * 8
                        term = terms[at : at + 8] * sc[cy * 8 : cy * 8 + 8]
                        s = term if s is None else s + term
                parts.append(s)
            sums.append(jnp.concatenate(parts, axis=0))
        return sums[0] + shift_up(sums[1])

    def put_plane(ref, z, rows):
        ref[z] = jnp.concatenate([rows, shift_down(rows)], axis=0).astype(BF16)

    def build_own(x_of):
        for z in range(B):
            put_plane(vb, z + 1, jnp.concatenate([x_of(z, d) for d in range(3)], axis=0))

    def build_halo(p):
        sides = rw[p, 0:2].reshape(96, half)
        inner = jnp.concatenate([dot(t("put_y%d" % h), sides) for h in range(2)], axis=1)
        ends = jnp.concatenate([dot(t("put_c%d" % b), rc[p]) for b in range(4)], axis=1)
        for z in range(B):
            put_plane(vh, z + 1, inner[8 * z : 8 * z + 8])
        for k, z in enumerate((0, B + 1)):
            put_plane(vh, z, ends[8 * k : 8 * k + 8])
            put_plane(vb, z, joined(rw[p, 2 + k].astype(F32)))

    def planes_of(own, edge, z, n):
        return jnp.concatenate([own[pl.ds(z, 3)].reshape(144, n), edge[pl.ds(z, 3)].reshape(48, n)], axis=0)

    build_own(lambda z, d: start[d, z])
    cs[...] = dot(picked[32:48].astype(BF16), t("pairs")).astype(BF16)
    cr[64:80] = cs[...]

    for m in range(3):

        @pl.when(exists(-mask_to[m][0], -mask_to[m][1]))
        def _():
            mask_copy(m).wait_recv()

    came = [joined(mr[m].astype(F32)) for m in range(3)]
    all_masks = jnp.concatenate([mask_wide] + came + [jnp.zeros((8, nx), F32)], axis=0).astype(BF16)
    ss[...] = dot(t("mask_put"), all_masks).reshape(B + 1, 16, nx)

    def prepare(z, carry):
        for d in range(3):
            dg = diagonal(lambda layer, cy: ss[layer + 1, cy * 8 : cy * 8 + 8], z, d)
            no = jnp.where(dg == 0.0, 1.0, 0.0)
            inv[z, d * 8 : d * 8 + 8] = 1.0 / ((dg + no) * bound)
            if d == 0:
                idle[z] = no
        return carry

    lax.fori_loop(0, B, prepare, 0)

    ratio = (1.0 + LOW) / (1.0 - LOW)
    rho = [1.0 / ratio]
    for _ in range(2):
        rho.append(1.0 / (2.0 * ratio - rho[-1]))
    steps = [(0.0, 1.0 / (0.5 * (1.0 + LOW)))]
    for i in range(2):
        steps.append((rho[i + 1] * rho[i], 2.0 * rho[i + 1] / (0.5 * (1.0 - LOW))))

    def stack(ref, z):
        return jnp.concatenate([ref[0, z], ref[1, z], ref[2, z]], axis=0)

    def three(v):
        return jnp.concatenate([v, v, v], axis=0)

    moves["load"].wait()
    moves["tab2"].wait()
    for p in range(4):
        if p > 0:
            pack_field(p, [xs[z, 8 * d : 8 * d + 8] for z in range(B) for d in range(3)])
            each(lambda k: field_copy(p, k), begin)
            if p == 1:
                each(scale_copy, begin)
            build_own(lambda z, d: xs[z, 8 * d : 8 * d + 8])
        arrived(lambda k: field_copy(p, k))
        build_halo(p)

        def plane(z):
            x = stack(start, z) if p == 0 else xs[z]
            kv = apply(planes_of(vb, vh, z, nx), ss[z + 1], ss[z])
            r = stack(load, z) - kv - three(idle[z]) * x
            if p < 3:
                u = steps[p][1] * inv[z] * r
                if p > 0:
                    u = u + steps[p][0] * upd[z]
                xs[z] = x + u
                upd[z] = u
            else:
                upd[z] = r

        def two(i, carry):
            for j in range(4):
                plane(4 * i + j)
            return carry

        lax.fori_loop(0, B // 4, two, 0)

    def split(v):
        hi = v.astype(BF16)
        return hi, (v - hi.astype(F32)).astype(BF16)

    hi, lo = split(upd[...].reshape(192, nx))
    narrow = dot(t("shrink"), hi) + dot(t("shrink"), lo)
    hi, lo = split(narrow)
    partial = dot(hi, t("down")) + dot(lo, t("down"))
    hi, lo = split(partial)
    rsend_buf[...] = dot(t("hand"), hi).astype(BF16)
    each(rhs_copy, begin)
    rr[RHS_ALL : RHS_ALL + 80] = hi
    rr[RHS_ALL + 80 : RHS_ALL + 160] = lo

    arrived(scale_copy)
    css[...] = dot(t("cs_put"), cr[...]).reshape(10, 32, half)
    last_z, last_y = gz == n_z - 1, gy == n_y - 1
    row8 = lax.broadcasted_iota(jnp.int32, (8, half), 0)
    good_y = jnp.where(jnp.logical_and(last_y, row8 >= C + 1), 0.0, 1.0)
    for k in range(9):
        good = good_y
        if k - 2 >= C:
            good = good * jnp.where(last_z, 0.0, 1.0)
        for d in range(3):
            dg = diagonal(lambda layer, cy: css[layer + 1, cy * 8 : cy * 8 + 8], k, d)
            no = jnp.where(dg == 0.0, 1.0, 0.0)
            cinv[k, d * 8 : d * 8 + 8] = good / ((dg + no) * bound)
            if d == 0:
                cidle[k] = no
        sums = []
        for c in range(2):
            s = None
            for cz in range(2):
                for cy in range(2):
                    at = (4 * cz + 2 * cy + c) * 8
                    term = diag_col_x[at : at + 8] * css[k + 1 - cz, 16 + cy * 8 : 24 + cy * 8]
                    s = term if s is None else s + term
            sums.append(s)
        dg = sums[0] + shift_up(sums[1])
        no = jnp.where(dg == 0.0, 1.0, 0.0)
        extra = 1.0 / ((dg + no) * bound)
        if k - 2 >= C:
            extra = extra * jnp.where(last_z, 0.0, 1.0)
        cinv[k, 24:32] = extra

    arrived(rhs_copy)
    right = dot(t("gather"), rr[...])
    for k in range(9):
        total = right[32 * k : 32 * k + 32]
        crhs[k] = total[0:24]
        x = steps[0][1] * cinv[k] * total
        cx[k] = x[0:24]
        cu[k] = x[0:24]
        put_plane(cvb, k, x[0:24])
        put_plane(cvh, k, x[24:32])

    for p, (first, last) in ((1, (1, 7)), (2, (2, 6))):
        for k in range(first, last + 1):
            kv = apply(planes_of(cvb, cvh, k - 1, half), css[k + 1], css[k])
            x = cx[k]
            r = crhs[k] - kv - three(cidle[k]) * x
            u = steps[p][0] * cu[k] + steps[p][1] * cinv[k, 0:24] * r
            cx[k] = x + u
            cu[k] = u
        if p == 1:
            for k in range(first, last + 1):
                put_plane(cvb, k, cx[k])
                cvh[k] = jnp.zeros((16, half), BF16)

    fix = cx[2:7].reshape(120, half).astype(BF16)
    hi, lo = split(dot(t("grow"), fix))
    side = dot(hi, t("up")) + dot(lo, t("up"))
    for z in range(B):
        for d in range(3):
            at = z * 24 + d * 8
            out[d, z] = xs[z, 8 * d : 8 * d + 8] + side[at : at + 8]

    for p in range(4):
        each(lambda k: field_copy(p, k), lambda c: c.wait_send())
    each(scale_copy, lambda c: c.wait_send())
    each(rhs_copy, lambda c: c.wait_send())
    for m in range(3):

        @pl.when(exists(*mask_to[m]))
        def _():
            mask_copy(m).wait_send()


def body(n_z, n_y, load, start, mask, stiff):
    nx = load.shape[-1]
    half, quarter = nx // 2, nx // 4
    where, packed = pack_tables(nx)
    given = [load, start, mask, stiff] + [jnp.asarray(v) for v in packed]
    dma = pltpu.SemaphoreType.DMA
    vmem = pl.BlockSpec(memory_space=pltpu.VMEM)
    hbm = pl.BlockSpec(memory_space=pltpu.HBM)
    return pl.pallas_call(
        functools.partial(kernel, where, n_z, n_y),
        out_shape=jax.ShapeDtypeStruct(load.shape, F32),
        in_specs=[hbm] * len(given),
        out_specs=vmem,
        scratch_shapes=[pltpu.VMEM(v.shape, v.dtype) for v in given]
        + [
            pltpu.VMEM((B, 24, nx), F32),
            pltpu.VMEM((B, 24, nx), F32),
            pltpu.VMEM((B, 24, nx), F32),
            pltpu.VMEM((B, 8, nx), F32),
            pltpu.VMEM((B + 1, 16, nx), F32),
            pltpu.VMEM((B + 2, 48, nx), BF16),
            pltpu.VMEM((B + 2, 16, nx), BF16),
            pltpu.VMEM((4, 4, 48, half), BF16),
            pltpu.VMEM((4, 64, quarter), BF16),
            pltpu.VMEM((4, 4, 48, half), BF16),
            pltpu.VMEM((4, 64, quarter), BF16),
            pltpu.VMEM((3, 16, half), BF16),
            pltpu.VMEM((3, 16, half), BF16),
            pltpu.VMEM((16, half), BF16),
            pltpu.VMEM((144, half), BF16),
            pltpu.VMEM((RHS_ALL, half), BF16),
            pltpu.VMEM((RHS_ALL + 160, half), BF16),
            pltpu.VMEM((9, 24, half), F32),
            pltpu.VMEM((9, 24, half), F32),
            pltpu.VMEM((9, 32, half), F32),
            pltpu.VMEM((9, 8, half), F32),
            pltpu.VMEM((10, 32, half), F32),
            pltpu.VMEM((9, 24, half), F32),
            pltpu.VMEM((9, 48, half), BF16),
            pltpu.VMEM((9, 16, half), BF16),
            pltpu.VMEM((192, 192), BF16),
            dma((7,)), dma((4, 8)), dma((4, 8)), dma((3,)), dma((3,)), dma((8,)), dma((8,)), dma((8,)), dma((8,)),
        ],
        compiler_params=pltpu.CompilerParams(collective_id=0, has_side_effects=True, vmem_limit_bytes=48 * 1024 * 1024),
    )(*given)


def solution(mesh):
    in_specs = (P(None, "gz", "gy", None), P(None, "gz", "gy", None), P("gz", "gy", None), P())
    out_specs = P(None, "gz", "gy", None)
    fn = functools.partial(body, mesh.shape["gz"], mesh.shape["gy"])
    return jax.shard_map(fn, mesh=mesh, in_specs=in_specs, out_specs=out_specs, check_vma=False)
```

```python
import functools

import jax
import jax.numpy as jnp
import ml_dtypes
import numpy as np
from jax import lax
from jax.experimental import pallas as pl
from jax.experimental.pallas import tpu as pltpu
from jax.sharding import PartitionSpec as P

DOF = 3
EDOF = 24
B = 8
C = B // 2
LOW = 0.1
MESH = pl.DeviceIdType.MESH
F32, BF16 = jnp.float32, jnp.bfloat16

NEAR = [(-1, -1), (-1, 1), (1, -1), (1, 1), (0, -1), (0, 1), (-1, 0), (1, 0)]
EDGE = {-1: (0, 3), 0: (0, 5), 1: (2, 3)}
RHS_ROWS = [32, 32, 32, 32, 48, 48, 48, 48]
RHS_AT = [0, 32, 64, 96, 128, 176, 224, 272]
RHS_ALL = 320


def col_code(col):
    if col < 144:
        return col // 48, col % 48 // 24, col % 24 // 8, col % 8
    p, sx, r = (col - 144) // 16, col % 16 // 8, col % 8
    if r < 6:
        return p, sx, r % 3, -1 if r < 3 else 8
    return None


def tables(nx):
    half = nx // 2
    out = {}
    rep = np.zeros((192, EDOF))
    for r in range(192):
        rep[r, (r // 24) * 3 + (r % 24) // 8] = 1
    out["rep"] = rep
    rep_x = np.zeros((64, EDOF))
    for q in range(8):
        for d in range(3):
            rep_x[q * 8 + d, q * 3 + d] = 1
    out["rep_x"] = rep_x
    for cz2 in range(2):
        for cy2 in range(2):
            pick = np.zeros((32, 192))
            keep = np.zeros((192, 192))
            for col in range(192):
                code = col_code(col)
                if code is None:
                    continue
                p, sx, d, y2 = code
                pick[3 * (4 * cz2 + 2 * cy2 + sx) + d, col] = 1
                for r in range(192):
                    q, y = r // 24, r % 8
                    cz, cy = q // 4, (q // 2) % 2
                    if p == 1 - cz + cz2 and y2 == y - cy + cy2:
                        keep[r, col] = 1
            out["pick%d%d" % (cz2, cy2)] = pick
            out["keep%d%d" % (cz2, cy2)] = keep
    sel = np.zeros((80, 192))
    for d in range(3):
        for z in range(B):
            sel[z * 3 + d, z * 24 + d * 8] = 1
            sel[24 + z * 3 + d, z * 24 + d * 8 + 7] = 1
        for k, (dz, dy) in enumerate(NEAR[:4]):
            z, y = 7 if dz > 0 else 0, 7 if dy > 0 else 0
            sel[48 + 8 * k + (0 if dz > 0 else 3) + d, z * 24 + d * 8 + y] = 1
    out["sel"] = sel
    rep_y = np.zeros((192, EDOF))
    rows_y = []
    for r in range(192):
        side, cz, cx, d, z = r // 96, r // 48 % 2, r // 24 % 2, r // 8 % 3, r % 8
        rep_y[r, 3 * (4 * cz + 2 * (1 - side) + cx) + d] = 1
        rows_y.append((side, cz, z))
    out["rep_y"] = rep_y
    for cz2 in range(2):
        pick = np.zeros((32, 128))
        keep = np.zeros((192, 128))
        for col in range(128):
            side, sx, rc = col // 64, col // 32 % 2, col % 32
            if rc >= 30:
                continue
            z2 = rc // 3 if rc < 24 else (-1 if rc < 27 else 8)
            pick[3 * (4 * cz2 + 2 * side + sx) + rc % 3, col] = 1
            for r, (row_side, cz, z) in enumerate(rows_y):
                if row_side == side and z2 == z - cz + cz2:
                    keep[r, col] = 1
        out["pick_y%d" % cz2], out["keep_y%d" % cz2] = pick, keep
    mask_sel = np.zeros((48, 64))
    for i in range(8):
        mask_sel[i, 56 + i] = 1
        mask_sel[8 + i, i * 8 + 7] = 1
    mask_sel[16, 63] = 1
    for z in range(B):
        for y in range(B):
            mask_sel[32 + (z // 2) * C + y // 2, z * 8 + y] = 0.25
    out["mask_sel"] = mask_sel
    mask_put = np.zeros((176, 96))
    for z in range(B):
        for cz in range(2):
            layer = z - cz
            mask_put[144 + cz * 8 + z, 72 + layer if layer >= 0 else 80] = 1
            mask_put[160 + cz * 8 + z, layer * 8 + 7 if layer >= 0 else 71] = 1
    for layer in range(-1, B):
        for y in range(B):
            for cy in range(2):
                row, y2 = (layer + 1) * 16 + cy * 8 + y, y - cy
                if layer >= 0:
                    mask_put[row, layer * 8 + y2 if y2 >= 0 else 72 + layer] = 1
                else:
                    mask_put[row, 64 + y2 if y2 >= 0 else 80] = 1
    out["mask_put"] = mask_put
    pairs = np.zeros((nx, half))
    down = np.zeros((nx, half))
    for i in range(nx):
        pairs[i, i // 2] = 1
        if i % 2 == 0:
            down[i, i // 2] = 1
        else:
            down[i, i // 2] = 0.5
            if i // 2 + 1 < half:
                down[i, i // 2 + 1] = 0.5
    out["pairs"], out["down"] = pairs, down
    up = down.T
    out["up"] = up
    cs_put = np.zeros((320, 144))

    def place(index):
        return (index + C) // C, (index + C) % C

    for layer in range(-3, 7):
        zs, kz = place(layer)
        base = (layer + 3) * 32
        for t in range(8):
            for cy in range(2):
                ys, ky = place(t - 1 - cy)
                cs_put[base + cy * 8 + t, (zs * 3 + ys) * 16 + kz * C + ky] = 1
        for d in range(3):
            for cy in range(2):
                ys, ky = place(-2 - cy)
                cs_put[base + 16 + cy * 8 + d, (zs * 3 + ys) * 16 + kz * C + ky] = 1
    out["cs_put"] = cs_put
    line = np.zeros((C + 1, B))
    for i in range(B):
        if i % 2 == 0:
            line[i // 2, i] = 1
        else:
            line[i // 2, i] = 0.5
            line[i // 2 + 1, i] = 0.5
    shrink = np.zeros((80, 192))
    grow = np.zeros((192, 120))
    for k in range(C + 1):
        for j in range(C + 1):
            for z in range(B):
                for y in range(B):
                    for d in range(3):
                        w = line[k, z] * line[j, y]
                        shrink[k * 16 + j * 3 + d, z * 24 + d * 8 + y] = w
                        grow[z * 24 + d * 8 + y, k * 24 + d * 8 + j + 1] = w
    out["shrink"], out["grow"] = shrink, grow
    hand = np.zeros((RHS_ALL, 80))
    gather = np.zeros((288, RHS_ALL + 160))

    def message(dz, dy):
        (z0, nz), (y0, ny) = EDGE[dz], EDGE[dy]
        return [(k, y, d) for k in range(z0, z0 + nz) for y in range(y0, y0 + ny) for d in range(3)]

    for n, (dz, dy) in enumerate(NEAR):
        for i, (k, y, d) in enumerate(message(dz, dy)):
            hand[RHS_AT[n] + i, k * 16 + y * 3 + d] = 1
    sources = [(RHS_AT[n], dz, dy, message(-dz, -dy)) for n, (dz, dy) in enumerate(NEAR)]
    own = {(k, y, d): k * 16 + y * 3 + d for k in range(5) for y in range(5) for d in range(3)}
    for at, dz, dy, rows in sources:
        for i, (k, y, d) in enumerate(rows):
            k2, y2 = k + C * dz, y + C * dy
            if -2 <= k2 <= 6 and -1 <= y2 <= 6:
                gather[(k2 + 2) * 32 + d * 8 + y2 + 1, at + i] = 1
            if -2 <= k2 <= 6 and y2 == -2:
                gather[(k2 + 2) * 32 + 24 + d, at + i] = 1
    for (k, y, d), i in own.items():
        for at in (RHS_ALL, RHS_ALL + 80):
            gather[(k + 2) * 32 + d * 8 + y + 1, at + i] = 1
    out["hand"], out["gather"] = hand, gather
    return out


EARLY = ["sel", "mask_sel"]


def pack_tables(nx):
    all_tables = tables(nx)
    wide = [n for n, v in all_tables.items() if v.shape[1] > 256]
    rest = [n for n in all_tables if n not in EARLY and n not in wide]
    where, packed = {}, []
    for group, names in enumerate((EARLY, rest, wide)):
        width = max(all_tables[n].shape[1] for n in names)
        width = -(-width // 128) * 128
        parts, at = [], 0
        for name in names:
            rows, cols = all_tables[name].shape
            where[name] = (group, at, rows, cols)
            tall = -(-rows // 16) * 16
            padded = np.zeros((tall, width), np.float32)
            padded[:rows, :cols] = all_tables[name]
            parts.append(padded)
            at += tall
        packed.append(np.concatenate(parts).astype(ml_dtypes.bfloat16))
    return where, packed


def kernel(where, n_z, n_y, load_h, start_h, mask_h, stiff_h, tab0_h, tab1_h, tab2_h, out, load, start, mask, stiff, tab0, tab1, tab2,
           xs, upd, inv, idle, res, edge, ss, se, vb, sw, sc, rw, rc, mr, ms, cs, cr, rsend_buf, rr, cx, cu, cinv, cidle, css, crhs, cvb, cvh,
           wmat, wside, local_sem, send_sem, recv_sem, msend, mrecv, csend, crecv, rsend, rrecv):
    nx = load.shape[-1]
    half, quarter = nx // 2, nx // 4
    gz, gy = lax.axis_index("gz"), lax.axis_index("gy")
    moves = {}
    for k, (name, src, dst) in enumerate([("start", start_h, start), ("tab0", tab0_h, tab0), ("mask", mask_h, mask), ("tab1", tab1_h, tab1),
                                          ("stiff", stiff_h, stiff), ("load", load_h, load), ("tab2", tab2_h, tab2)]):
        moves[name] = pltpu.make_async_copy(src, dst, local_sem.at[k])
        moves[name].start()

    def t(name, rows=None):
        group, at, r, c = where[name]
        return (tab0, tab1, tab2)[group][at : at + (rows or r), :c]

    def dot(a, b):
        return jnp.dot(a, b, preferred_element_type=F32)

    def exists(dz, dy):
        ok = None
        for delta, pos, n in ((dz, gz, n_z), (dy, gy, n_y)):
            if delta:
                test = pos > 0 if delta < 0 else pos < n - 1
                ok = test if ok is None else jnp.logical_and(ok, test)
        return ok

    mask_to = [(1, 0), (0, 1), (1, 1)]
    barrier = pltpu.get_barrier_semaphore()
    count = 0
    for dz, dy in NEAR:
        ok = exists(dz, dy)
        count = count + ok.astype(jnp.int32)

        @pl.when(ok)
        def _():
            pl.semaphore_signal(barrier, inc=1, device_id=(gz + dz, gy + dy), device_id_type=MESH)

    for k, (dz, dy) in enumerate(NEAR):

        @pl.when(jnp.logical_not(exists(dz, dy)))
        def _():
            if k < 4:
                rc[:, k] = jnp.zeros((4, 32, quarter), BF16)
            else:
                rw[:, k - 4] = jnp.zeros((4, 48, half), BF16)
            slot = ((dz + 1) * 3 + dy + 1) * 16
            cr[slot : slot + 16] = jnp.zeros((16, half), BF16)
            if (-dz, -dy) in mask_to:
                mr[mask_to.index((-dz, -dy))] = jnp.zeros((16, half), BF16)
            rr[RHS_AT[k] : RHS_AT[k] + RHS_ROWS[k]] = jnp.zeros((RHS_ROWS[k], half), BF16)

    def push(src, dst, send, recv, k):
        dz, dy = NEAR[k]
        return pltpu.make_async_remote_copy(
            src_ref=src, dst_ref=dst, send_sem=send, recv_sem=recv, device_id=(gz + dz, gy + dy), device_id_type=MESH)

    def back(k):
        return NEAR.index((-NEAR[k][0], -NEAR[k][1]))

    def field_copy(p, k):
        j = back(k)
        if k < 4:
            src, dst = sc.at[p, k], rc.at[p, j]
        else:
            src, dst = sw.at[p, k - 4], rw.at[p, j - 4]
        return push(src, dst, send_sem.at[p, k], recv_sem.at[p, j], k)

    def mask_copy(m):
        return push(ms.at[m], mr.at[m], msend.at[m], mrecv.at[m], NEAR.index(mask_to[m]))

    def scale_copy(k):
        dz, dy = NEAR[k]
        to = ((1 - dz) * 3 + 1 - dy) * 16
        return push(cs, cr.at[to : to + 16], csend.at[k], crecv.at[back(k)], k)

    def rhs_copy(k):
        j, n = back(k), RHS_ROWS[k]
        return push(rsend_buf.at[RHS_AT[k] : RHS_AT[k] + n], rr.at[RHS_AT[j] : RHS_AT[j] + n], rsend.at[k], rrecv.at[j], k)

    def halves(v):
        return jnp.concatenate([v[:, :half], v[:, half:]], axis=0)

    def joined(v):
        n = v.shape[0] // 2
        return jnp.concatenate([v[:n], v[n:]], axis=1)

    def pack_field(p, planes):
        own = jnp.concatenate(planes, axis=0).astype(BF16)
        rows = dot(t("sel"), own)
        for k in range(4):
            v = rows[48 + 8 * k : 56 + 8 * k]
            sc[p, k] = jnp.concatenate([v[:, b * quarter : (b + 1) * quarter] for b in range(4)], axis=0).astype(BF16)
        sw[p, 0] = halves(rows[0:24]).astype(BF16)
        sw[p, 1] = halves(rows[24:48]).astype(BF16)
        sw[p, 2] = halves(jnp.concatenate(planes[0:3], axis=0)).astype(BF16)
        sw[p, 3] = halves(jnp.concatenate(planes[21:24], axis=0)).astype(BF16)

    def each(copy, do, ks=range(8)):
        for k in ks:

            @pl.when(exists(*NEAR[k]))
            def _():
                do(copy(k))

    def begin(c):
        c.start()

    def arrived(copy):
        each(lambda k: copy(back(k)), lambda c: c.wait_recv())

    moves["start"].wait()
    moves["tab0"].wait()
    pack_field(0, [start[d, z] for z in range(B) for d in range(3)])
    moves["mask"].wait()
    mask_wide = jnp.concatenate([mask[z] for z in range(B)], axis=0).astype(F32)
    picked = dot(t("mask_sel"), mask_wide.astype(BF16))
    for m in range(3):
        ms[m] = halves(picked[8 * m : 8 * m + 8]).astype(BF16)

    pl.semaphore_wait(barrier, count)
    for m in range(3):

        @pl.when(exists(*mask_to[m]))
        def _():
            mask_copy(m).start()

    each(lambda k: field_copy(0, k), begin)

    moves["tab1"].wait()
    moves["stiff"].wait()
    stiff_bf = stiff[...]
    stiff_wide = stiff_bf.astype(F32)
    eye = lax.broadcasted_iota(jnp.int32, (EDOF, EDOF), 0) == lax.broadcasted_iota(jnp.int32, (EDOF, EDOF), 1)
    diag_mat = jnp.where(eye, stiff_wide, 0.0)
    bound = jnp.max(jnp.sum(jnp.abs(stiff_wide), axis=1, keepdims=True) / jnp.sum(diag_mat, axis=1, keepdims=True), axis=0, keepdims=True)
    rows_of = dot(t("rep"), stiff_bf).astype(BF16)
    total = None
    for cz2 in range(2):
        for cy2 in range(2):
            name = "%d%d" % (cz2, cy2)
            term = dot(rows_of, t("pick" + name, EDOF)) * t("keep" + name).astype(F32)
            total = term if total is None else total + term
    wmat[...] = total.astype(BF16)
    rows_of = dot(t("rep_y"), stiff_bf).astype(BF16)
    total = None
    for cz2 in range(2):
        term = dot(rows_of, t("pick_y%d" % cz2, EDOF)) * t("keep_y%d" % cz2).astype(F32)
        total = term if total is None else total + term
    wside[...] = total.astype(BF16)
    diag_bf = diag_mat.astype(BF16)
    diag_col = jnp.sum(dot(t("rep"), diag_bf), axis=1, keepdims=True)
    diag_col_x = jnp.sum(dot(t("rep_x"), diag_bf), axis=1, keepdims=True)

    def shift_up(v):
        lane = lax.broadcasted_iota(jnp.int32, v.shape, 1)
        return jnp.where(lane == 0, 0.0, pltpu.roll(v, 1, axis=1))

    def shift_down(v):
        n = v.shape[1]
        lane = lax.broadcasted_iota(jnp.int32, v.shape, 1)
        return jnp.where(lane == n - 1, 0.0, pltpu.roll(v, n - 1, axis=1))

    def diagonal(scale, z, d):
        sums = []
        for c in range(2):
            s = None
            for cz in range(2):
                for cy in range(2):
                    at = (4 * cz + 2 * cy + c) * 24 + d * 8
                    term = diag_col[at : at + 8] * scale(z - cz, cy)
                    s = term if s is None else s + term
            sums.append(s)
        return sums[0] + shift_up(sums[1])

    def put_plane(ref, z, rows):
        ref[z] = jnp.concatenate([rows, shift_down(rows)], axis=0).astype(BF16)

    def sums_of(terms, scales):
        sums = []
        for c in range(2):
            parts = []
            for d in range(3):
                s = None
                for g, sc_g in enumerate(scales):
                    at = (2 * g + c) * 24 + d * 8
                    term = terms[at : at + 8] * sc_g
                    s = term if s is None else s + term
                parts.append(s)
            sums.append(jnp.concatenate(parts, axis=0))
        return sums[0] + shift_up(sums[1])

    def add_edges(p):
        ends = []
        for k in range(4):
            v = rc[p, k].astype(F32)
            ends.append(jnp.concatenate([v[8 * b : 8 * b + 8] for b in range(4)], axis=1))
        sides = []
        for side in range(2):
            v = jnp.concatenate([joined(rw[p, side].astype(F32)), ends[side] + ends[side + 2]], axis=0)
            sides += [v, shift_down(v)]
        terms = dot(wside[...], jnp.concatenate(sides, axis=0).astype(BF16))
        for side in range(2):
            scales = [se[16 * side + 8 * cz : 16 * side + 8 * cz + 8] for cz in range(2)]
            edge[side] = sums_of(terms[96 * side : 96 * side + 96], scales)
        for side in range(2):
            v = joined(rw[p, 2 + side].astype(F32))
            v = jnp.concatenate([v, shift_down(v)], axis=0).astype(BF16)
            none = jnp.zeros((96, nx), BF16)
            first = 96 * (1 - side)
            v = jnp.concatenate([none, v] if side else [v, none], axis=0)
            terms = dot(wmat[first : first + 96, :144], v)
            edge[2 + side] = sums_of(terms, [ss[B * side, 8 * cy : 8 * cy + 8] for cy in range(2)])

    def apply(terms, scale_now, scale_below):
        return sums_of(terms, [v[8 * cy : 8 * cy + 8] for v in (scale_now, scale_below) for cy in range(2)])

    def planes_of(own, edge, z, n):
        return jnp.concatenate([own[pl.ds(z, 3)].reshape(144, n), edge[pl.ds(z, 3)].reshape(48, n)], axis=0)

    for z in range(B):
        for d in range(3):
            xs[z, 8 * d : 8 * d + 8] = start[d, z]
    upd[...] = jnp.zeros_like(upd)
    vb[0] = jnp.zeros((48, nx), BF16)
    vb[B + 1] = jnp.zeros((48, nx), BF16)
    cs[...] = dot(picked[32:48].astype(BF16), t("pairs")).astype(BF16)
    cr[64:80] = cs[...]

    for m in range(3):

        @pl.when(exists(-mask_to[m][0], -mask_to[m][1]))
        def _():
            mask_copy(m).wait_recv()

    came = [joined(mr[m].astype(F32)) for m in range(3)]
    all_masks = jnp.concatenate([mask_wide] + came + [jnp.zeros((8, nx), F32)], axis=0).astype(BF16)
    laid = dot(t("mask_put"), all_masks)
    ss[...] = laid[0:144].reshape(B + 1, 16, nx)
    se[...] = laid[144:176]

    def prepare(z, carry):
        for d in range(3):
            dg = diagonal(lambda layer, cy: ss[layer + 1, cy * 8 : cy * 8 + 8], z, d)
            no = jnp.where(dg == 0.0, 1.0, 0.0)
            inv[z, d * 8 : d * 8 + 8] = 1.0 / ((dg + no) * bound)
            if d == 0:
                idle[z] = no
        return carry

    lax.fori_loop(0, B, prepare, 0)

    ratio = (1.0 + LOW) / (1.0 - LOW)
    rho = [1.0 / ratio]
    for _ in range(2):
        rho.append(1.0 / (2.0 * ratio - rho[-1]))
    steps = [(0.0, 1.0 / (0.5 * (1.0 + LOW)))]
    for i in range(2):
        steps.append((rho[i + 1] * rho[i], 2.0 * rho[i + 1] / (0.5 * (1.0 - LOW))))

    def stack(ref, z):
        return jnp.concatenate([ref[0, z], ref[1, z], ref[2, z]], axis=0)

    def three(v):
        return jnp.concatenate([v, v, v], axis=0)

    moves["load"].wait()
    moves["tab2"].wait()
    row24 = lax.broadcasted_iota(jnp.int32, (24, nx), 0) % 8

    def sweep(p, carry):
        def pick(values):
            v = jnp.float32(values[-1])
            for i in range(len(values) - 2, -1, -1):
                v = jnp.where(p == i, jnp.float32(values[i]), v)
            return v

        keep, gain = pick([0.0, steps[1][0], steps[2][0], 0.0]), pick([steps[0][1], steps[1][1], steps[2][1], 0.0])
        for z in range(B):
            put_plane(vb, z + 1, xs[z])
        for z in range(B):
            terms = dot(wmat[:, :144], vb[z : z + 3].reshape(144, nx))
            res[z] = stack(load, z) - apply(terms, ss[z + 1], ss[z]) - three(idle[z]) * xs[z]
        arrived(lambda k: field_copy(p, k))
        add_edges(p)
        for z in range(B):
            sides = []
            for side in range(2):
                sides.append(jnp.concatenate([jnp.broadcast_to(edge[side, 8 * d + z : 8 * d + z + 1], (8, nx)) for d in range(3)], axis=0))
            r = res[z] - jnp.where(row24 == 0, sides[0], jnp.where(row24 == 7, sides[1], 0.0))
            if z == 0:
                r = r - edge[2]
            if z == B - 1:
                r = r - edge[3]
            u = gain * inv[z] * r + keep * upd[z]
            res[z] = r
            xs[z] = xs[z] + u
            upd[z] = u

        @pl.when(p < 3)
        def _():
            pack_field(p + 1, [xs[z, 8 * d : 8 * d + 8] for z in range(B) for d in range(3)])
            each(lambda k: field_copy(p + 1, k), begin)

        @pl.when(p == 0)
        def _():
            each(scale_copy, begin)

        return carry

    lax.fori_loop(0, 4, sweep, 0)

    def split(v):
        hi = v.astype(BF16)
        return hi, (v - hi.astype(F32)).astype(BF16)

    hi, lo = split(res[...].reshape(192, nx))
    narrow = dot(t("shrink"), hi) + dot(t("shrink"), lo)
    hi, lo = split(narrow)
    partial = dot(hi, t("down")) + dot(lo, t("down"))
    hi, lo = split(partial)
    rsend_buf[...] = dot(t("hand"), hi).astype(BF16)
    each(rhs_copy, begin)
    rr[RHS_ALL : RHS_ALL + 80] = hi
    rr[RHS_ALL + 80 : RHS_ALL + 160] = lo

    arrived(scale_copy)
    css[...] = dot(t("cs_put"), cr[...]).reshape(10, 32, half)
    last_z, last_y = gz == n_z - 1, gy == n_y - 1
    row8 = lax.broadcasted_iota(jnp.int32, (8, half), 0)
    good_y = jnp.where(jnp.logical_and(last_y, row8 >= C + 1), 0.0, 1.0)
    for k in range(9):
        good = good_y
        if k - 2 >= C:
            good = good * jnp.where(last_z, 0.0, 1.0)
        for d in range(3):
            dg = diagonal(lambda layer, cy: css[layer + 1, cy * 8 : cy * 8 + 8], k, d)
            no = jnp.where(dg == 0.0, 1.0, 0.0)
            cinv[k, d * 8 : d * 8 + 8] = good / ((dg + no) * bound)
            if d == 0:
                cidle[k] = no
        sums = []
        for c in range(2):
            s = None
            for cz in range(2):
                for cy in range(2):
                    at = (4 * cz + 2 * cy + c) * 8
                    term = diag_col_x[at : at + 8] * css[k + 1 - cz, 16 + cy * 8 : 24 + cy * 8]
                    s = term if s is None else s + term
            sums.append(s)
        dg = sums[0] + shift_up(sums[1])
        no = jnp.where(dg == 0.0, 1.0, 0.0)
        extra = 1.0 / ((dg + no) * bound)
        if k - 2 >= C:
            extra = extra * jnp.where(last_z, 0.0, 1.0)
        cinv[k, 24:32] = extra

    arrived(rhs_copy)
    right = dot(t("gather"), rr[...])
    for k in range(9):
        total = right[32 * k : 32 * k + 32]
        crhs[k] = total[0:24]
        x = steps[0][1] * cinv[k] * total
        cx[k] = x[0:24]
        cu[k] = x[0:24]
        put_plane(cvb, k, x[0:24])
        put_plane(cvh, k, x[24:32])

    for p, (first, last) in ((1, (1, 7)), (2, (2, 6))):
        for k in range(first, last + 1):
            kv = apply(dot(wmat[...], planes_of(cvb, cvh, k - 1, half)), css[k + 1], css[k])
            x = cx[k]
            r = crhs[k] - kv - three(cidle[k]) * x
            u = steps[p][0] * cu[k] + steps[p][1] * cinv[k, 0:24] * r
            cx[k] = x + u
            cu[k] = u
        if p == 1:
            for k in range(first, last + 1):
                put_plane(cvb, k, cx[k])
                cvh[k] = jnp.zeros((16, half), BF16)

    fix = cx[2:7].reshape(120, half).astype(BF16)
    hi, lo = split(dot(t("grow"), fix))
    side = dot(hi, t("up")) + dot(lo, t("up"))
    for z in range(B):
        for d in range(3):
            at = z * 24 + d * 8
            out[d, z] = xs[z, 8 * d : 8 * d + 8] + side[at : at + 8]

    for p in range(4):
        each(lambda k: field_copy(p, k), lambda c: c.wait_send())
    each(scale_copy, lambda c: c.wait_send())
    each(rhs_copy, lambda c: c.wait_send())
    for m in range(3):

        @pl.when(exists(*mask_to[m]))
        def _():
            mask_copy(m).wait_send()


def body(n_z, n_y, load, start, mask, stiff):
    nx = load.shape[-1]
    half, quarter = nx // 2, nx // 4
    where, packed = pack_tables(nx)
    given = [load, start, mask, stiff] + [jnp.asarray(v) for v in packed]
    dma = pltpu.SemaphoreType.DMA
    vmem = pl.BlockSpec(memory_space=pltpu.VMEM)
    hbm = pl.BlockSpec(memory_space=pltpu.HBM)
    return pl.pallas_call(
        functools.partial(kernel, where, n_z, n_y),
        out_shape=jax.ShapeDtypeStruct(load.shape, F32),
        in_specs=[hbm] * len(given),
        out_specs=vmem,
        scratch_shapes=[pltpu.VMEM(v.shape, v.dtype) for v in given]
        + [
            pltpu.VMEM((B, 24, nx), F32),
            pltpu.VMEM((B, 24, nx), F32),
            pltpu.VMEM((B, 24, nx), F32),
            pltpu.VMEM((B, 8, nx), F32),
            pltpu.VMEM((B, 24, nx), F32),
            pltpu.VMEM((4, 24, nx), F32),
            pltpu.VMEM((B + 1, 16, nx), F32),
            pltpu.VMEM((32, nx), F32),
            pltpu.VMEM((B + 2, 48, nx), BF16),
            pltpu.VMEM((4, 4, 48, half), BF16),
            pltpu.VMEM((4, 4, 32, quarter), BF16),
            pltpu.VMEM((4, 4, 48, half), BF16),
            pltpu.VMEM((4, 4, 32, quarter), BF16),
            pltpu.VMEM((3, 16, half), BF16),
            pltpu.VMEM((3, 16, half), BF16),
            pltpu.VMEM((16, half), BF16),
            pltpu.VMEM((144, half), BF16),
            pltpu.VMEM((RHS_ALL, half), BF16),
            pltpu.VMEM((RHS_ALL + 160, half), BF16),
            pltpu.VMEM((9, 24, half), F32),
            pltpu.VMEM((9, 24, half), F32),
            pltpu.VMEM((9, 32, half), F32),
            pltpu.VMEM((9, 8, half), F32),
            pltpu.VMEM((10, 32, half), F32),
            pltpu.VMEM((9, 24, half), F32),
            pltpu.VMEM((9, 48, half), BF16),
            pltpu.VMEM((9, 16, half), BF16),
            pltpu.VMEM((192, 192), BF16),
            pltpu.VMEM((192, 128), BF16),
            dma((7,)), dma((4, 8)), dma((4, 8)), dma((3,)), dma((3,)), dma((8,)), dma((8,)), dma((8,)), dma((8,)),
        ],
        compiler_params=pltpu.CompilerParams(collective_id=0, has_side_effects=True, vmem_limit_bytes=62 * 1024 * 1024),
    )(*given)


def solution(mesh):
    in_specs = (P(None, "gz", "gy", None), P(None, "gz", "gy", None), P("gz", "gy", None), P())
    out_specs = P(None, "gz", "gy", None)
    fn = functools.partial(body, mesh.shape["gz"], mesh.shape["gy"])
    return jax.shard_map(fn, mesh=mesh, in_specs=in_specs, out_specs=out_specs, check_vma=False)
```

```python
import functools

import jax
import jax.numpy as jnp
import ml_dtypes
import numpy as np
from jax import lax
from jax.experimental import pallas as pl
from jax.experimental.pallas import tpu as pltpu
from jax.sharding import PartitionSpec as P

DOF = 3
EDOF = 24
B = 8
C = B // 2
LOW = 0.1
MESH = pl.DeviceIdType.MESH
F32, BF16 = jnp.float32, jnp.bfloat16

NEAR = [(-1, -1), (-1, 1), (1, -1), (1, 1), (0, -1), (0, 1), (-1, 0), (1, 0)]
EDGE = {-1: (0, 3), 0: (0, 5), 1: (2, 3)}
RHS_ROWS = [32, 32, 32, 32, 48, 48, 48, 48]
RHS_AT = [0, 32, 64, 96, 128, 176, 224, 272]
RHS_ALL = 320


def col_code(col):
    if col < 144:
        return col // 48, col % 48 // 24, col % 24 // 8, col % 8
    p, sx, r = (col - 144) // 16, col % 16 // 8, col % 8
    if r < 6:
        return p, sx, r % 3, -1 if r < 3 else 8
    return None


def tables(nx):
    half = nx // 2
    out = {}
    rep = np.zeros((192, EDOF))
    for r in range(192):
        rep[r, (r // 24) * 3 + (r % 24) // 8] = 1
    out["rep"] = rep
    rep_x = np.zeros((64, EDOF))
    for q in range(8):
        for d in range(3):
            rep_x[q * 8 + d, q * 3 + d] = 1
    out["rep_x"] = rep_x
    for cz2 in range(2):
        for cy2 in range(2):
            pick = np.zeros((32, 192))
            keep = np.zeros((192, 192))
            for col in range(192):
                code = col_code(col)
                if code is None:
                    continue
                p, sx, d, y2 = code
                pick[3 * (4 * cz2 + 2 * cy2 + sx) + d, col] = 1
                for r in range(192):
                    q, y = r // 24, r % 8
                    cz, cy = q // 4, (q // 2) % 2
                    if p == 1 - cz + cz2 and y2 == y - cy + cy2:
                        keep[r, col] = 1
            out["pick%d%d" % (cz2, cy2)] = pick
            out["keep%d%d" % (cz2, cy2)] = keep
    sel = np.zeros((80, 192))
    for d in range(3):
        for z in range(B):
            sel[z * 3 + d, z * 24 + d * 8] = 1
            sel[24 + z * 3 + d, z * 24 + d * 8 + 7] = 1
        for k, (dz, dy) in enumerate(NEAR[:4]):
            z, y = 7 if dz > 0 else 0, 7 if dy > 0 else 0
            sel[48 + 8 * k + d, z * 24 + d * 8 + y] = 1
            sel[52 + 8 * k + d, z * 24 + d * 8 + y] = 1
    out["sel"] = sel
    rep_y = np.zeros((192, EDOF))
    rows_y = []
    for r in range(192):
        side, cz, cx, d, z = r // 96, r // 48 % 2, r // 24 % 2, r // 8 % 3, r % 8
        rep_y[r, 3 * (4 * cz + 2 * (1 - side) + cx) + d] = 1
        rows_y.append((side, cz, z))
    out["rep_y"] = rep_y
    for cz2 in range(2):
        pick = np.zeros((32, 128))
        keep = np.zeros((192, 128))
        for col in range(128):
            side, sx, rc = col // 64, col // 32 % 2, col % 32
            if rc >= 24 and rc % 4 == 3:
                continue
            z2, d = (rc // 3, rc % 3) if rc < 24 else (-1 if rc < 28 else 8, rc % 4)
            pick[3 * (4 * cz2 + 2 * side + sx) + d, col] = 1
            for r, (row_side, cz, z) in enumerate(rows_y):
                if row_side == side and z2 == z - cz + cz2:
                    keep[r, col] = 1
        out["pick_y%d" % cz2], out["keep_y%d" % cz2] = pick, keep
    mask_sel = np.zeros((48, 64))
    for i in range(8):
        mask_sel[i, 56 + i] = 1
        mask_sel[8 + i, i * 8 + 7] = 1
    mask_sel[16, 63] = 1
    for z in range(B):
        for y in range(B):
            mask_sel[32 + (z // 2) * C + y // 2, z * 8 + y] = 0.25
    out["mask_sel"] = mask_sel
    mask_put = np.zeros((176, 96))
    for z in range(B):
        for cz in range(2):
            layer = z - cz
            mask_put[144 + cz * 8 + z, 72 + layer if layer >= 0 else 80] = 1
            mask_put[160 + cz * 8 + z, layer * 8 + 7 if layer >= 0 else 71] = 1
    for layer in range(-1, B):
        for y in range(B):
            for cy in range(2):
                row, y2 = (layer + 1) * 16 + cy * 8 + y, y - cy
                if layer >= 0:
                    mask_put[row, layer * 8 + y2 if y2 >= 0 else 72 + layer] = 1
                else:
                    mask_put[row, 64 + y2 if y2 >= 0 else 80] = 1
    out["mask_put"] = mask_put
    pairs = np.zeros((nx, half))
    down = np.zeros((nx, half))
    for i in range(nx):
        pairs[i, i // 2] = 1
        if i % 2 == 0:
            down[i, i // 2] = 1
        else:
            down[i, i // 2] = 0.5
            if i // 2 + 1 < half:
                down[i, i // 2 + 1] = 0.5
    out["pairs"], out["down"] = pairs, down
    up = down.T
    out["up"] = up
    cs_put = np.zeros((320, 144))

    def place(index):
        return (index + C) // C, (index + C) % C

    for layer in range(-3, 7):
        zs, kz = place(layer)
        base = (layer + 3) * 32
        for t in range(8):
            for cy in range(2):
                ys, ky = place(t - 1 - cy)
                cs_put[base + cy * 8 + t, (zs * 3 + ys) * 16 + kz * C + ky] = 1
        for d in range(3):
            for cy in range(2):
                ys, ky = place(-2 - cy)
                cs_put[base + 16 + cy * 8 + d, (zs * 3 + ys) * 16 + kz * C + ky] = 1
    out["cs_put"] = cs_put
    line = np.zeros((C + 1, B))
    for i in range(B):
        if i % 2 == 0:
            line[i // 2, i] = 1
        else:
            line[i // 2, i] = 0.5
            line[i // 2 + 1, i] = 0.5
    shrink = np.zeros((80, 192))
    grow = np.zeros((192, 120))
    for k in range(C + 1):
        for j in range(C + 1):
            for z in range(B):
                for y in range(B):
                    for d in range(3):
                        w = line[k, z] * line[j, y]
                        shrink[k * 16 + j * 3 + d, z * 24 + d * 8 + y] = w
                        grow[z * 24 + d * 8 + y, k * 24 + d * 8 + j + 1] = w
    out["shrink"], out["grow"] = shrink, grow
    hand = np.zeros((RHS_ALL, 80))
    gather = np.zeros((288, RHS_ALL + 80))

    def message(dz, dy):
        (z0, nz), (y0, ny) = EDGE[dz], EDGE[dy]
        return [(k, y, d) for k in range(z0, z0 + nz) for y in range(y0, y0 + ny) for d in range(3)]

    for n, (dz, dy) in enumerate(NEAR):
        for i, (k, y, d) in enumerate(message(dz, dy)):
            hand[RHS_AT[n] + i, k * 16 + y * 3 + d] = 1
    sources = [(RHS_AT[n], dz, dy, message(-dz, -dy)) for n, (dz, dy) in enumerate(NEAR)]
    own = {(k, y, d): k * 16 + y * 3 + d for k in range(5) for y in range(5) for d in range(3)}
    for at, dz, dy, rows in sources:
        for i, (k, y, d) in enumerate(rows):
            k2, y2 = k + C * dz, y + C * dy
            if -2 <= k2 <= 6 and -1 <= y2 <= 6:
                gather[(k2 + 2) * 32 + d * 8 + y2 + 1, at + i] = 1
            if -2 <= k2 <= 6 and y2 == -2:
                gather[(k2 + 2) * 32 + 24 + d, at + i] = 1
    for (k, y, d), i in own.items():
        gather[(k + 2) * 32 + d * 8 + y + 1, RHS_ALL + i] = 1
    out["hand"], out["gather"] = hand, gather
    return out


EARLY = ["sel", "mask_sel"]


def pack_tables(nx):
    all_tables = tables(nx)
    wide = [n for n, v in all_tables.items() if v.shape[1] > 256]
    rest = [n for n in all_tables if n not in EARLY and n not in wide]
    where, packed = {}, []
    for group, names in enumerate((EARLY, rest, wide)):
        width = max(all_tables[n].shape[1] for n in names)
        width = -(-width // 128) * 128
        parts, at = [], 0
        for name in names:
            rows, cols = all_tables[name].shape
            where[name] = (group, at, rows, cols)
            tall = -(-rows // 16) * 16
            padded = np.zeros((tall, width), np.float32)
            padded[:rows, :cols] = all_tables[name]
            parts.append(padded)
            at += tall
        packed.append(np.concatenate(parts).astype(ml_dtypes.bfloat16))
    return where, packed


def kernel(where, n_z, n_y, load_h, start_h, mask_h, stiff_h, tab0_h, tab1_h, tab2_h, smooth_h, fix_h, load, start, mask, stiff, tab0, tab1, tab2,
           xs, upd, inv, idle, res, edge, ss, se, vb, sw, sc, rw, rc, mr, ms, cs, cr, rsend_buf, rr, cx, cu, cinv, cidle, css, crhs, cvb, cvh,
           wmat, wside, local_sem, out_sem, send_sem, recv_sem, msend, mrecv, csend, crecv, rsend, rrecv):
    nx = load.shape[-1]
    half, quarter = nx // 2, nx // 4
    gz, gy = lax.axis_index("gz"), lax.axis_index("gy")
    moves = {}
    for k, (name, src, dst) in enumerate([("start", start_h, start), ("tab0", tab0_h, tab0), ("mask", mask_h, mask), ("tab1", tab1_h, tab1),
                                          ("stiff", stiff_h, stiff), ("load", load_h, load), ("tab2", tab2_h, tab2)]):
        moves[name] = pltpu.make_async_copy(src, dst, local_sem.at[k])
        moves[name].start()

    def t(name, rows=None):
        group, at, r, c = where[name]
        return (tab0, tab1, tab2)[group][at : at + (rows or r), :c]

    def dot(a, b):
        return jnp.dot(a, b, preferred_element_type=F32)

    def exists(dz, dy):
        ok = None
        for delta, pos, n in ((dz, gz, n_z), (dy, gy, n_y)):
            if delta:
                test = pos > 0 if delta < 0 else pos < n - 1
                ok = test if ok is None else jnp.logical_and(ok, test)
        return ok

    mask_to = [(1, 0), (0, 1), (1, 1)]
    barrier = pltpu.get_barrier_semaphore()
    count = 0
    for dz, dy in NEAR:
        ok = exists(dz, dy)
        count = count + ok.astype(jnp.int32)

        @pl.when(ok)
        def _():
            pl.semaphore_signal(barrier, inc=1, device_id=(gz + dz, gy + dy), device_id_type=MESH)

    for k, (dz, dy) in enumerate(NEAR):

        @pl.when(jnp.logical_not(exists(dz, dy)))
        def _():
            if k < 4:
                rc[:, k] = jnp.zeros((4, 16, quarter), BF16)
            else:
                rw[:, k - 4] = jnp.zeros((4, 48, half), BF16)
            slot = ((dz + 1) * 3 + dy + 1) * 16
            cr[slot : slot + 16] = jnp.zeros((16, half), BF16)
            if (-dz, -dy) in mask_to:
                mr[mask_to.index((-dz, -dy))] = jnp.zeros((16, half), BF16)
            rr[RHS_AT[k] : RHS_AT[k] + RHS_ROWS[k]] = jnp.zeros((RHS_ROWS[k], half), BF16)

    def push(src, dst, send, recv, k):
        dz, dy = NEAR[k]
        return pltpu.make_async_remote_copy(
            src_ref=src, dst_ref=dst, send_sem=send, recv_sem=recv, device_id=(gz + dz, gy + dy), device_id_type=MESH)

    def back(k):
        return NEAR.index((-NEAR[k][0], -NEAR[k][1]))

    def field_copy(p, k):
        j = back(k)
        if k < 4:
            src, dst = sc.at[p, k], rc.at[p, j]
        else:
            src, dst = sw.at[p, k - 4], rw.at[p, j - 4]
        return push(src, dst, send_sem.at[p, k], recv_sem.at[p, j], k)

    def mask_copy(m):
        return push(ms.at[m], mr.at[m], msend.at[m], mrecv.at[m], NEAR.index(mask_to[m]))

    def scale_copy(k):
        dz, dy = NEAR[k]
        to = ((1 - dz) * 3 + 1 - dy) * 16
        return push(cs, cr.at[to : to + 16], csend.at[k], crecv.at[back(k)], k)

    def rhs_copy(k):
        j, n = back(k), RHS_ROWS[k]
        return push(rsend_buf.at[RHS_AT[k] : RHS_AT[k] + n], rr.at[RHS_AT[j] : RHS_AT[j] + n], rsend.at[k], rrecv.at[j], k)

    def halves(v):
        return jnp.concatenate([v[:, :half], v[:, half:]], axis=0)

    def joined(v):
        n = v.shape[0] // 2
        return jnp.concatenate([v[:n], v[n:]], axis=1)

    low4 = lax.broadcasted_iota(jnp.int32, (8, quarter), 0) < 4

    def pack_field(p, planes):
        own = jnp.concatenate(planes, axis=0).astype(BF16)
        rows = dot(t("sel"), own)
        for k in range(4):
            v = rows[48 + 8 * k : 56 + 8 * k]
            v = [v[:, b * quarter : (b + 1) * quarter] for b in range(4)]
            sc[p, k] = jnp.concatenate([jnp.where(low4, v[0], v[1]), jnp.where(low4, v[2], v[3])], axis=0).astype(BF16)
        sw[p, 0] = halves(rows[0:24]).astype(BF16)
        sw[p, 1] = halves(rows[24:48]).astype(BF16)
        sw[p, 2] = halves(jnp.concatenate(planes[0:3], axis=0)).astype(BF16)
        sw[p, 3] = halves(jnp.concatenate(planes[21:24], axis=0)).astype(BF16)

    def each(copy, do, ks=range(8)):
        for k in ks:

            @pl.when(exists(*NEAR[k]))
            def _():
                do(copy(k))

    def begin(c):
        c.start()

    def arrived(copy):
        each(lambda k: copy(back(k)), lambda c: c.wait_recv())

    moves["start"].wait()
    moves["tab0"].wait()
    pack_field(0, [start[d, z] for z in range(B) for d in range(3)])
    moves["mask"].wait()
    mask_wide = jnp.concatenate([mask[z] for z in range(B)], axis=0).astype(F32)
    picked = dot(t("mask_sel"), mask_wide.astype(BF16))
    for m in range(3):
        ms[m] = halves(picked[8 * m : 8 * m + 8]).astype(BF16)

    pl.semaphore_wait(barrier, count)
    for m in range(3):

        @pl.when(exists(*mask_to[m]))
        def _():
            mask_copy(m).start()

    each(lambda k: field_copy(0, k), begin)

    moves["tab1"].wait()
    moves["stiff"].wait()
    stiff_bf = stiff[...]
    stiff_wide = stiff_bf.astype(F32)
    eye = lax.broadcasted_iota(jnp.int32, (EDOF, EDOF), 0) == lax.broadcasted_iota(jnp.int32, (EDOF, EDOF), 1)
    diag_mat = jnp.where(eye, stiff_wide, 0.0)
    bound = jnp.max(jnp.sum(jnp.abs(stiff_wide), axis=1, keepdims=True) / jnp.sum(diag_mat, axis=1, keepdims=True), axis=0, keepdims=True)
    rows_of = dot(t("rep"), stiff_bf).astype(BF16)
    total = None
    for cz2 in range(2):
        for cy2 in range(2):
            name = "%d%d" % (cz2, cy2)
            term = dot(rows_of, t("pick" + name, EDOF)) * t("keep" + name).astype(F32)
            total = term if total is None else total + term
    wmat[...] = total.astype(BF16)
    rows_of = dot(t("rep_y"), stiff_bf).astype(BF16)
    total = None
    for cz2 in range(2):
        term = dot(rows_of, t("pick_y%d" % cz2, EDOF)) * t("keep_y%d" % cz2).astype(F32)
        total = term if total is None else total + term
    wside[...] = total.astype(BF16)
    diag_bf = diag_mat.astype(BF16)
    diag_col = jnp.sum(dot(t("rep"), diag_bf), axis=1, keepdims=True)
    diag_col_x = jnp.sum(dot(t("rep_x"), diag_bf), axis=1, keepdims=True)

    def shift_up(v):
        lane = lax.broadcasted_iota(jnp.int32, v.shape, 1)
        return jnp.where(lane == 0, 0.0, pltpu.roll(v, 1, axis=1))

    def shift_down(v):
        n = v.shape[1]
        lane = lax.broadcasted_iota(jnp.int32, v.shape, 1)
        return jnp.where(lane == n - 1, 0.0, pltpu.roll(v, n - 1, axis=1))

    def diagonal(scale, z, d):
        sums = []
        for c in range(2):
            s = None
            for cz in range(2):
                for cy in range(2):
                    at = (4 * cz + 2 * cy + c) * 24 + d * 8
                    term = diag_col[at : at + 8] * scale(z - cz, cy)
                    s = term if s is None else s + term
            sums.append(s)
        return sums[0] + shift_up(sums[1])

    def put_plane(ref, z, rows):
        ref[z] = jnp.concatenate([rows, shift_down(rows)], axis=0).astype(BF16)

    def sums_of(terms, scales):
        sums = []
        for c in range(2):
            parts = []
            for d in range(3):
                s = None
                for g, sc_g in enumerate(scales):
                    at = (2 * g + c) * 24 + d * 8
                    term = terms[at : at + 8] * sc_g
                    s = term if s is None else s + term
                parts.append(s)
            sums.append(jnp.concatenate(parts, axis=0))
        return sums[0] + shift_up(sums[1])

    def add_edges(p):
        ends = []
        for side in range(2):
            near, far = rc[p, side].astype(F32), rc[p, side + 2].astype(F32)
            blocks = []
            for b in range(4):
                rows = slice(8 * (b // 2), 8 * (b // 2) + 8)
                if b % 2:
                    blocks.append(jnp.where(low4, pltpu.roll(near[rows], 4, axis=0), far[rows]))
                else:
                    blocks.append(jnp.where(low4, near[rows], pltpu.roll(far[rows], 4, axis=0)))
            ends.append(jnp.concatenate(blocks, axis=1))
        sides = []
        for side in range(2):
            v = jnp.concatenate([joined(rw[p, side].astype(F32)), ends[side]], axis=0)
            sides += [v, shift_down(v)]
        terms = dot(wside[...], jnp.concatenate(sides, axis=0).astype(BF16))
        for side in range(2):
            scales = [se[16 * side + 8 * cz : 16 * side + 8 * cz + 8] for cz in range(2)]
            edge[side] = sums_of(terms[96 * side : 96 * side + 96], scales)
        for side in range(2):
            v = joined(rw[p, 2 + side].astype(F32))
            v = jnp.concatenate([v, shift_down(v)], axis=0).astype(BF16)
            none = jnp.zeros((96, nx), BF16)
            first = 96 * (1 - side)
            v = jnp.concatenate([none, v] if side else [v, none], axis=0)
            terms = dot(wmat[first : first + 96, :144], v)
            edge[2 + side] = sums_of(terms, [ss[B * side, 8 * cy : 8 * cy + 8] for cy in range(2)])

    def apply(terms, scale_now, scale_below):
        return sums_of(terms, [v[8 * cy : 8 * cy + 8] for v in (scale_now, scale_below) for cy in range(2)])

    def planes_of(own, edge, z, n):
        return jnp.concatenate([own[pl.ds(z, 3)].reshape(144, n), edge[pl.ds(z, 3)].reshape(48, n)], axis=0)

    for z in range(B):
        for d in range(3):
            xs[z, 8 * d : 8 * d + 8] = start[d, z]
    upd[...] = jnp.zeros_like(upd)
    vb[0] = jnp.zeros((48, nx), BF16)
    vb[B + 1] = jnp.zeros((48, nx), BF16)
    cs[...] = dot(picked[32:48].astype(BF16), t("pairs")).astype(BF16)
    cr[64:80] = cs[...]

    for m in range(3):

        @pl.when(exists(-mask_to[m][0], -mask_to[m][1]))
        def _():
            mask_copy(m).wait_recv()

    came = [joined(mr[m].astype(F32)) for m in range(3)]
    all_masks = jnp.concatenate([mask_wide] + came + [jnp.zeros((8, nx), F32)], axis=0).astype(BF16)
    laid = dot(t("mask_put"), all_masks)
    ss[...] = laid[0:144].reshape(B + 1, 16, nx)
    se[...] = laid[144:176]

    def prepare(z, carry):
        for d in range(3):
            dg = diagonal(lambda layer, cy: ss[layer + 1, cy * 8 : cy * 8 + 8], z, d)
            no = jnp.where(dg == 0.0, 1.0, 0.0)
            inv[z, d * 8 : d * 8 + 8] = 1.0 / ((dg + no) * bound)
            if d == 0:
                idle[z] = no
        return carry

    lax.fori_loop(0, B, prepare, 0)

    ratio = (1.0 + LOW) / (1.0 - LOW)
    rho = [1.0 / ratio]
    for _ in range(2):
        rho.append(1.0 / (2.0 * ratio - rho[-1]))
    steps = [(0.0, 1.0 / (0.5 * (1.0 + LOW)))]
    for i in range(2):
        steps.append((rho[i + 1] * rho[i], 2.0 * rho[i + 1] / (0.5 * (1.0 - LOW))))

    def stack(ref, z):
        return jnp.concatenate([ref[0, z], ref[1, z], ref[2, z]], axis=0)

    def three(v):
        return jnp.concatenate([v, v, v], axis=0)

    moves["load"].wait()
    moves["tab2"].wait()
    row24 = lax.broadcasted_iota(jnp.int32, (24, nx), 0) % 8

    def sweep(p, carry):
        def pick(values):
            v = jnp.float32(values[-1])
            for i in range(len(values) - 2, -1, -1):
                v = jnp.where(p == i, jnp.float32(values[i]), v)
            return v

        keep, gain = pick([0.0, steps[1][0], steps[2][0], 0.0]), pick([steps[0][1], steps[1][1], steps[2][1], 0.0])
        for z in range(B):
            put_plane(vb, z + 1, xs[z])
        for z in range(B):
            terms = dot(wmat[:, :144], vb[z : z + 3].reshape(144, nx))
            res[z] = stack(load, z) - apply(terms, ss[z + 1], ss[z]) - three(idle[z]) * xs[z]
        arrived(lambda k: field_copy(p, k))
        add_edges(p)
        for z in range(B):
            sides = []
            for side in range(2):
                sides.append(jnp.concatenate([jnp.broadcast_to(edge[side, 8 * d + z : 8 * d + z + 1], (8, nx)) for d in range(3)], axis=0))
            r = res[z] - jnp.where(row24 == 0, sides[0], jnp.where(row24 == 7, sides[1], 0.0))
            if z == 0:
                r = r - edge[2]
            if z == B - 1:
                r = r - edge[3]
            u = gain * inv[z] * r + keep * upd[z]
            res[z] = r
            xs[z] = xs[z] + u
            upd[z] = u

        @pl.when(p < 3)
        def _():
            pack_field(p + 1, [xs[z, 8 * d : 8 * d + 8] for z in range(B) for d in range(3)])
            each(lambda k: field_copy(p + 1, k), begin)

        @pl.when(p == 0)
        def _():
            each(scale_copy, begin)

        return carry

    lax.fori_loop(0, 4, sweep, 0)

    for d in range(3):
        pltpu.make_async_copy(xs.at[:, 8 * d : 8 * d + 8], smooth_h.at[d], out_sem.at[d]).start()

    narrow = dot(t("shrink"), res[...].reshape(192, nx).astype(BF16))
    hi = dot(narrow.astype(BF16), t("down")).astype(BF16)
    rsend_buf[...] = dot(t("hand"), hi).astype(BF16)
    each(rhs_copy, begin)
    rr[RHS_ALL : RHS_ALL + 80] = hi

    arrived(scale_copy)
    css[...] = dot(t("cs_put"), cr[...]).reshape(10, 32, half)
    last_z, last_y = gz == n_z - 1, gy == n_y - 1
    row8 = lax.broadcasted_iota(jnp.int32, (8, half), 0)
    good_y = jnp.where(jnp.logical_and(last_y, row8 >= C + 1), 0.0, 1.0)
    for k in range(9):
        good = good_y
        if k - 2 >= C:
            good = good * jnp.where(last_z, 0.0, 1.0)
        for d in range(3):
            dg = diagonal(lambda layer, cy: css[layer + 1, cy * 8 : cy * 8 + 8], k, d)
            no = jnp.where(dg == 0.0, 1.0, 0.0)
            cinv[k, d * 8 : d * 8 + 8] = good / ((dg + no) * bound)
            if d == 0:
                cidle[k] = no
        sums = []
        for c in range(2):
            s = None
            for cz in range(2):
                for cy in range(2):
                    at = (4 * cz + 2 * cy + c) * 8
                    term = diag_col_x[at : at + 8] * css[k + 1 - cz, 16 + cy * 8 : 24 + cy * 8]
                    s = term if s is None else s + term
            sums.append(s)
        dg = sums[0] + shift_up(sums[1])
        no = jnp.where(dg == 0.0, 1.0, 0.0)
        extra = 1.0 / ((dg + no) * bound)
        if k - 2 >= C:
            extra = extra * jnp.where(last_z, 0.0, 1.0)
        cinv[k, 24:32] = extra

    arrived(rhs_copy)
    right = dot(t("gather"), rr[...])
    for k in range(9):
        total = right[32 * k : 32 * k + 32]
        crhs[k] = total[0:24]
        x = steps[0][1] * cinv[k] * total
        cx[k] = x[0:24]
        cu[k] = x[0:24]
        put_plane(cvb, k, x[0:24])
        put_plane(cvh, k, x[24:32])

    for p, (first, last) in ((1, (1, 7)), (2, (2, 6))):
        for k in range(first, last + 1):
            kv = apply(dot(wmat[...], planes_of(cvb, cvh, k - 1, half)), css[k + 1], css[k])
            x = cx[k]
            r = crhs[k] - kv - three(cidle[k]) * x
            u = steps[p][0] * cu[k] + steps[p][1] * cinv[k, 0:24] * r
            cx[k] = x + u
            cu[k] = u
        if p == 1:
            for k in range(first, last + 1):
                put_plane(cvb, k, cx[k])
                cvh[k] = jnp.zeros((16, half), BF16)

    fix = cx[2:7].reshape(120, half).astype(BF16)
    side = dot(dot(t("grow"), fix).astype(BF16), t("up"))
    res[...] = side.reshape(B, 24, nx)
    for d in range(3):
        pltpu.make_async_copy(res.at[:, 8 * d : 8 * d + 8], fix_h.at[d], out_sem.at[3 + d]).start()

    for p in range(4):
        each(lambda k: field_copy(p, k), lambda c: c.wait_send())
    each(scale_copy, lambda c: c.wait_send())
    each(rhs_copy, lambda c: c.wait_send())
    for m in range(3):

        @pl.when(exists(*mask_to[m]))
        def _():
            mask_copy(m).wait_send()
    for d in range(3):
        pltpu.make_async_copy(xs.at[:, 8 * d : 8 * d + 8], smooth_h.at[d], out_sem.at[d]).wait()
        pltpu.make_async_copy(res.at[:, 8 * d : 8 * d + 8], fix_h.at[d], out_sem.at[3 + d]).wait()


def body(n_z, n_y, load, start, mask, stiff):
    nx = load.shape[-1]
    half, quarter = nx // 2, nx // 4
    where, packed = pack_tables(nx)
    given = [load, start, mask, stiff] + [jnp.asarray(v) for v in packed]
    dma = pltpu.SemaphoreType.DMA
    hbm = pl.BlockSpec(memory_space=pltpu.HBM)
    smooth, fix = pl.pallas_call(
        functools.partial(kernel, where, n_z, n_y),
        out_shape=[jax.ShapeDtypeStruct(load.shape, F32)] * 2,
        in_specs=[hbm] * len(given),
        out_specs=[hbm] * 2,
        scratch_shapes=[pltpu.VMEM(v.shape, v.dtype) for v in given]
        + [
            pltpu.VMEM((B, 24, nx), F32),
            pltpu.VMEM((B, 24, nx), F32),
            pltpu.VMEM((B, 24, nx), F32),
            pltpu.VMEM((B, 8, nx), F32),
            pltpu.VMEM((B, 24, nx), F32),
            pltpu.VMEM((4, 24, nx), F32),
            pltpu.VMEM((B + 1, 16, nx), F32),
            pltpu.VMEM((32, nx), F32),
            pltpu.VMEM((B + 2, 48, nx), BF16),
            pltpu.VMEM((4, 4, 48, half), BF16),
            pltpu.VMEM((4, 4, 16, quarter), BF16),
            pltpu.VMEM((4, 4, 48, half), BF16),
            pltpu.VMEM((4, 4, 16, quarter), BF16),
            pltpu.VMEM((3, 16, half), BF16),
            pltpu.VMEM((3, 16, half), BF16),
            pltpu.VMEM((16, half), BF16),
            pltpu.VMEM((144, half), BF16),
            pltpu.VMEM((RHS_ALL, half), BF16),
            pltpu.VMEM((RHS_ALL + 80, half), BF16),
            pltpu.VMEM((9, 24, half), F32),
            pltpu.VMEM((9, 24, half), F32),
            pltpu.VMEM((9, 32, half), F32),
            pltpu.VMEM((9, 8, half), F32),
            pltpu.VMEM((10, 32, half), F32),
            pltpu.VMEM((9, 24, half), F32),
            pltpu.VMEM((9, 48, half), BF16),
            pltpu.VMEM((9, 16, half), BF16),
            pltpu.VMEM((192, 192), BF16),
            pltpu.VMEM((192, 128), BF16),
            dma((7,)), dma((6,)), dma((4, 8)), dma((4, 8)), dma((3,)), dma((3,)), dma((8,)), dma((8,)), dma((8,)), dma((8,)),
        ],
        compiler_params=pltpu.CompilerParams(collective_id=0, has_side_effects=True, vmem_limit_bytes=62 * 1024 * 1024),
    )(*given)
    return smooth + fix


def solution(mesh):
    in_specs = (P(None, "gz", "gy", None), P(None, "gz", "gy", None), P("gz", "gy", None), P())
    out_specs = P(None, "gz", "gy", None)
    fn = functools.partial(body, mesh.shape["gz"], mesh.shape["gy"])
    return jax.shard_map(fn, mesh=mesh, in_specs=in_specs, out_specs=out_specs, check_vma=False)
```

```python
import functools

import jax
import jax.numpy as jnp
import ml_dtypes
import numpy as np
from jax import lax
from jax.experimental import pallas as pl
from jax.experimental.pallas import tpu as pltpu
from jax.sharding import PartitionSpec as P

DOF = 3
EDOF = 24
B = 8
C = B // 2
LOW = 0.1
MESH = pl.DeviceIdType.MESH
F32, BF16 = jnp.float32, jnp.bfloat16

NEAR = [(-1, -1), (-1, 1), (1, -1), (1, 1), (0, -1), (0, 1), (-1, 0), (1, 0)]
EDGE = {-1: (0, 3), 0: (0, 5), 1: (2, 3)}
RHS_ROWS = [32, 32, 32, 32, 48, 48, 48, 48]
RHS_AT = [0, 32, 64, 96, 128, 176, 224, 272]
RHS_ALL = 320


def col_code(col):
    if col < 144:
        return col // 48, col % 48 // 24, col % 24 // 8, col % 8
    p, sx, r = (col - 144) // 16, col % 16 // 8, col % 8
    if r < 6:
        return p, sx, r % 3, -1 if r < 3 else 8
    return None


def tables(nx):
    half = nx // 2
    out = {}
    rep = np.zeros((192, EDOF))
    for r in range(192):
        rep[r, (r // 24) * 3 + (r % 24) // 8] = 1
    out["rep"] = rep
    rep_x = np.zeros((64, EDOF))
    for q in range(8):
        for d in range(3):
            rep_x[q * 8 + d, q * 3 + d] = 1
    out["rep_x"] = rep_x
    for cz2 in range(2):
        for cy2 in range(2):
            pick = np.zeros((32, 192))
            keep = np.zeros((192, 192))
            for col in range(192):
                code = col_code(col)
                if code is None:
                    continue
                p, sx, d, y2 = code
                pick[3 * (4 * cz2 + 2 * cy2 + sx) + d, col] = 1
                for r in range(192):
                    q, y = r // 24, r % 8
                    cz, cy = q // 4, (q // 2) % 2
                    if p == 1 - cz + cz2 and y2 == y - cy + cy2:
                        keep[r, col] = 1
            out["pick%d%d" % (cz2, cy2)] = pick
            out["keep%d%d" % (cz2, cy2)] = keep
    rep_y = np.zeros((192, EDOF))
    rows_y = []
    for r in range(192):
        side, cz, cx, d, z = r // 96, r // 48 % 2, r // 24 % 2, r // 8 % 3, r % 8
        rep_y[r, 3 * (4 * cz + 2 * (1 - side) + cx) + d] = 1
        rows_y.append((side, cz, z))
    out["rep_y"] = rep_y
    for cz2 in range(2):
        pick = np.zeros((32, 128))
        keep = np.zeros((192, 128))
        for col in range(128):
            side, sx, rc = col // 64, col // 32 % 2, col % 32
            if rc >= 24 and rc % 4 == 3:
                continue
            z2, d = (rc % 8, rc // 8) if rc < 24 else (-1 if rc < 28 else 8, rc % 4)
            pick[3 * (4 * cz2 + 2 * side + sx) + d, col] = 1
            for r, (row_side, cz, z) in enumerate(rows_y):
                if row_side == side and z2 == z - cz + cz2:
                    keep[r, col] = 1
        out["pick_y%d" % cz2], out["keep_y%d" % cz2] = pick, keep
    mask_sel = np.zeros((48, 64))
    for i in range(8):
        mask_sel[i, 56 + i] = 1
        mask_sel[8 + i, i * 8 + 7] = 1
    mask_sel[16, 63] = 1
    for z in range(B):
        for y in range(B):
            mask_sel[32 + (z // 2) * C + y // 2, z * 8 + y] = 0.25
    out["mask_sel"] = mask_sel
    mask_put = np.zeros((176, 96))
    for z in range(B):
        for cz in range(2):
            layer = z - cz
            mask_put[144 + cz * 8 + z, 72 + layer if layer >= 0 else 80] = 1
            mask_put[160 + cz * 8 + z, layer * 8 + 7 if layer >= 0 else 71] = 1
    for layer in range(-1, B):
        for y in range(B):
            for cy in range(2):
                row, y2 = (layer + 1) * 16 + cy * 8 + y, y - cy
                if layer >= 0:
                    mask_put[row, layer * 8 + y2 if y2 >= 0 else 72 + layer] = 1
                else:
                    mask_put[row, 64 + y2 if y2 >= 0 else 80] = 1
    out["mask_put"] = mask_put
    pairs = np.zeros((nx, half))
    down = np.zeros((nx, half))
    for i in range(nx):
        pairs[i, i // 2] = 1
        if i % 2 == 0:
            down[i, i // 2] = 1
        else:
            down[i, i // 2] = 0.5
            if i // 2 + 1 < half:
                down[i, i // 2 + 1] = 0.5
    out["pairs"], out["down"] = pairs, down
    up = down.T
    out["up"] = up
    cs_put = np.zeros((320, 144))

    def place(index):
        return (index + C) // C, (index + C) % C

    for layer in range(-3, 7):
        zs, kz = place(layer)
        base = (layer + 3) * 32
        for t in range(8):
            for cy in range(2):
                ys, ky = place(t - 1 - cy)
                cs_put[base + cy * 8 + t, (zs * 3 + ys) * 16 + kz * C + ky] = 1
        for d in range(3):
            for cy in range(2):
                ys, ky = place(-2 - cy)
                cs_put[base + 16 + cy * 8 + d, (zs * 3 + ys) * 16 + kz * C + ky] = 1
    out["cs_put"] = cs_put
    line = np.zeros((C + 1, B))
    for i in range(B):
        if i % 2 == 0:
            line[i // 2, i] = 1
        else:
            line[i // 2, i] = 0.5
            line[i // 2 + 1, i] = 0.5
    shrink = np.zeros((80, 192))
    grow = np.zeros((192, 120))
    for k in range(C + 1):
        for j in range(C + 1):
            for z in range(B):
                for y in range(B):
                    for d in range(3):
                        w = line[k, z] * line[j, y]
                        shrink[k * 16 + j * 3 + d, z * 24 + d * 8 + y] = w
                        grow[z * 24 + d * 8 + y, k * 24 + d * 8 + j + 1] = w
    out["shrink"], out["grow"] = shrink, grow
    hand = np.zeros((RHS_ALL, 80))
    gather = np.zeros((288, RHS_ALL + 80))

    def message(dz, dy):
        (z0, nz), (y0, ny) = EDGE[dz], EDGE[dy]
        return [(k, y, d) for k in range(z0, z0 + nz) for y in range(y0, y0 + ny) for d in range(3)]

    for n, (dz, dy) in enumerate(NEAR):
        for i, (k, y, d) in enumerate(message(dz, dy)):
            hand[RHS_AT[n] + i, k * 16 + y * 3 + d] = 1
    sources = [(RHS_AT[n], dz, dy, message(-dz, -dy)) for n, (dz, dy) in enumerate(NEAR)]
    own = {(k, y, d): k * 16 + y * 3 + d for k in range(5) for y in range(5) for d in range(3)}
    for at, dz, dy, rows in sources:
        for i, (k, y, d) in enumerate(rows):
            k2, y2 = k + C * dz, y + C * dy
            if -2 <= k2 <= 6 and -1 <= y2 <= 6:
                gather[(k2 + 2) * 32 + d * 8 + y2 + 1, at + i] = 1
            if -2 <= k2 <= 6 and y2 == -2:
                gather[(k2 + 2) * 32 + 24 + d, at + i] = 1
    for (k, y, d), i in own.items():
        gather[(k + 2) * 32 + d * 8 + y + 1, RHS_ALL + i] = 1
    out["hand"], out["gather"] = hand, gather
    return out


EARLY = ["mask_sel"]


def pack_tables(nx):
    all_tables = tables(nx)
    wide = [n for n, v in all_tables.items() if v.shape[1] > 256]
    rest = [n for n in all_tables if n not in EARLY and n not in wide]
    where, packed = {}, []
    for group, names in enumerate((EARLY, rest, wide)):
        width = max(all_tables[n].shape[1] for n in names)
        width = -(-width // 128) * 128
        parts, at = [], 0
        for name in names:
            rows, cols = all_tables[name].shape
            where[name] = (group, at, rows, cols)
            tall = -(-rows // 16) * 16
            padded = np.zeros((tall, width), np.float32)
            padded[:rows, :cols] = all_tables[name]
            parts.append(padded)
            at += tall
        packed.append(np.concatenate(parts).astype(ml_dtypes.bfloat16))
    return where, packed


def kernel(where, n_z, n_y, load_h, start_h, mask_h, stiff_h, tab0_h, tab1_h, tab2_h, smooth_h, fix_h, load, start, mask, stiff, tab0, tab1, tab2,
           xs, upd, inv, idle, res, edge, ss, se, vb, sw, sc, rw, rc, mr, ms, cs, cr, rsend_buf, rr, cx, cu, cinv, cidle, css, crhs, cvb, cvh,
           wmat, wside, local_sem, out_sem, send_sem, recv_sem, msend, mrecv, csend, crecv, rsend, rrecv):
    nx = load.shape[-1]
    half, quarter = nx // 2, nx // 4
    gz, gy = lax.axis_index("gz"), lax.axis_index("gy")
    moves = {}
    for k, (name, src, dst) in enumerate([("start", start_h, start), ("tab0", tab0_h, tab0), ("mask", mask_h, mask), ("tab1", tab1_h, tab1),
                                          ("stiff", stiff_h, stiff), ("load", load_h, load), ("tab2", tab2_h, tab2)]):
        moves[name] = pltpu.make_async_copy(src, dst, local_sem.at[k])
        moves[name].start()

    def t(name, rows=None):
        group, at, r, c = where[name]
        return (tab0, tab1, tab2)[group][at : at + (rows or r), :c]

    def dot(a, b):
        return jnp.dot(a, b, preferred_element_type=F32)

    def exists(dz, dy):
        ok = None
        for delta, pos, n in ((dz, gz, n_z), (dy, gy, n_y)):
            if delta:
                test = pos > 0 if delta < 0 else pos < n - 1
                ok = test if ok is None else jnp.logical_and(ok, test)
        return ok

    mask_to = [(1, 0), (0, 1), (1, 1)]
    barrier = pltpu.get_barrier_semaphore()
    count = 0
    for dz, dy in NEAR:
        ok = exists(dz, dy)
        count = count + ok.astype(jnp.int32)

        @pl.when(ok)
        def _():
            pl.semaphore_signal(barrier, inc=1, device_id=(gz + dz, gy + dy), device_id_type=MESH)

    for k, (dz, dy) in enumerate(NEAR):

        @pl.when(jnp.logical_not(exists(dz, dy)))
        def _():
            if k < 4:
                rc[:, k] = jnp.zeros((4, 16, quarter), BF16)
            else:
                rw[:, k - 4] = jnp.zeros((4, 48, half), BF16)
            slot = ((dz + 1) * 3 + dy + 1) * 16
            cr[slot : slot + 16] = jnp.zeros((16, half), BF16)
            if (-dz, -dy) in mask_to:
                mr[mask_to.index((-dz, -dy))] = jnp.zeros((16, half), BF16)
            rr[RHS_AT[k] : RHS_AT[k] + RHS_ROWS[k]] = jnp.zeros((RHS_ROWS[k], half), BF16)

    def push(src, dst, send, recv, k):
        dz, dy = NEAR[k]
        return pltpu.make_async_remote_copy(
            src_ref=src, dst_ref=dst, send_sem=send, recv_sem=recv, device_id=(gz + dz, gy + dy), device_id_type=MESH)

    def back(k):
        return NEAR.index((-NEAR[k][0], -NEAR[k][1]))

    def field_copy(p, k):
        j = back(k)
        if k < 4:
            src, dst = sc.at[p, k], rc.at[p, j]
        else:
            src, dst = sw.at[p, k - 4], rw.at[p, j - 4]
        return push(src, dst, send_sem.at[p, k], recv_sem.at[p, j], k)

    def mask_copy(m):
        return push(ms.at[m], mr.at[m], msend.at[m], mrecv.at[m], NEAR.index(mask_to[m]))

    def scale_copy(k):
        dz, dy = NEAR[k]
        to = ((1 - dz) * 3 + 1 - dy) * 16
        return push(cs, cr.at[to : to + 16], csend.at[k], crecv.at[back(k)], k)

    def rhs_copy(k):
        j, n = back(k), RHS_ROWS[k]
        return push(rsend_buf.at[RHS_AT[k] : RHS_AT[k] + n], rr.at[RHS_AT[j] : RHS_AT[j] + n], rsend.at[k], rrecv.at[j], k)

    def halves(v):
        return jnp.concatenate([v[:, :half], v[:, half:]], axis=0)

    def joined(v):
        n = v.shape[0] // 2
        return jnp.concatenate([v[:n], v[n:]], axis=1)

    low4 = lax.broadcasted_iota(jnp.int32, (8, quarter), 0) < 4

    row8 = lax.broadcasted_iota(jnp.int32, (8, nx), 0)

    def spread(row):
        return jnp.broadcast_to(row, (8, nx))

    def pack_field(p):
        for side, y in enumerate((0, 7)):
            rows = []
            for d in range(3):
                v = spread(xs[0, 8 * d + y : 8 * d + y + 1])
                for z in range(1, B):
                    v = jnp.where(row8 == z, spread(xs[z, 8 * d + y : 8 * d + y + 1]), v)
                rows.append(v)
            sw[p, side] = halves(jnp.concatenate(rows, axis=0)).astype(BF16)
        for k in range(4):
            z, y = 7 if NEAR[k][0] > 0 else 0, 7 if NEAR[k][1] > 0 else 0
            v = spread(xs[z, y : y + 1])
            for d in (1, 2):
                v = jnp.where(row8 % 4 == d, spread(xs[z, 8 * d + y : 8 * d + y + 1]), v)
            v = jnp.where(row8 % 4 == 3, 0.0, v)
            v = [v[:, b * quarter : (b + 1) * quarter] for b in range(4)]
            sc[p, k] = jnp.concatenate([jnp.where(low4, v[0], v[1]), jnp.where(low4, v[2], v[3])], axis=0).astype(BF16)
        sw[p, 2] = halves(xs[0]).astype(BF16)
        sw[p, 3] = halves(xs[B - 1]).astype(BF16)

    def each(copy, do, ks=range(8)):
        for k in ks:

            @pl.when(exists(*NEAR[k]))
            def _():
                do(copy(k))

    def begin(c):
        c.start()

    def arrived(copy):
        each(lambda k: copy(back(k)), lambda c: c.wait_recv())

    moves["start"].wait()
    for z in range(B):
        for d in range(3):
            xs[z, 8 * d : 8 * d + 8] = start[d, z]
    pack_field(0)
    moves["tab0"].wait()
    moves["mask"].wait()
    mask_wide = jnp.concatenate([mask[z] for z in range(B)], axis=0).astype(F32)
    picked = dot(t("mask_sel"), mask_wide.astype(BF16))
    for m in range(3):
        ms[m] = halves(picked[8 * m : 8 * m + 8]).astype(BF16)

    pl.semaphore_wait(barrier, count)
    for m in range(3):

        @pl.when(exists(*mask_to[m]))
        def _():
            mask_copy(m).start()

    each(lambda k: field_copy(0, k), begin)

    moves["tab1"].wait()
    moves["stiff"].wait()
    stiff_bf = stiff[...]
    stiff_wide = stiff_bf.astype(F32)
    eye = lax.broadcasted_iota(jnp.int32, (EDOF, EDOF), 0) == lax.broadcasted_iota(jnp.int32, (EDOF, EDOF), 1)
    diag_mat = jnp.where(eye, stiff_wide, 0.0)
    bound = jnp.max(jnp.sum(jnp.abs(stiff_wide), axis=1, keepdims=True) / jnp.sum(diag_mat, axis=1, keepdims=True), axis=0, keepdims=True)
    rows_of = dot(t("rep"), stiff_bf).astype(BF16)
    total = None
    for cz2 in range(2):
        for cy2 in range(2):
            name = "%d%d" % (cz2, cy2)
            term = dot(rows_of, t("pick" + name, EDOF)) * t("keep" + name).astype(F32)
            total = term if total is None else total + term
    wmat[...] = total.astype(BF16)
    rows_of = dot(t("rep_y"), stiff_bf).astype(BF16)
    total = None
    for cz2 in range(2):
        term = dot(rows_of, t("pick_y%d" % cz2, EDOF)) * t("keep_y%d" % cz2).astype(F32)
        total = term if total is None else total + term
    wside[...] = total.astype(BF16)
    diag_bf = diag_mat.astype(BF16)
    diag_col = jnp.sum(dot(t("rep"), diag_bf), axis=1, keepdims=True)
    diag_col_x = jnp.sum(dot(t("rep_x"), diag_bf), axis=1, keepdims=True)

    def shift_up(v):
        lane = lax.broadcasted_iota(jnp.int32, v.shape, 1)
        return jnp.where(lane == 0, 0.0, pltpu.roll(v, 1, axis=1))

    def shift_down(v):
        n = v.shape[1]
        lane = lax.broadcasted_iota(jnp.int32, v.shape, 1)
        return jnp.where(lane == n - 1, 0.0, pltpu.roll(v, n - 1, axis=1))

    def diagonal(scale, z, d):
        sums = []
        for c in range(2):
            s = None
            for cz in range(2):
                for cy in range(2):
                    at = (4 * cz + 2 * cy + c) * 24 + d * 8
                    term = diag_col[at : at + 8] * scale(z - cz, cy)
                    s = term if s is None else s + term
            sums.append(s)
        return sums[0] + shift_up(sums[1])

    def put_plane(ref, z, rows):
        ref[z] = jnp.concatenate([rows, shift_down(rows)], axis=0).astype(BF16)

    def sums_of(terms, scales):
        sums = []
        for c in range(2):
            parts = []
            for d in range(3):
                s = None
                for g, sc_g in enumerate(scales):
                    at = (2 * g + c) * 24 + d * 8
                    term = terms[at : at + 8] * sc_g
                    s = term if s is None else s + term
                parts.append(s)
            sums.append(jnp.concatenate(parts, axis=0))
        return sums[0] + shift_up(sums[1])

    def add_edges(p):
        ends = []
        for side in range(2):
            near, far = rc[p, side].astype(F32), rc[p, side + 2].astype(F32)
            blocks = []
            for b in range(4):
                rows = slice(8 * (b // 2), 8 * (b // 2) + 8)
                if b % 2:
                    blocks.append(jnp.where(low4, pltpu.roll(near[rows], 4, axis=0), far[rows]))
                else:
                    blocks.append(jnp.where(low4, near[rows], pltpu.roll(far[rows], 4, axis=0)))
            ends.append(jnp.concatenate(blocks, axis=1))
        sides = []
        for side in range(2):
            v = jnp.concatenate([joined(rw[p, side].astype(F32)), ends[side]], axis=0)
            sides += [v, shift_down(v)]
        terms = dot(wside[...], jnp.concatenate(sides, axis=0).astype(BF16))
        for side in range(2):
            scales = [se[16 * side + 8 * cz : 16 * side + 8 * cz + 8] for cz in range(2)]
            edge[side] = sums_of(terms[96 * side : 96 * side + 96], scales)
        for side in range(2):
            v = joined(rw[p, 2 + side].astype(F32))
            v = jnp.concatenate([v, shift_down(v)], axis=0).astype(BF16)
            none = jnp.zeros((96, nx), BF16)
            first = 96 * (1 - side)
            v = jnp.concatenate([none, v] if side else [v, none], axis=0)
            terms = dot(wmat[first : first + 96, :144], v)
            edge[2 + side] = sums_of(terms, [ss[B * side, 8 * cy : 8 * cy + 8] for cy in range(2)])

    def apply(terms, scale_now, scale_below):
        return sums_of(terms, [v[8 * cy : 8 * cy + 8] for v in (scale_now, scale_below) for cy in range(2)])

    def planes_of(own, edge, z, n):
        return jnp.concatenate([own[pl.ds(z, 3)].reshape(144, n), edge[pl.ds(z, 3)].reshape(48, n)], axis=0)

    upd[...] = jnp.zeros_like(upd)
    vb[0] = jnp.zeros((48, nx), BF16)
    vb[B + 1] = jnp.zeros((48, nx), BF16)
    cs[...] = dot(picked[32:48].astype(BF16), t("pairs")).astype(BF16)
    cr[64:80] = cs[...]

    for m in range(3):

        @pl.when(exists(-mask_to[m][0], -mask_to[m][1]))
        def _():
            mask_copy(m).wait_recv()

    came = [joined(mr[m].astype(F32)) for m in range(3)]
    all_masks = jnp.concatenate([mask_wide] + came + [jnp.zeros((8, nx), F32)], axis=0).astype(BF16)
    laid = dot(t("mask_put"), all_masks)
    ss[...] = laid[0:144].reshape(B + 1, 16, nx)
    se[...] = laid[144:176]

    for z in range(B):
        for d in range(3):
            dg = diagonal(lambda layer, cy: ss[layer + 1, cy * 8 : cy * 8 + 8], z, d)
            no = jnp.where(dg == 0.0, 1.0, 0.0)
            inv[z, d * 8 : d * 8 + 8] = 1.0 / ((dg + no) * bound)
            if d == 0:
                idle[z] = no

    ratio = (1.0 + LOW) / (1.0 - LOW)
    rho = [1.0 / ratio]
    for _ in range(2):
        rho.append(1.0 / (2.0 * ratio - rho[-1]))
    steps = [(0.0, 1.0 / (0.5 * (1.0 + LOW)))]
    for i in range(2):
        steps.append((rho[i + 1] * rho[i], 2.0 * rho[i + 1] / (0.5 * (1.0 - LOW))))

    def stack(ref, z):
        return jnp.concatenate([ref[0, z], ref[1, z], ref[2, z]], axis=0)

    def three(v):
        return jnp.concatenate([v, v, v], axis=0)

    moves["load"].wait()
    moves["tab2"].wait()
    row24 = lax.broadcasted_iota(jnp.int32, (24, nx), 0) % 8

    def sweep(p, carry):
        def pick(values):
            v = jnp.float32(values[-1])
            for i in range(len(values) - 2, -1, -1):
                v = jnp.where(p == i, jnp.float32(values[i]), v)
            return v

        keep, gain = pick([0.0, steps[1][0], steps[2][0], 0.0]), pick([steps[0][1], steps[1][1], steps[2][1], 0.0])
        for z in range(B):
            put_plane(vb, z + 1, xs[z])
        for z in range(B):
            terms = dot(wmat[:, :144], vb[z : z + 3].reshape(144, nx))
            res[z] = stack(load, z) - apply(terms, ss[z + 1], ss[z]) - three(idle[z]) * xs[z]
        arrived(lambda k: field_copy(p, k))
        add_edges(p)
        for z in range(B):
            sides = []
            for side in range(2):
                sides.append(jnp.concatenate([jnp.broadcast_to(edge[side, 8 * d + z : 8 * d + z + 1], (8, nx)) for d in range(3)], axis=0))
            r = res[z] - jnp.where(row24 == 0, sides[0], jnp.where(row24 == 7, sides[1], 0.0))
            if z == 0:
                r = r - edge[2]
            if z == B - 1:
                r = r - edge[3]
            u = gain * inv[z] * r + keep * upd[z]
            res[z] = r
            xs[z] = xs[z] + u
            upd[z] = u

        @pl.when(p < 3)
        def _():
            pack_field(p + 1)
            each(lambda k: field_copy(p + 1, k), begin)

        @pl.when(p == 0)
        def _():
            each(scale_copy, begin)

        return carry

    lax.fori_loop(0, 4, sweep, 0)

    for d in range(3):
        pltpu.make_async_copy(xs.at[:, 8 * d : 8 * d + 8], smooth_h.at[d], out_sem.at[d]).start()

    narrow = dot(t("shrink"), res[...].reshape(192, nx).astype(BF16))
    hi = dot(narrow.astype(BF16), t("down")).astype(BF16)
    rsend_buf[...] = dot(t("hand"), hi).astype(BF16)
    each(rhs_copy, begin)
    rr[RHS_ALL : RHS_ALL + 80] = hi

    arrived(scale_copy)
    css[...] = dot(t("cs_put"), cr[...]).reshape(10, 32, half)
    last_z, last_y = gz == n_z - 1, gy == n_y - 1
    good_y = jnp.where(jnp.logical_and(last_y, row8[:, :half] >= C + 1), 0.0, 1.0)
    for k in range(9):
        good = good_y
        if k - 2 >= C:
            good = good * jnp.where(last_z, 0.0, 1.0)
        for d in range(3):
            dg = diagonal(lambda layer, cy: css[layer + 1, cy * 8 : cy * 8 + 8], k, d)
            no = jnp.where(dg == 0.0, 1.0, 0.0)
            cinv[k, d * 8 : d * 8 + 8] = good / ((dg + no) * bound)
            if d == 0:
                cidle[k] = no
        sums = []
        for c in range(2):
            s = None
            for cz in range(2):
                for cy in range(2):
                    at = (4 * cz + 2 * cy + c) * 8
                    term = diag_col_x[at : at + 8] * css[k + 1 - cz, 16 + cy * 8 : 24 + cy * 8]
                    s = term if s is None else s + term
            sums.append(s)
        dg = sums[0] + shift_up(sums[1])
        no = jnp.where(dg == 0.0, 1.0, 0.0)
        extra = 1.0 / ((dg + no) * bound)
        if k - 2 >= C:
            extra = extra * jnp.where(last_z, 0.0, 1.0)
        cinv[k, 24:32] = extra

    arrived(rhs_copy)
    right = dot(t("gather"), rr[...])
    for k in range(9):
        total = right[32 * k : 32 * k + 32]
        crhs[k] = total[0:24]
        x = steps[0][1] * cinv[k] * total
        cx[k] = x[0:24]
        cu[k] = x[0:24]
        put_plane(cvb, k, x[0:24])
        put_plane(cvh, k, x[24:32])

    for p, (first, last) in ((1, (1, 7)), (2, (2, 6))):
        for k in range(first, last + 1):
            kv = apply(dot(wmat[...], planes_of(cvb, cvh, k - 1, half)), css[k + 1], css[k])
            x = cx[k]
            r = crhs[k] - kv - three(cidle[k]) * x
            u = steps[p][0] * cu[k] + steps[p][1] * cinv[k, 0:24] * r
            cx[k] = x + u
            cu[k] = u
        if p == 1:
            for k in range(first, last + 1):
                put_plane(cvb, k, cx[k])
                cvh[k] = jnp.zeros((16, half), BF16)

    fix = cx[2:7].reshape(120, half).astype(BF16)
    side = dot(dot(t("grow"), fix).astype(BF16), t("up"))
    res[...] = side.reshape(B, 24, nx)
    for d in range(3):
        pltpu.make_async_copy(res.at[:, 8 * d : 8 * d + 8], fix_h.at[d], out_sem.at[3 + d]).start()

    for p in range(4):
        each(lambda k: field_copy(p, k), lambda c: c.wait_send())
    each(scale_copy, lambda c: c.wait_send())
    each(rhs_copy, lambda c: c.wait_send())
    for m in range(3):

        @pl.when(exists(*mask_to[m]))
        def _():
            mask_copy(m).wait_send()
    for d in range(3):
        pltpu.make_async_copy(xs.at[:, 8 * d : 8 * d + 8], smooth_h.at[d], out_sem.at[d]).wait()
        pltpu.make_async_copy(res.at[:, 8 * d : 8 * d + 8], fix_h.at[d], out_sem.at[3 + d]).wait()


def body(n_z, n_y, load, start, mask, stiff):
    nx = load.shape[-1]
    half, quarter = nx // 2, nx // 4
    where, packed = pack_tables(nx)
    given = [load, start, mask, stiff] + [jnp.asarray(v) for v in packed]
    dma = pltpu.SemaphoreType.DMA
    hbm = pl.BlockSpec(memory_space=pltpu.HBM)
    smooth, fix = pl.pallas_call(
        functools.partial(kernel, where, n_z, n_y),
        out_shape=[jax.ShapeDtypeStruct(load.shape, F32)] * 2,
        in_specs=[hbm] * len(given),
        out_specs=[hbm] * 2,
        scratch_shapes=[pltpu.VMEM(v.shape, v.dtype) for v in given]
        + [
            pltpu.VMEM((B, 24, nx), F32),
            pltpu.VMEM((B, 24, nx), F32),
            pltpu.VMEM((B, 24, nx), F32),
            pltpu.VMEM((B, 8, nx), F32),
            pltpu.VMEM((B, 24, nx), F32),
            pltpu.VMEM((4, 24, nx), F32),
            pltpu.VMEM((B + 1, 16, nx), F32),
            pltpu.VMEM((32, nx), F32),
            pltpu.VMEM((B + 2, 48, nx), BF16),
            pltpu.VMEM((4, 4, 48, half), BF16),
            pltpu.VMEM((4, 4, 16, quarter), BF16),
            pltpu.VMEM((4, 4, 48, half), BF16),
            pltpu.VMEM((4, 4, 16, quarter), BF16),
            pltpu.VMEM((3, 16, half), BF16),
            pltpu.VMEM((3, 16, half), BF16),
            pltpu.VMEM((16, half), BF16),
            pltpu.VMEM((144, half), BF16),
            pltpu.VMEM((RHS_ALL, half), BF16),
            pltpu.VMEM((RHS_ALL + 80, half), BF16),
            pltpu.VMEM((9, 24, half), F32),
            pltpu.VMEM((9, 24, half), F32),
            pltpu.VMEM((9, 32, half), F32),
            pltpu.VMEM((9, 8, half), F32),
            pltpu.VMEM((10, 32, half), F32),
            pltpu.VMEM((9, 24, half), F32),
            pltpu.VMEM((9, 48, half), BF16),
            pltpu.VMEM((9, 16, half), BF16),
            pltpu.VMEM((192, 192), BF16),
            pltpu.VMEM((192, 128), BF16),
            dma((7,)), dma((6,)), dma((4, 8)), dma((4, 8)), dma((3,)), dma((3,)), dma((8,)), dma((8,)), dma((8,)), dma((8,)),
        ],
        compiler_params=pltpu.CompilerParams(collective_id=0, has_side_effects=True, vmem_limit_bytes=62 * 1024 * 1024),
    )(*given)
    return smooth + fix


def solution(mesh):
    in_specs = (P(None, "gz", "gy", None), P(None, "gz", "gy", None), P("gz", "gy", None), P())
    out_specs = P(None, "gz", "gy", None)
    fn = functools.partial(body, mesh.shape["gz"], mesh.shape["gy"])
    return jax.shard_map(fn, mesh=mesh, in_specs=in_specs, out_specs=out_specs, check_vma=False)
```

```python
import functools

import jax
import jax.numpy as jnp
import ml_dtypes
import numpy as np
from jax import lax
from jax.experimental import pallas as pl
from jax.experimental.pallas import tpu as pltpu
from jax.sharding import PartitionSpec as P

DOF = 3
EDOF = 24
B = 8
C = B // 2
LOW = 0.1
MESH = pl.DeviceIdType.MESH
F32, BF16 = jnp.float32, jnp.bfloat16

NEAR = [(-1, -1), (-1, 1), (1, -1), (1, 1), (0, -1), (0, 1), (-1, 0), (1, 0)]
EDGE = {-1: (0, 3), 0: (0, 5), 1: (2, 3)}
RHS_ROWS = [32, 32, 32, 32, 48, 48, 48, 48]
RHS_AT = [0, 32, 64, 96, 128, 176, 224, 272]
RHS_ALL = 320


def col_code(col):
    if col < 144:
        return col // 48, col % 48 // 24, col % 24 // 8, col % 8
    p, sx, r = (col - 144) // 16, col % 16 // 8, col % 8
    if r < 6:
        return p, sx, r % 3, -1 if r < 3 else 8
    return None


def tables(nx):
    half = nx // 2
    out = {}
    rep = np.zeros((192, EDOF))
    for r in range(192):
        rep[r, (r // 24) * 3 + (r % 24) // 8] = 1
    out["rep"] = rep
    rep_x = np.zeros((64, EDOF))
    for q in range(8):
        for d in range(3):
            rep_x[q * 8 + d, q * 3 + d] = 1
    out["rep_x"] = rep_x
    for cz2 in range(2):
        for cy2 in range(2):
            pick = np.zeros((32, 192))
            keep = np.zeros((192, 192))
            for col in range(192):
                code = col_code(col)
                if code is None:
                    continue
                p, sx, d, y2 = code
                pick[3 * (4 * cz2 + 2 * cy2 + sx) + d, col] = 1
                for r in range(192):
                    q, y = r // 24, r % 8
                    cz, cy = q // 4, (q // 2) % 2
                    if p == 1 - cz + cz2 and y2 == y - cy + cy2:
                        keep[r, col] = 1
            out["pick%d%d" % (cz2, cy2)] = pick
            out["keep%d%d" % (cz2, cy2)] = keep
    rep_y = np.zeros((192, EDOF))
    rows_y = []
    for r in range(192):
        side, cz, cx, d, z = r // 96, r // 48 % 2, r // 24 % 2, r // 8 % 3, r % 8
        rep_y[r, 3 * (4 * cz + 2 * (1 - side) + cx) + d] = 1
        rows_y.append((side, cz, z))
    out["rep_y"] = rep_y
    for cz2 in range(2):
        pick = np.zeros((32, 128))
        keep = np.zeros((192, 128))
        for col in range(128):
            side, sx, rc = col // 64, col // 32 % 2, col % 32
            if rc >= 24 and rc % 4 == 3:
                continue
            z2, d = (rc % 8, rc // 8) if rc < 24 else (-1 if rc < 28 else 8, rc % 4)
            pick[3 * (4 * cz2 + 2 * side + sx) + d, col] = 1
            for r, (row_side, cz, z) in enumerate(rows_y):
                if row_side == side and z2 == z - cz + cz2:
                    keep[r, col] = 1
        out["pick_y%d" % cz2], out["keep_y%d" % cz2] = pick, keep
    mask_sel = np.zeros((48, 64))
    for i in range(8):
        mask_sel[i, 56 + i] = 1
        mask_sel[8 + i, i * 8 + 7] = 1
    mask_sel[16, 63] = 1
    for z in range(B):
        for y in range(B):
            mask_sel[32 + (z // 2) * C + y // 2, z * 8 + y] = 0.25
    out["mask_sel"] = mask_sel
    mask_put = np.zeros((176, 96))
    for z in range(B):
        for cz in range(2):
            layer = z - cz
            mask_put[144 + cz * 8 + z, 72 + layer if layer >= 0 else 80] = 1
            mask_put[160 + cz * 8 + z, layer * 8 + 7 if layer >= 0 else 71] = 1
    for layer in range(-1, B):
        for y in range(B):
            for cy in range(2):
                row, y2 = (layer + 1) * 16 + cy * 8 + y, y - cy
                if layer >= 0:
                    mask_put[row, layer * 8 + y2 if y2 >= 0 else 72 + layer] = 1
                else:
                    mask_put[row, 64 + y2 if y2 >= 0 else 80] = 1
    out["mask_put"] = mask_put
    pairs = np.zeros((nx, half))
    down = np.zeros((nx, half))
    for i in range(nx):
        pairs[i, i // 2] = 1
        if i % 2 == 0:
            down[i, i // 2] = 1
        else:
            down[i, i // 2] = 0.5
            if i // 2 + 1 < half:
                down[i, i // 2 + 1] = 0.5
    out["pairs"], out["down"] = pairs, down
    up = down.T
    out["up"] = up
    cs_put = np.zeros((320, 144))

    def place(index):
        return (index + C) // C, (index + C) % C

    for layer in range(-3, 7):
        zs, kz = place(layer)
        base = (layer + 3) * 32
        for t in range(8):
            for cy in range(2):
                ys, ky = place(t - 1 - cy)
                cs_put[base + cy * 8 + t, (zs * 3 + ys) * 16 + kz * C + ky] = 1
        for d in range(3):
            for cy in range(2):
                ys, ky = place(-2 - cy)
                cs_put[base + 16 + cy * 8 + d, (zs * 3 + ys) * 16 + kz * C + ky] = 1
    out["cs_put"] = cs_put
    line = np.zeros((C + 1, B))
    for i in range(B):
        if i % 2 == 0:
            line[i // 2, i] = 1
        else:
            line[i // 2, i] = 0.5
            line[i // 2 + 1, i] = 0.5
    shrink = np.zeros((80, 192))
    grow = np.zeros((192, 120))
    for k in range(C + 1):
        for j in range(C + 1):
            for z in range(B):
                for y in range(B):
                    for d in range(3):
                        w = line[k, z] * line[j, y]
                        shrink[k * 16 + j * 3 + d, z * 24 + d * 8 + y] = w
                        grow[z * 24 + d * 8 + y, k * 24 + d * 8 + j + 1] = w
    out["shrink"], out["grow"] = shrink, grow
    hand = np.zeros((RHS_ALL, 80))
    gather = np.zeros((288, RHS_ALL + 80))

    def message(dz, dy):
        (z0, nz), (y0, ny) = EDGE[dz], EDGE[dy]
        return [(k, y, d) for k in range(z0, z0 + nz) for y in range(y0, y0 + ny) for d in range(3)]

    for n, (dz, dy) in enumerate(NEAR):
        for i, (k, y, d) in enumerate(message(dz, dy)):
            hand[RHS_AT[n] + i, k * 16 + y * 3 + d] = 1
    sources = [(RHS_AT[n], dz, dy, message(-dz, -dy)) for n, (dz, dy) in enumerate(NEAR)]
    own = {(k, y, d): k * 16 + y * 3 + d for k in range(5) for y in range(5) for d in range(3)}
    for at, dz, dy, rows in sources:
        for i, (k, y, d) in enumerate(rows):
            k2, y2 = k + C * dz, y + C * dy
            if -2 <= k2 <= 6 and -1 <= y2 <= 6:
                gather[(k2 + 2) * 32 + d * 8 + y2 + 1, at + i] = 1
            if -2 <= k2 <= 6 and y2 == -2:
                gather[(k2 + 2) * 32 + 24 + d, at + i] = 1
    for (k, y, d), i in own.items():
        gather[(k + 2) * 32 + d * 8 + y + 1, RHS_ALL + i] = 1
    out["hand"], out["gather"] = hand, gather
    return out


EARLY = ["mask_sel"]


def pack_tables(nx):
    all_tables = tables(nx)
    wide = [n for n, v in all_tables.items() if v.shape[1] > 256]
    rest = [n for n in all_tables if n not in EARLY and n not in wide]
    where, packed = {}, []
    for group, names in enumerate((EARLY, rest, wide)):
        width = max(all_tables[n].shape[1] for n in names)
        width = -(-width // 128) * 128
        parts, at = [], 0
        for name in names:
            rows, cols = all_tables[name].shape
            where[name] = (group, at, rows, cols)
            tall = -(-rows // 16) * 16
            padded = np.zeros((tall, width), np.float32)
            padded[:rows, :cols] = all_tables[name]
            parts.append(padded)
            at += tall
        packed.append(np.concatenate(parts).astype(ml_dtypes.bfloat16))
    return where, packed


def kernel(where, n_z, n_y, load_h, start_h, mask_h, stiff_h, tab0_h, tab1_h, tab2_h, smooth_h, fix_h, load, start, mask, stiff, tab0, tab1, tab2,
           xs, upd, inv, idle, res, edge, ss, se, vb, sw, sc, rw, rc, mr, ms, pk, cs, cr, rsend_buf, rr, cx, cu, cinv, cidle, css, crhs, cvb, cvh,
           wmat, wside, local_sem, out_sem, send_sem, recv_sem, msend, mrecv, csend, crecv, rsend, rrecv):
    nx = load.shape[-1]
    half, quarter = nx // 2, nx // 4
    gz, gy = lax.axis_index("gz"), lax.axis_index("gy")
    moves = {}
    for k, (name, src, dst) in enumerate([("start", start_h, start), ("tab0", tab0_h, tab0), ("mask", mask_h, mask), ("tab1", tab1_h, tab1),
                                          ("stiff", stiff_h, stiff), ("load", load_h, load), ("tab2", tab2_h, tab2)]):
        moves[name] = pltpu.make_async_copy(src, dst, local_sem.at[k])
        moves[name].start()

    def t(name, rows=None):
        group, at, r, c = where[name]
        return (tab0, tab1, tab2)[group][at : at + (rows or r), :c]

    def dot(a, b):
        return jnp.dot(a, b, preferred_element_type=F32)

    def exists(dz, dy):
        ok = None
        for delta, pos, n in ((dz, gz, n_z), (dy, gy, n_y)):
            if delta:
                test = pos > 0 if delta < 0 else pos < n - 1
                ok = test if ok is None else jnp.logical_and(ok, test)
        return ok

    mask_to = [(1, 0), (0, 1), (1, 1)]
    barrier = pltpu.get_barrier_semaphore()
    count = 0
    for dz, dy in NEAR:
        ok = exists(dz, dy)
        count = count + ok.astype(jnp.int32)

        @pl.when(ok)
        def _():
            pl.semaphore_signal(barrier, inc=1, device_id=(gz + dz, gy + dy), device_id_type=MESH)

    for k, (dz, dy) in enumerate(NEAR):

        @pl.when(jnp.logical_not(exists(dz, dy)))
        def _():
            if k < 4:
                rc[:, k] = jnp.zeros((4, 16, quarter), BF16)
            else:
                rw[:, k - 4] = jnp.zeros((4, 48, half), BF16)
            slot = ((dz + 1) * 3 + dy + 1) * 16
            cr[slot : slot + 16] = jnp.zeros((16, half), BF16)
            if (-dz, -dy) in mask_to:
                mr[mask_to.index((-dz, -dy))] = jnp.zeros((16, half), BF16)
            rr[RHS_AT[k] : RHS_AT[k] + RHS_ROWS[k]] = jnp.zeros((RHS_ROWS[k], half), BF16)

    def push(src, dst, send, recv, k):
        dz, dy = NEAR[k]
        return pltpu.make_async_remote_copy(
            src_ref=src, dst_ref=dst, send_sem=send, recv_sem=recv, device_id=(gz + dz, gy + dy), device_id_type=MESH)

    def back(k):
        return NEAR.index((-NEAR[k][0], -NEAR[k][1]))

    def field_copy(p, k):
        j = back(k)
        if k < 4:
            src, dst = sc.at[p, k], rc.at[p, j]
        else:
            src, dst = sw.at[p, k - 4], rw.at[p, j - 4]
        return push(src, dst, send_sem.at[p, k], recv_sem.at[p, j], k)

    def mask_copy(m):
        return push(ms.at[m], mr.at[m], msend.at[m], mrecv.at[m], NEAR.index(mask_to[m]))

    def scale_copy(k):
        dz, dy = NEAR[k]
        to = ((1 - dz) * 3 + 1 - dy) * 16
        return push(cs, cr.at[to : to + 16], csend.at[k], crecv.at[back(k)], k)

    def rhs_copy(k):
        j, n = back(k), RHS_ROWS[k]
        return push(rsend_buf.at[RHS_AT[k] : RHS_AT[k] + n], rr.at[RHS_AT[j] : RHS_AT[j] + n], rsend.at[k], rrecv.at[j], k)

    def halves(v):
        return jnp.concatenate([v[:, :half], v[:, half:]], axis=0)

    def joined(v):
        n = v.shape[0] // 2
        return jnp.concatenate([v[:n], v[n:]], axis=1)

    low4 = lax.broadcasted_iota(jnp.int32, (8, quarter), 0) < 4

    row8 = lax.broadcasted_iota(jnp.int32, (8, nx), 0)

    def spread(row):
        return jnp.broadcast_to(row, (8, nx))

    def pack_field(p):
        for side, y in enumerate((0, 7)):
            rows = []
            for d in range(3):
                v = spread(xs[0, 8 * d + y : 8 * d + y + 1])
                for z in range(1, B):
                    v = jnp.where(row8 == z, spread(xs[z, 8 * d + y : 8 * d + y + 1]), v)
                rows.append(v)
            sw[p, side] = halves(jnp.concatenate(rows, axis=0)).astype(BF16)
        for k in range(4):
            z, y = 7 if NEAR[k][0] > 0 else 0, 7 if NEAR[k][1] > 0 else 0
            v = spread(xs[z, y : y + 1])
            for d in (1, 2):
                v = jnp.where(row8 % 4 == d, spread(xs[z, 8 * d + y : 8 * d + y + 1]), v)
            v = jnp.where(row8 % 4 == 3, 0.0, v)
            v = [v[:, b * quarter : (b + 1) * quarter] for b in range(4)]
            sc[p, k] = jnp.concatenate([jnp.where(low4, v[0], v[1]), jnp.where(low4, v[2], v[3])], axis=0).astype(BF16)
        sw[p, 2] = halves(xs[0]).astype(BF16)
        sw[p, 3] = halves(xs[B - 1]).astype(BF16)

    def each(copy, do, ks=range(8)):
        for k in ks:

            @pl.when(exists(*NEAR[k]))
            def _():
                do(copy(k))

    def begin(c):
        c.start()

    def arrived(copy):
        each(lambda k: copy(back(k)), lambda c: c.wait_recv())

    upd[...] = jnp.zeros_like(upd)
    vb[0] = jnp.zeros((48, nx), BF16)
    vb[B + 1] = jnp.zeros((48, nx), BF16)
    moves["start"].wait()
    for z in range(B):
        for d in range(3):
            xs[z, 8 * d : 8 * d + 8] = start[d, z]
    pack_field(0)
    moves["tab0"].wait()
    moves["mask"].wait()
    mask_wide = jnp.concatenate([mask[z] for z in range(B)], axis=0).astype(F32)
    picked = dot(t("mask_sel"), mask_wide.astype(BF16))
    pk[...] = picked[32:48].astype(BF16)
    for m in range(3):
        ms[m] = halves(picked[8 * m : 8 * m + 8]).astype(BF16)

    pl.semaphore_wait(barrier, count)
    for m in range(3):

        @pl.when(exists(*mask_to[m]))
        def _():
            mask_copy(m).start()

    each(lambda k: field_copy(0, k), begin)

    moves["tab1"].wait()
    moves["stiff"].wait()
    stiff_bf = stiff[...]
    stiff_wide = stiff_bf.astype(F32)
    eye = lax.broadcasted_iota(jnp.int32, (EDOF, EDOF), 0) == lax.broadcasted_iota(jnp.int32, (EDOF, EDOF), 1)
    diag_mat = jnp.where(eye, stiff_wide, 0.0)
    bound = jnp.max(jnp.sum(jnp.abs(stiff_wide), axis=1, keepdims=True) / jnp.sum(diag_mat, axis=1, keepdims=True), axis=0, keepdims=True)
    rows_of = dot(t("rep"), stiff_bf).astype(BF16)
    total = None
    for cz2 in range(2):
        for cy2 in range(2):
            name = "%d%d" % (cz2, cy2)
            term = dot(rows_of, t("pick" + name, EDOF)) * t("keep" + name).astype(F32)
            total = term if total is None else total + term
    wmat[...] = total.astype(BF16)
    rows_of = dot(t("rep_y"), stiff_bf).astype(BF16)
    total = None
    for cz2 in range(2):
        term = dot(rows_of, t("pick_y%d" % cz2, EDOF)) * t("keep_y%d" % cz2).astype(F32)
        total = term if total is None else total + term
    wside[...] = total.astype(BF16)
    diag_bf = diag_mat.astype(BF16)
    diag_col = jnp.sum(dot(t("rep"), diag_bf), axis=1, keepdims=True)
    diag_col_x = jnp.sum(dot(t("rep_x"), diag_bf), axis=1, keepdims=True)

    def shift_up(v):
        lane = lax.broadcasted_iota(jnp.int32, v.shape, 1)
        return jnp.where(lane == 0, 0.0, pltpu.roll(v, 1, axis=1))

    def shift_down(v):
        n = v.shape[1]
        lane = lax.broadcasted_iota(jnp.int32, v.shape, 1)
        return jnp.where(lane == n - 1, 0.0, pltpu.roll(v, n - 1, axis=1))

    def diagonal(scale, z, d):
        sums = []
        for c in range(2):
            s = None
            for cz in range(2):
                for cy in range(2):
                    at = (4 * cz + 2 * cy + c) * 24 + d * 8
                    term = diag_col[at : at + 8] * scale(z - cz, cy)
                    s = term if s is None else s + term
            sums.append(s)
        return sums[0] + shift_up(sums[1])

    def put_plane(ref, z, rows):
        ref[z] = jnp.concatenate([rows, shift_down(rows)], axis=0).astype(BF16)

    def sums_of(matrix, planes, scales):
        n = planes.shape[1]
        sums = [[], []]
        for first in range(0, n, 256):
            lanes = slice(first, min(first + 256, n))
            terms = dot(matrix, planes[:, lanes])
            for c in range(2):
                parts = []
                for d in range(3):
                    s = None
                    for g, sc_g in enumerate(scales):
                        at = (2 * g + c) * 24 + d * 8
                        term = terms[at : at + 8] * sc_g[:, lanes]
                        s = term if s is None else s + term
                    parts.append(s)
                sums[c].append(jnp.concatenate(parts, axis=0))
        low, high = [jnp.concatenate(v, axis=1) if len(v) > 1 else v[0] for v in sums]
        return low + shift_up(high)

    def add_edges(p):
        ends = []
        for side in range(2):
            near, far = rc[p, side].astype(F32), rc[p, side + 2].astype(F32)
            blocks = []
            for b in range(4):
                rows = slice(8 * (b // 2), 8 * (b // 2) + 8)
                if b % 2:
                    blocks.append(jnp.where(low4, pltpu.roll(near[rows], 4, axis=0), far[rows]))
                else:
                    blocks.append(jnp.where(low4, near[rows], pltpu.roll(far[rows], 4, axis=0)))
            ends.append(jnp.concatenate(blocks, axis=1))
        sides = []
        for side in range(2):
            v = jnp.concatenate([joined(rw[p, side].astype(F32)), ends[side]], axis=0)
            sides += [v, shift_down(v)]
        sides = jnp.concatenate(sides, axis=0).astype(BF16)
        for side in range(2):
            scales = [se[16 * side + 8 * cz : 16 * side + 8 * cz + 8] for cz in range(2)]
            edge[side] = sums_of(wside[96 * side : 96 * side + 96], sides, scales)
        for side in range(2):
            v = joined(rw[p, 2 + side].astype(F32))
            v = jnp.concatenate([v, shift_down(v)], axis=0).astype(BF16)
            none = jnp.zeros((96, nx), BF16)
            first = 96 * (1 - side)
            v = jnp.concatenate([none, v] if side else [v, none], axis=0)
            edge[2 + side] = sums_of(wmat[first : first + 96, :144], v, [ss[B * side, 8 * cy : 8 * cy + 8] for cy in range(2)])

    def apply(matrix, planes, scale_now, scale_below):
        return sums_of(matrix, planes, [v[8 * cy : 8 * cy + 8] for v in (scale_now, scale_below) for cy in range(2)])

    def planes_of(own, edge, z, n):
        return jnp.concatenate([own[pl.ds(z, 3)].reshape(144, n), edge[pl.ds(z, 3)].reshape(48, n)], axis=0)


    for m in range(3):

        @pl.when(exists(-mask_to[m][0], -mask_to[m][1]))
        def _():
            mask_copy(m).wait_recv()

    came = [joined(mr[m].astype(F32)) for m in range(3)]
    all_masks = jnp.concatenate([mask_wide] + came + [jnp.zeros((8, nx), F32)], axis=0).astype(BF16)
    laid = dot(t("mask_put"), all_masks)
    ss[...] = laid[0:144].reshape(B + 1, 16, nx)
    se[...] = laid[144:176]

    for z in range(B):
        for d in range(3):
            dg = diagonal(lambda layer, cy: ss[layer + 1, cy * 8 : cy * 8 + 8], z, d)
            no = jnp.where(dg == 0.0, 1.0, 0.0)
            inv[z, d * 8 : d * 8 + 8] = 1.0 / ((dg + no) * bound)
            if d == 0:
                idle[z] = no

    ratio = (1.0 + LOW) / (1.0 - LOW)
    rho = [1.0 / ratio]
    for _ in range(2):
        rho.append(1.0 / (2.0 * ratio - rho[-1]))
    steps = [(0.0, 1.0 / (0.5 * (1.0 + LOW)))]
    for i in range(2):
        steps.append((rho[i + 1] * rho[i], 2.0 * rho[i + 1] / (0.5 * (1.0 - LOW))))

    def stack(ref, z):
        return jnp.concatenate([ref[0, z], ref[1, z], ref[2, z]], axis=0)

    def three(v):
        return jnp.concatenate([v, v, v], axis=0)

    moves["load"].wait()
    moves["tab2"].wait()
    row24 = lax.broadcasted_iota(jnp.int32, (24, nx), 0) % 8

    def sweep(p, carry):
        def pick(values):
            v = jnp.float32(values[-1])
            for i in range(len(values) - 2, -1, -1):
                v = jnp.where(p == i, jnp.float32(values[i]), v)
            return v

        keep, gain = pick([0.0, steps[1][0], steps[2][0], 0.0]), pick([steps[0][1], steps[1][1], steps[2][1], 0.0])
        for z in range(B):
            put_plane(vb, z + 1, xs[z])
        for z in range(B):
            planes = vb[z : z + 3].reshape(144, nx)
            res[z] = stack(load, z) - apply(wmat[:, :144], planes, ss[z + 1], ss[z]) - three(idle[z]) * xs[z]
        arrived(lambda k: field_copy(p, k))
        add_edges(p)
        for z in range(B):
            sides = []
            for side in range(2):
                sides.append(jnp.concatenate([jnp.broadcast_to(edge[side, 8 * d + z : 8 * d + z + 1], (8, nx)) for d in range(3)], axis=0))
            r = res[z] - jnp.where(row24 == 0, sides[0], jnp.where(row24 == 7, sides[1], 0.0))
            if z == 0:
                r = r - edge[2]
            if z == B - 1:
                r = r - edge[3]
            u = gain * inv[z] * r + keep * upd[z]
            res[z] = r
            xs[z] = xs[z] + u
            upd[z] = u

        @pl.when(p < 3)
        def _():
            pack_field(p + 1)
            each(lambda k: field_copy(p + 1, k), begin)

        @pl.when(p == 0)
        def _():
            cs[...] = dot(pk[...], t("pairs")).astype(BF16)
            cr[64:80] = cs[...]
            each(scale_copy, begin)

        return carry

    lax.fori_loop(0, 4, sweep, 0)

    for d in range(3):
        pltpu.make_async_copy(xs.at[:, 8 * d : 8 * d + 8], smooth_h.at[d], out_sem.at[d]).start()

    narrow = dot(t("shrink"), res[...].reshape(192, nx).astype(BF16))
    hi = dot(narrow.astype(BF16), t("down")).astype(BF16)
    rsend_buf[...] = dot(t("hand"), hi).astype(BF16)
    each(rhs_copy, begin)
    rr[RHS_ALL : RHS_ALL + 80] = hi

    arrived(scale_copy)
    css[...] = dot(t("cs_put"), cr[...]).reshape(10, 32, half)
    last_z, last_y = gz == n_z - 1, gy == n_y - 1
    good_y = jnp.where(jnp.logical_and(last_y, row8[:, :half] >= C + 1), 0.0, 1.0)
    for k in range(9):
        good = good_y
        if k - 2 >= C:
            good = good * jnp.where(last_z, 0.0, 1.0)
        for d in range(3):
            dg = diagonal(lambda layer, cy: css[layer + 1, cy * 8 : cy * 8 + 8], k, d)
            no = jnp.where(dg == 0.0, 1.0, 0.0)
            cinv[k, d * 8 : d * 8 + 8] = good / ((dg + no) * bound)
            if d == 0:
                cidle[k] = no
        sums = []
        for c in range(2):
            s = None
            for cz in range(2):
                for cy in range(2):
                    at = (4 * cz + 2 * cy + c) * 8
                    term = diag_col_x[at : at + 8] * css[k + 1 - cz, 16 + cy * 8 : 24 + cy * 8]
                    s = term if s is None else s + term
            sums.append(s)
        dg = sums[0] + shift_up(sums[1])
        no = jnp.where(dg == 0.0, 1.0, 0.0)
        extra = 1.0 / ((dg + no) * bound)
        if k - 2 >= C:
            extra = extra * jnp.where(last_z, 0.0, 1.0)
        cinv[k, 24:32] = extra

    arrived(rhs_copy)
    right = dot(t("gather"), rr[...])
    for k in range(9):
        total = right[32 * k : 32 * k + 32]
        crhs[k] = total[0:24]
        x = steps[0][1] * cinv[k] * total
        cx[k] = x[0:24]
        cu[k] = x[0:24]
        put_plane(cvb, k, x[0:24])
        put_plane(cvh, k, x[24:32])

    for p, (first, last) in ((1, (1, 7)), (2, (2, 6))):
        for k in range(first, last + 1):
            kv = apply(wmat[...], planes_of(cvb, cvh, k - 1, half), css[k + 1], css[k])
            x = cx[k]
            r = crhs[k] - kv - three(cidle[k]) * x
            u = steps[p][0] * cu[k] + steps[p][1] * cinv[k, 0:24] * r
            cx[k] = x + u
            cu[k] = u
        if p == 1:
            for k in range(first, last + 1):
                put_plane(cvb, k, cx[k])
                cvh[k] = jnp.zeros((16, half), BF16)

    fix = cx[2:7].reshape(120, half).astype(BF16)
    grown = dot(t("grow"), fix).astype(BF16)

    def fix_copy(part, d):
        at = C * part
        return pltpu.make_async_copy(res.at[at : at + C, 8 * d : 8 * d + 8], fix_h.at[d, at : at + C], out_sem.at[3 + 3 * part + d])

    for part in range(2):
        res[C * part : C * part + C] = dot(grown[96 * part : 96 * part + 96], t("up")).reshape(C, 24, nx)
        for d in range(3):
            fix_copy(part, d).start()

    for p in range(4):
        each(lambda k: field_copy(p, k), lambda c: c.wait_send())
    each(scale_copy, lambda c: c.wait_send())
    each(rhs_copy, lambda c: c.wait_send())
    for m in range(3):

        @pl.when(exists(*mask_to[m]))
        def _():
            mask_copy(m).wait_send()
    for d in range(3):
        pltpu.make_async_copy(xs.at[:, 8 * d : 8 * d + 8], smooth_h.at[d], out_sem.at[d]).wait()
        for part in range(2):
            fix_copy(part, d).wait()


def body(n_z, n_y, load, start, mask, stiff):
    nx = load.shape[-1]
    half, quarter = nx // 2, nx // 4
    where, packed = pack_tables(nx)
    given = [load, start, mask, stiff] + [jnp.asarray(v) for v in packed]
    dma = pltpu.SemaphoreType.DMA
    hbm = pl.BlockSpec(memory_space=pltpu.HBM)
    smooth, fix = pl.pallas_call(
        functools.partial(kernel, where, n_z, n_y),
        out_shape=[jax.ShapeDtypeStruct(load.shape, F32)] * 2,
        in_specs=[hbm] * len(given),
        out_specs=[hbm] * 2,
        scratch_shapes=[pltpu.VMEM(v.shape, v.dtype) for v in given]
        + [
            pltpu.VMEM((B, 24, nx), F32),
            pltpu.VMEM((B, 24, nx), F32),
            pltpu.VMEM((B, 24, nx), F32),
            pltpu.VMEM((B, 8, nx), F32),
            pltpu.VMEM((B, 24, nx), F32),
            pltpu.VMEM((4, 24, nx), F32),
            pltpu.VMEM((B + 1, 16, nx), F32),
            pltpu.VMEM((32, nx), F32),
            pltpu.VMEM((B + 2, 48, nx), BF16),
            pltpu.VMEM((4, 4, 48, half), BF16),
            pltpu.VMEM((4, 4, 16, quarter), BF16),
            pltpu.VMEM((4, 4, 48, half), BF16),
            pltpu.VMEM((4, 4, 16, quarter), BF16),
            pltpu.VMEM((3, 16, half), BF16),
            pltpu.VMEM((3, 16, half), BF16),
            pltpu.VMEM((16, nx), BF16),
            pltpu.VMEM((16, half), BF16),
            pltpu.VMEM((144, half), BF16),
            pltpu.VMEM((RHS_ALL, half), BF16),
            pltpu.VMEM((RHS_ALL + 80, half), BF16),
            pltpu.VMEM((9, 24, half), F32),
            pltpu.VMEM((9, 24, half), F32),
            pltpu.VMEM((9, 32, half), F32),
            pltpu.VMEM((9, 8, half), F32),
            pltpu.VMEM((10, 32, half), F32),
            pltpu.VMEM((9, 24, half), F32),
            pltpu.VMEM((9, 48, half), BF16),
            pltpu.VMEM((9, 16, half), BF16),
            pltpu.VMEM((192, 192), BF16),
            pltpu.VMEM((192, 128), BF16),
            dma((7,)), dma((9,)), dma((4, 8)), dma((4, 8)), dma((3,)), dma((3,)), dma((8,)), dma((8,)), dma((8,)), dma((8,)),
        ],
        compiler_params=pltpu.CompilerParams(collective_id=0, has_side_effects=True, vmem_limit_bytes=62 * 1024 * 1024),
    )(*given)
    return smooth + fix


def solution(mesh):
    in_specs = (P(None, "gz", "gy", None), P(None, "gz", "gy", None), P("gz", "gy", None), P())
    out_specs = P(None, "gz", "gy", None)
    fn = functools.partial(body, mesh.shape["gz"], mesh.shape["gy"])
    return jax.shard_map(fn, mesh=mesh, in_specs=in_specs, out_specs=out_specs, check_vma=False)
```

```python
import functools

import jax
import jax.numpy as jnp
import ml_dtypes
import numpy as np
from jax import lax
from jax.experimental import pallas as pl
from jax.experimental.pallas import tpu as pltpu
from jax.sharding import PartitionSpec as P

DOF = 3
EDOF = 24
B = 8
C = B // 2
LOW = 0.1
MESH = pl.DeviceIdType.MESH
F32, BF16 = jnp.float32, jnp.bfloat16

NEAR = [(-1, -1), (-1, 1), (1, -1), (1, 1), (0, -1), (0, 1), (-1, 0), (1, 0)]
EDGE = {-1: (0, 3), 0: (0, 5), 1: (2, 3)}
RHS_ROWS = [32, 32, 32, 32, 48, 48, 48, 48]
RHS_AT = [0, 32, 64, 96, 128, 176, 224, 272]
RHS_ALL = 320


def col_code(col):
    if col < 144:
        return col // 48, col % 48 // 24, col % 24 // 8, col % 8
    p, sx, r = (col - 144) // 16, col % 16 // 8, col % 8
    if r < 6:
        return p, sx, r % 3, -1 if r < 3 else 8
    return None


def tables(nx):
    half = nx // 2
    out = {}
    rep = np.zeros((192, EDOF))
    for r in range(192):
        rep[r, (r // 24) * 3 + (r % 24) // 8] = 1
    out["rep"] = rep
    rep_x = np.zeros((64, EDOF))
    for q in range(8):
        for d in range(3):
            rep_x[q * 8 + d, q * 3 + d] = 1
    out["rep_x"] = rep_x
    for cz2 in range(2):
        for cy2 in range(2):
            pick = np.zeros((32, 192))
            keep = np.zeros((192, 192))
            for col in range(192):
                code = col_code(col)
                if code is None:
                    continue
                p, sx, d, y2 = code
                pick[3 * (4 * cz2 + 2 * cy2 + sx) + d, col] = 1
                for r in range(192):
                    q, y = r // 24, r % 8
                    cz, cy = q // 4, (q // 2) % 2
                    if p == 1 - cz + cz2 and y2 == y - cy + cy2:
                        keep[r, col] = 1
            out["pick%d%d" % (cz2, cy2)] = pick
            out["keep%d%d" % (cz2, cy2)] = keep
    rep_y = np.zeros((192, EDOF))
    rows_y = []
    for r in range(192):
        side, cz, cx, d, z = r // 96, r // 48 % 2, r // 24 % 2, r // 8 % 3, r % 8
        rep_y[r, 3 * (4 * cz + 2 * (1 - side) + cx) + d] = 1
        rows_y.append((side, cz, z))
    out["rep_y"] = rep_y
    for cz2 in range(2):
        pick = np.zeros((32, 128))
        keep = np.zeros((192, 128))
        for col in range(128):
            side, sx, rc = col // 64, col // 32 % 2, col % 32
            if rc >= 24 and rc % 4 == 3:
                continue
            z2, d = (rc % 8, rc // 8) if rc < 24 else (-1 if rc < 28 else 8, rc % 4)
            pick[3 * (4 * cz2 + 2 * side + sx) + d, col] = 1
            for r, (row_side, cz, z) in enumerate(rows_y):
                if row_side == side and z2 == z - cz + cz2:
                    keep[r, col] = 1
        out["pick_y%d" % cz2], out["keep_y%d" % cz2] = pick, keep
    mask_sel = np.zeros((48, 64))
    for i in range(8):
        mask_sel[i, 56 + i] = 1
        mask_sel[8 + i, i * 8 + 7] = 1
    mask_sel[16, 63] = 1
    for z in range(B):
        for y in range(B):
            mask_sel[32 + (z // 2) * C + y // 2, z * 8 + y] = 0.25
    out["mask_sel"] = mask_sel
    mask_put = np.zeros((176, 96))
    for z in range(B):
        for cz in range(2):
            layer = z - cz
            mask_put[144 + cz * 8 + z, 72 + layer if layer >= 0 else 80] = 1
            mask_put[160 + cz * 8 + z, layer * 8 + 7 if layer >= 0 else 71] = 1
    for layer in range(-1, B):
        for y in range(B):
            for cy in range(2):
                row, y2 = (layer + 1) * 16 + cy * 8 + y, y - cy
                if layer >= 0:
                    mask_put[row, layer * 8 + y2 if y2 >= 0 else 72 + layer] = 1
                else:
                    mask_put[row, 64 + y2 if y2 >= 0 else 80] = 1
    out["mask_put"] = mask_put
    pairs = np.zeros((nx, half))
    down = np.zeros((nx, half))
    for i in range(nx):
        pairs[i, i // 2] = 1
        if i % 2 == 0:
            down[i, i // 2] = 1
        else:
            down[i, i // 2] = 0.5
            if i // 2 + 1 < half:
                down[i, i // 2 + 1] = 0.5
    out["pairs"], out["down"] = pairs, down
    up = down.T
    out["up"] = up
    cs_put = np.zeros((320, 144))

    def place(index):
        return (index + C) // C, (index + C) % C

    for layer in range(-3, 7):
        zs, kz = place(layer)
        base = (layer + 3) * 32
        for t in range(8):
            for cy in range(2):
                ys, ky = place(t - 1 - cy)
                cs_put[base + cy * 8 + t, (zs * 3 + ys) * 16 + kz * C + ky] = 1
        for d in range(3):
            for cy in range(2):
                ys, ky = place(-2 - cy)
                cs_put[base + 16 + cy * 8 + d, (zs * 3 + ys) * 16 + kz * C + ky] = 1
    out["cs_put"] = cs_put
    line = np.zeros((C + 1, B))
    for i in range(B):
        if i % 2 == 0:
            line[i // 2, i] = 1
        else:
            line[i // 2, i] = 0.5
            line[i // 2 + 1, i] = 0.5
    shrink = np.zeros((80, 192))
    grow = np.zeros((192, 120))
    for k in range(C + 1):
        for j in range(C + 1):
            for z in range(B):
                for y in range(B):
                    for d in range(3):
                        w = line[k, z] * line[j, y]
                        shrink[k * 16 + j * 3 + d, z * 24 + d * 8 + y] = w
                        grow[z * 24 + d * 8 + y, k * 24 + d * 8 + j + 1] = w
    out["shrink"], out["grow"] = shrink, grow
    hand = np.zeros((RHS_ALL, 80))
    gather = np.zeros((288, RHS_ALL + 80))

    def message(dz, dy):
        (z0, nz), (y0, ny) = EDGE[dz], EDGE[dy]
        return [(k, y, d) for k in range(z0, z0 + nz) for y in range(y0, y0 + ny) for d in range(3)]

    for n, (dz, dy) in enumerate(NEAR):
        for i, (k, y, d) in enumerate(message(dz, dy)):
            hand[RHS_AT[n] + i, k * 16 + y * 3 + d] = 1
    sources = [(RHS_AT[n], dz, dy, message(-dz, -dy)) for n, (dz, dy) in enumerate(NEAR)]
    own = {(k, y, d): k * 16 + y * 3 + d for k in range(5) for y in range(5) for d in range(3)}
    for at, dz, dy, rows in sources:
        for i, (k, y, d) in enumerate(rows):
            k2, y2 = k + C * dz, y + C * dy
            if -2 <= k2 <= 6 and -1 <= y2 <= 6:
                gather[(k2 + 2) * 32 + d * 8 + y2 + 1, at + i] = 1
            if -2 <= k2 <= 6 and y2 == -2:
                gather[(k2 + 2) * 32 + 24 + d, at + i] = 1
    for (k, y, d), i in own.items():
        gather[(k + 2) * 32 + d * 8 + y + 1, RHS_ALL + i] = 1
    out["hand"], out["gather"] = hand, gather
    return out


EARLY = ["mask_sel"]


def pack_tables(nx):
    all_tables = tables(nx)
    wide = [n for n, v in all_tables.items() if v.shape[1] > 256]
    rest = [n for n in all_tables if n not in EARLY and n not in wide]
    where, packed = {}, []
    for group, names in enumerate((EARLY, rest, wide)):
        width = max(all_tables[n].shape[1] for n in names)
        width = -(-width // 128) * 128
        parts, at = [], 0
        for name in names:
            rows, cols = all_tables[name].shape
            where[name] = (group, at, rows, cols)
            tall = -(-rows // 16) * 16
            padded = np.zeros((tall, width), np.float32)
            padded[:rows, :cols] = all_tables[name]
            parts.append(padded)
            at += tall
        packed.append(np.concatenate(parts).astype(ml_dtypes.bfloat16))
    return where, packed


def kernel(where, n_z, n_y, load_h, start_h, mask_h, stiff_h, tab0_h, tab1_h, tab2_h, smooth_h, fix_h, load, start, mask, stiff, tab0, tab1, tab2,
           xs, upd, inv, idle, res, edge, ss, se, vb, sw, sc, rw, rc, mr, ms, pk, cs, cr, rsend_buf, rr, cx, cu, cinv, cidle, css, crhs, cvb, cvh,
           wmat, wside, local_sem, out_sem, send_sem, recv_sem, msend, mrecv, csend, crecv, rsend, rrecv):
    nx = load.shape[-1]
    half, quarter = nx // 2, nx // 4
    gz, gy = lax.axis_index("gz"), lax.axis_index("gy")
    moves = {}
    for k, (name, src, dst) in enumerate([("start", start_h, start), ("tab0", tab0_h, tab0), ("mask", mask_h, mask), ("tab1", tab1_h, tab1),
                                          ("stiff", stiff_h, stiff), ("load", load_h, load), ("tab2", tab2_h, tab2)]):
        moves[name] = pltpu.make_async_copy(src, dst, local_sem.at[k])
        moves[name].start()

    def t(name, rows=None):
        group, at, r, c = where[name]
        return (tab0, tab1, tab2)[group][at : at + (rows or r), :c]

    def dot(a, b):
        return jnp.dot(a, b, preferred_element_type=F32)

    def exists(dz, dy):
        ok = None
        for delta, pos, n in ((dz, gz, n_z), (dy, gy, n_y)):
            if delta:
                test = pos > 0 if delta < 0 else pos < n - 1
                ok = test if ok is None else jnp.logical_and(ok, test)
        return ok

    mask_to = [(1, 0), (0, 1), (1, 1)]
    barrier = pltpu.get_barrier_semaphore()
    count = 0
    for dz, dy in NEAR:
        ok = exists(dz, dy)
        count = count + ok.astype(jnp.int32)

        @pl.when(ok)
        def _():
            pl.semaphore_signal(barrier, inc=1, device_id=(gz + dz, gy + dy), device_id_type=MESH)

    for k, (dz, dy) in enumerate(NEAR):

        @pl.when(jnp.logical_not(exists(dz, dy)))
        def _():
            if k < 4:
                rc[:, k] = jnp.zeros((4, 16, quarter), BF16)
            else:
                rw[:, k - 4] = jnp.zeros((4, 48, half), BF16)
            slot = ((dz + 1) * 3 + dy + 1) * 16
            cr[slot : slot + 16] = jnp.zeros((16, half), BF16)
            if (-dz, -dy) in mask_to:
                mr[mask_to.index((-dz, -dy))] = jnp.zeros((16, half), BF16)
            rr[RHS_AT[k] : RHS_AT[k] + RHS_ROWS[k]] = jnp.zeros((RHS_ROWS[k], half), BF16)

    def push(src, dst, send, recv, k):
        dz, dy = NEAR[k]
        return pltpu.make_async_remote_copy(
            src_ref=src, dst_ref=dst, send_sem=send, recv_sem=recv, device_id=(gz + dz, gy + dy), device_id_type=MESH)

    def back(k):
        return NEAR.index((-NEAR[k][0], -NEAR[k][1]))

    def field_copy(p, k):
        j = back(k)
        if k < 4:
            src, dst = sc.at[p, k], rc.at[p, j]
        else:
            src, dst = sw.at[p, k - 4], rw.at[p, j - 4]
        return push(src, dst, send_sem.at[p, k], recv_sem.at[p, j], k)

    def mask_copy(m):
        return push(ms.at[m], mr.at[m], msend.at[m], mrecv.at[m], NEAR.index(mask_to[m]))

    def scale_copy(k):
        dz, dy = NEAR[k]
        to = ((1 - dz) * 3 + 1 - dy) * 16
        return push(cs, cr.at[to : to + 16], csend.at[k], crecv.at[back(k)], k)

    def rhs_copy(k):
        j, n = back(k), RHS_ROWS[k]
        return push(rsend_buf.at[RHS_AT[k] : RHS_AT[k] + n], rr.at[RHS_AT[j] : RHS_AT[j] + n], rsend.at[k], rrecv.at[j], k)

    def halves(v):
        return jnp.concatenate([v[:, :half], v[:, half:]], axis=0)

    def joined(v):
        n = v.shape[0] // 2
        return jnp.concatenate([v[:n], v[n:]], axis=1)

    low4 = lax.broadcasted_iota(jnp.int32, (8, quarter), 0) < 4

    row8 = lax.broadcasted_iota(jnp.int32, (8, nx), 0)

    def spread(row):
        return jnp.broadcast_to(row, (8, nx))

    def pack_field(p):
        for side, y in enumerate((0, 7)):
            rows = []
            for d in range(3):
                v = spread(xs[0, 8 * d + y : 8 * d + y + 1])
                for z in range(1, B):
                    v = jnp.where(row8 == z, spread(xs[z, 8 * d + y : 8 * d + y + 1]), v)
                rows.append(v)
            sw[p, side] = halves(jnp.concatenate(rows, axis=0)).astype(BF16)
        for k in range(4):
            z, y = 7 if NEAR[k][0] > 0 else 0, 7 if NEAR[k][1] > 0 else 0
            v = spread(xs[z, y : y + 1])
            for d in (1, 2):
                v = jnp.where(row8 % 4 == d, spread(xs[z, 8 * d + y : 8 * d + y + 1]), v)
            v = jnp.where(row8 % 4 == 3, 0.0, v)
            v = [v[:, b * quarter : (b + 1) * quarter] for b in range(4)]
            sc[p, k] = jnp.concatenate([jnp.where(low4, v[0], v[1]), jnp.where(low4, v[2], v[3])], axis=0).astype(BF16)

    def pack_ends(p):
        sw[p, 2] = halves(xs[0]).astype(BF16)
        sw[p, 3] = halves(xs[B - 1]).astype(BF16)

    def each(copy, do, ks=range(8)):
        for k in ks:

            @pl.when(exists(*NEAR[k]))
            def _():
                do(copy(k))

    def begin(c):
        c.start()

    def arrived(copy, ks=range(8)):
        for k in ks:

            @pl.when(exists(*NEAR[k]))
            def _():
                copy(back(k)).wait_recv()

    upd[...] = jnp.zeros_like(upd)
    vb[0] = jnp.zeros((48, nx), BF16)
    vb[B + 1] = jnp.zeros((48, nx), BF16)
    moves["start"].wait()
    for z in range(B):
        for d in range(3):
            xs[z, 8 * d : 8 * d + 8] = start[d, z]
    pack_field(0)
    pack_ends(0)
    moves["tab0"].wait()
    moves["mask"].wait()
    mask_wide = jnp.concatenate([mask[z] for z in range(B)], axis=0).astype(F32)
    picked = dot(t("mask_sel"), mask_wide.astype(BF16))
    pk[...] = picked[32:48].astype(BF16)
    for m in range(3):
        ms[m] = halves(picked[8 * m : 8 * m + 8]).astype(BF16)

    pl.semaphore_wait(barrier, count)
    for m in range(3):

        @pl.when(exists(*mask_to[m]))
        def _():
            mask_copy(m).start()

    each(lambda k: field_copy(0, k), begin)

    moves["tab1"].wait()
    moves["stiff"].wait()
    stiff_bf = stiff[...]
    stiff_wide = stiff_bf.astype(F32)
    eye = lax.broadcasted_iota(jnp.int32, (EDOF, EDOF), 0) == lax.broadcasted_iota(jnp.int32, (EDOF, EDOF), 1)
    diag_mat = jnp.where(eye, stiff_wide, 0.0)
    bound = jnp.max(jnp.sum(jnp.abs(stiff_wide), axis=1, keepdims=True) / jnp.sum(diag_mat, axis=1, keepdims=True), axis=0, keepdims=True)
    rows_of = dot(t("rep"), stiff_bf).astype(BF16)
    total = None
    for cz2 in range(2):
        for cy2 in range(2):
            name = "%d%d" % (cz2, cy2)
            term = dot(rows_of, t("pick" + name, EDOF)) * t("keep" + name).astype(F32)
            total = term if total is None else total + term
    wmat[...] = total.astype(BF16)
    rows_of = dot(t("rep_y"), stiff_bf).astype(BF16)
    total = None
    for cz2 in range(2):
        term = dot(rows_of, t("pick_y%d" % cz2, EDOF)) * t("keep_y%d" % cz2).astype(F32)
        total = term if total is None else total + term
    wside[...] = total.astype(BF16)
    diag_bf = diag_mat.astype(BF16)
    diag_col = jnp.sum(dot(t("rep"), diag_bf), axis=1, keepdims=True)
    diag_col_x = jnp.sum(dot(t("rep_x"), diag_bf), axis=1, keepdims=True)

    def shift_up(v):
        lane = lax.broadcasted_iota(jnp.int32, v.shape, 1)
        return jnp.where(lane == 0, 0.0, pltpu.roll(v, 1, axis=1))

    def shift_down(v):
        n = v.shape[1]
        lane = lax.broadcasted_iota(jnp.int32, v.shape, 1)
        return jnp.where(lane == n - 1, 0.0, pltpu.roll(v, n - 1, axis=1))

    def diagonal(scale, z, d):
        sums = []
        for c in range(2):
            s = None
            for cz in range(2):
                for cy in range(2):
                    at = (4 * cz + 2 * cy + c) * 24 + d * 8
                    term = diag_col[at : at + 8] * scale(z - cz, cy)
                    s = term if s is None else s + term
            sums.append(s)
        return sums[0] + shift_up(sums[1])

    def put_plane(ref, z, rows):
        ref[z] = jnp.concatenate([rows, shift_down(rows)], axis=0).astype(BF16)

    def sums_of(matrix, planes, scales):
        n = planes.shape[1]
        sums = [[], []]
        for first in range(0, n, 256):
            lanes = slice(first, min(first + 256, n))
            terms = dot(matrix, planes[:, lanes])
            for c in range(2):
                parts = []
                for d in range(3):
                    s = None
                    for g, sc_g in enumerate(scales):
                        at = (2 * g + c) * 24 + d * 8
                        term = terms[at : at + 8] * sc_g[:, lanes]
                        s = term if s is None else s + term
                    parts.append(s)
                sums[c].append(jnp.concatenate(parts, axis=0))
        low, high = [jnp.concatenate(v, axis=1) if len(v) > 1 else v[0] for v in sums]
        return low + shift_up(high)

    def add_edges(p):
        ends = []
        for side in range(2):
            near, far = rc[p, side].astype(F32), rc[p, side + 2].astype(F32)
            blocks = []
            for b in range(4):
                rows = slice(8 * (b // 2), 8 * (b // 2) + 8)
                if b % 2:
                    blocks.append(jnp.where(low4, pltpu.roll(near[rows], 4, axis=0), far[rows]))
                else:
                    blocks.append(jnp.where(low4, near[rows], pltpu.roll(far[rows], 4, axis=0)))
            ends.append(jnp.concatenate(blocks, axis=1))
        sides = []
        for side in range(2):
            v = jnp.concatenate([joined(rw[p, side].astype(F32)), ends[side]], axis=0)
            sides += [v, shift_down(v)]
        sides = jnp.concatenate(sides, axis=0).astype(BF16)
        for side in range(2):
            scales = [se[16 * side + 8 * cz : 16 * side + 8 * cz + 8] for cz in range(2)]
            edge[side] = sums_of(wside[96 * side : 96 * side + 96], sides, scales)

    def add_ends(p):
        for side in range(2):
            v = joined(rw[p, 2 + side].astype(F32))
            v = jnp.concatenate([v, shift_down(v)], axis=0).astype(BF16)
            none = jnp.zeros((96, nx), BF16)
            first = 96 * (1 - side)
            v = jnp.concatenate([none, v] if side else [v, none], axis=0)
            edge[2 + side] = sums_of(wmat[first : first + 96, :144], v, [ss[B * side, 8 * cy : 8 * cy + 8] for cy in range(2)])

    def apply(matrix, planes, scale_now, scale_below):
        return sums_of(matrix, planes, [v[8 * cy : 8 * cy + 8] for v in (scale_now, scale_below) for cy in range(2)])

    def planes_of(own, edge, z, n):
        return jnp.concatenate([own[pl.ds(z, 3)].reshape(144, n), edge[pl.ds(z, 3)].reshape(48, n)], axis=0)


    for m in range(3):

        @pl.when(exists(-mask_to[m][0], -mask_to[m][1]))
        def _():
            mask_copy(m).wait_recv()

    came = [joined(mr[m].astype(F32)) for m in range(3)]
    all_masks = jnp.concatenate([mask_wide] + came + [jnp.zeros((8, nx), F32)], axis=0).astype(BF16)
    laid = dot(t("mask_put"), all_masks)
    ss[...] = laid[0:144].reshape(B + 1, 16, nx)
    se[...] = laid[144:176]

    for z in range(B):
        for d in range(3):
            dg = diagonal(lambda layer, cy: ss[layer + 1, cy * 8 : cy * 8 + 8], z, d)
            no = jnp.where(dg == 0.0, 1.0, 0.0)
            inv[z, d * 8 : d * 8 + 8] = 1.0 / ((dg + no) * bound)
            if d == 0:
                idle[z] = no

    ratio = (1.0 + LOW) / (1.0 - LOW)
    rho = [1.0 / ratio]
    for _ in range(2):
        rho.append(1.0 / (2.0 * ratio - rho[-1]))
    steps = [(0.0, 1.0 / (0.5 * (1.0 + LOW)))]
    for i in range(2):
        steps.append((rho[i + 1] * rho[i], 2.0 * rho[i + 1] / (0.5 * (1.0 - LOW))))

    def stack(ref, z):
        return jnp.concatenate([ref[0, z], ref[1, z], ref[2, z]], axis=0)

    def three(v):
        return jnp.concatenate([v, v, v], axis=0)

    moves["load"].wait()
    moves["tab2"].wait()
    row24 = lax.broadcasted_iota(jnp.int32, (24, nx), 0) % 8

    def sweep(p, carry):
        def pick(values):
            v = jnp.float32(values[-1])
            for i in range(len(values) - 2, -1, -1):
                v = jnp.where(p == i, jnp.float32(values[i]), v)
            return v

        keep, gain = pick([0.0, steps[1][0], steps[2][0], 0.0]), pick([steps[0][1], steps[1][1], steps[2][1], 0.0])
        for z in range(B):
            put_plane(vb, z + 1, xs[z])
        for z in range(B):
            planes = vb[z : z + 3].reshape(144, nx)
            res[z] = stack(load, z) - apply(wmat[:, :144], planes, ss[z + 1], ss[z]) - three(idle[z]) * xs[z]
        arrived(lambda k: field_copy(p, k), range(6, 8))
        add_ends(p)
        arrived(lambda k: field_copy(p, k), range(6))
        add_edges(p)
        for z in range(B):
            sides = []
            for side in range(2):
                sides.append(jnp.concatenate([jnp.broadcast_to(edge[side, 8 * d + z : 8 * d + z + 1], (8, nx)) for d in range(3)], axis=0))
            r = res[z] - jnp.where(row24 == 0, sides[0], jnp.where(row24 == 7, sides[1], 0.0))
            if z == 0:
                r = r - edge[2]
            if z == B - 1:
                r = r - edge[3]
            u = gain * inv[z] * r + keep * upd[z]
            res[z] = r
            xs[z] = xs[z] + u
            upd[z] = u

        @pl.when(p < 3)
        def _():
            pack_field(p + 1)
            each(lambda k: field_copy(p + 1, k), begin, range(6))
            pack_ends(p + 1)
            each(lambda k: field_copy(p + 1, k), begin, range(6, 8))

        @pl.when(p == 0)
        def _():
            cs[...] = dot(pk[...], t("pairs")).astype(BF16)
            cr[64:80] = cs[...]
            each(scale_copy, begin)

        return carry

    lax.fori_loop(0, 4, sweep, 0)

    for d in range(3):
        pltpu.make_async_copy(xs.at[:, 8 * d : 8 * d + 8], smooth_h.at[d], out_sem.at[d]).start()

    narrow = dot(t("shrink"), res[...].reshape(192, nx).astype(BF16))
    hi = dot(narrow.astype(BF16), t("down")).astype(BF16)
    rsend_buf[...] = dot(t("hand"), hi).astype(BF16)
    each(rhs_copy, begin)
    rr[RHS_ALL : RHS_ALL + 80] = hi

    arrived(scale_copy)
    css[...] = dot(t("cs_put"), cr[...]).reshape(10, 32, half)
    last_z, last_y = gz == n_z - 1, gy == n_y - 1
    good_y = jnp.where(jnp.logical_and(last_y, row8[:, :half] >= C + 1), 0.0, 1.0)
    for k in range(9):
        good = good_y
        if k - 2 >= C:
            good = good * jnp.where(last_z, 0.0, 1.0)
        for d in range(3):
            dg = diagonal(lambda layer, cy: css[layer + 1, cy * 8 : cy * 8 + 8], k, d)
            no = jnp.where(dg == 0.0, 1.0, 0.0)
            cinv[k, d * 8 : d * 8 + 8] = good / ((dg + no) * bound)
            if d == 0:
                cidle[k] = no
        sums = []
        for c in range(2):
            s = None
            for cz in range(2):
                for cy in range(2):
                    at = (4 * cz + 2 * cy + c) * 8
                    term = diag_col_x[at : at + 8] * css[k + 1 - cz, 16 + cy * 8 : 24 + cy * 8]
                    s = term if s is None else s + term
            sums.append(s)
        dg = sums[0] + shift_up(sums[1])
        no = jnp.where(dg == 0.0, 1.0, 0.0)
        extra = 1.0 / ((dg + no) * bound)
        if k - 2 >= C:
            extra = extra * jnp.where(last_z, 0.0, 1.0)
        cinv[k, 24:32] = extra

    arrived(rhs_copy)
    right = dot(t("gather"), rr[...])
    for k in range(9):
        total = right[32 * k : 32 * k + 32]
        crhs[k] = total[0:24]
        x = steps[0][1] * cinv[k] * total
        cx[k] = x[0:24]
        cu[k] = x[0:24]
        put_plane(cvb, k, x[0:24])
        put_plane(cvh, k, x[24:32])

    for p, (first, last) in ((1, (1, 7)), (2, (2, 6))):
        for k in range(first, last + 1):
            kv = apply(wmat[...], planes_of(cvb, cvh, k - 1, half), css[k + 1], css[k])
            x = cx[k]
            r = crhs[k] - kv - three(cidle[k]) * x
            u = steps[p][0] * cu[k] + steps[p][1] * cinv[k, 0:24] * r
            cx[k] = x + u
            cu[k] = u
        if p == 1:
            for k in range(first, last + 1):
                put_plane(cvb, k, cx[k])
                cvh[k] = jnp.zeros((16, half), BF16)

    fix = cx[2:7].reshape(120, half).astype(BF16)
    grown = dot(t("grow"), fix).astype(BF16)

    def fix_copy(part, d):
        at = C * part
        return pltpu.make_async_copy(res.at[at : at + C, 8 * d : 8 * d + 8], fix_h.at[d, at : at + C], out_sem.at[3 + 3 * part + d])

    for part in range(2):
        res[C * part : C * part + C] = dot(grown[96 * part : 96 * part + 96], t("up")).reshape(C, 24, nx)
        for d in range(3):
            fix_copy(part, d).start()

    for p in range(4):
        each(lambda k: field_copy(p, k), lambda c: c.wait_send())
    each(scale_copy, lambda c: c.wait_send())
    each(rhs_copy, lambda c: c.wait_send())
    for m in range(3):

        @pl.when(exists(*mask_to[m]))
        def _():
            mask_copy(m).wait_send()
    for d in range(3):
        pltpu.make_async_copy(xs.at[:, 8 * d : 8 * d + 8], smooth_h.at[d], out_sem.at[d]).wait()
        for part in range(2):
            fix_copy(part, d).wait()


def body(n_z, n_y, load, start, mask, stiff):
    nx = load.shape[-1]
    half, quarter = nx // 2, nx // 4
    where, packed = pack_tables(nx)
    given = [load, start, mask, stiff] + [jnp.asarray(v) for v in packed]
    dma = pltpu.SemaphoreType.DMA
    hbm = pl.BlockSpec(memory_space=pltpu.HBM)
    smooth, fix = pl.pallas_call(
        functools.partial(kernel, where, n_z, n_y),
        out_shape=[jax.ShapeDtypeStruct(load.shape, F32)] * 2,
        in_specs=[hbm] * len(given),
        out_specs=[hbm] * 2,
        scratch_shapes=[pltpu.VMEM(v.shape, v.dtype) for v in given]
        + [
            pltpu.VMEM((B, 24, nx), F32),
            pltpu.VMEM((B, 24, nx), F32),
            pltpu.VMEM((B, 24, nx), F32),
            pltpu.VMEM((B, 8, nx), F32),
            pltpu.VMEM((B, 24, nx), F32),
            pltpu.VMEM((4, 24, nx), F32),
            pltpu.VMEM((B + 1, 16, nx), F32),
            pltpu.VMEM((32, nx), F32),
            pltpu.VMEM((B + 2, 48, nx), BF16),
            pltpu.VMEM((4, 4, 48, half), BF16),
            pltpu.VMEM((4, 4, 16, quarter), BF16),
            pltpu.VMEM((4, 4, 48, half), BF16),
            pltpu.VMEM((4, 4, 16, quarter), BF16),
            pltpu.VMEM((3, 16, half), BF16),
            pltpu.VMEM((3, 16, half), BF16),
            pltpu.VMEM((16, nx), BF16),
            pltpu.VMEM((16, half), BF16),
            pltpu.VMEM((144, half), BF16),
            pltpu.VMEM((RHS_ALL, half), BF16),
            pltpu.VMEM((RHS_ALL + 80, half), BF16),
            pltpu.VMEM((9, 24, half), F32),
            pltpu.VMEM((9, 24, half), F32),
            pltpu.VMEM((9, 32, half), F32),
            pltpu.VMEM((9, 8, half), F32),
            pltpu.VMEM((10, 32, half), F32),
            pltpu.VMEM((9, 24, half), F32),
            pltpu.VMEM((9, 48, half), BF16),
            pltpu.VMEM((9, 16, half), BF16),
            pltpu.VMEM((192, 192), BF16),
            pltpu.VMEM((192, 128), BF16),
            dma((7,)), dma((9,)), dma((4, 8)), dma((4, 8)), dma((3,)), dma((3,)), dma((8,)), dma((8,)), dma((8,)), dma((8,)),
        ],
        compiler_params=pltpu.CompilerParams(collective_id=0, has_side_effects=True, vmem_limit_bytes=62 * 1024 * 1024),
    )(*given)
    return smooth + fix


def solution(mesh):
    in_specs = (P(None, "gz", "gy", None), P(None, "gz", "gy", None), P("gz", "gy", None), P())
    out_specs = P(None, "gz", "gy", None)
    fn = functools.partial(body, mesh.shape["gz"], mesh.shape["gy"])
    return jax.shard_map(fn, mesh=mesh, in_specs=in_specs, out_specs=out_specs, check_vma=False)
```
